128 devices in a mesh: gx: 32 (over y, x, core), sp: 4 (over z).
Axes of the slice: x: 4, y: 4, z: 4, core: 2. Of those that a mesh axis runs over, the one named last changes fastest.
Arguments:
- previous_head: float32 [8, 256, 512], P(None, 'gx', 'sp'), may hold values from -6 to 6
- recharge: float32 [8, 256, 512], P(None, 'gx', 'sp'), may hold values from -6 to 6
- soil_zone: int32 [8, 256, 512], P(None, 'gx', 'sp'), may hold values from 0 to 7
- soil_cond: float32 [8], replicated, may hold values from 0.1 to 1
- soil_store: float32 [8], replicated, may hold values from 0.05 to 0.5
- species: float32 [12, 8, 256, 512], P('sp', None, 'gx'), may hold values from -6 to 6
- mineral_zone: int32 [8, 256, 512], P(None, 'gx', 'sp'), may hold values from 0 to 5
- rate_table: float32 [6, 8], replicated, may hold values from 0.3 to 3
- stoich: float32 [12, 8], replicated, may hold values from -3 to 3
- log_equil: float32 [8], replicated, may hold values from -1 to 1
Outputs:
- head_field: float32 [8, 256, 512], P(None, 'gx', 'sp')
- species_out: float32 [12, 8, 256, 512], P('sp', None, 'gx')
The draws below stay inside these ranges and needn't reach their ends.
Inputs may be any that keep to these rules, and one draw needn't show every extreme that they name: `soil_zone`: a soil class of 8. `mineral_zone`: a mineral zone class of 6.
All inputs are finite; a program needn't handle non-finite values.
Results may differ from the reference program's by a relative error of at most 0.0003.
Values sent between devices are 32-bit elements; how exact they have to be, the bound alone decides.
A program may use at most 64 MiB of HBM per device.

```python
import math
import jax
import jax.numpy as jnp
from jax import lax

S = 12
NM = 8
NSOIL = 8
NMZONE = 6
NZ = 8
ITERS = 6
NEWTON = 2
NX = 256
NY = 512


def place_ends(values, stream_key, least, high):
    dims = values.shape
    index_at = [jax.random.randint(jax.random.fold_in(stream_key, axis), (), 0, dims[axis]) for axis in range(len(dims))]
    values = values.at[tuple(index_at)].set(least)
    longest = dims.index(max(dims))
    index_at[longest] = (index_at[longest] + 1) % dims[longest]
    return values.at[tuple(index_at)].set(high)


def block_scale(stream_key, extent, pieces, low, top_value):
    gain, own = 1.0, jax.random.fold_in(stream_key, 6)
    for axis_at, blocks in pieces:
        steps = jnp.exp(jax.random.uniform(jax.random.fold_in(own, axis_at), (blocks,), jnp.float32, low / len(pieces), top_value / len(pieces)))
        gain = gain * jnp.repeat(steps, extent[axis_at] // blocks).reshape([-1 if axis == axis_at else 1 for axis in range(len(extent))])
    return gain


def bell_draw(stream_key, shape, deviation, most, shards=(), kind=jnp.bfloat16):
    drawn = jax.random.normal(stream_key, shape, jnp.float32) * deviation
    if len(shards) > 0:
        drawn = block_scale(stream_key, shape, shards, -0.22, 0.18) * drawn
    return jnp.clip(drawn, min=-most, max=most).astype(kind)


def setup_inputs(seed: int = 0) -> dict:
    key_list = jax.random.split(jax.random.key(seed), 11)
    return {
        "previous_head": bell_draw(key_list[0], (NZ, NX, NY), 1.0, 6.0, ((1, 32), (2, 4)), jnp.float32),
        "recharge": bell_draw(key_list[1], (NZ, NX, NY), 1.0, 6.0, ((1, 32), (2, 4)), jnp.float32),
        "soil_zone": place_ends(jax.random.randint(key_list[2], (NZ, NX, NY), 0, NSOIL), jax.random.fold_in(key_list[2], 1), 0, NSOIL - 1).astype(jnp.int32),
        "soil_cond": jnp.clip(jnp.exp(jax.random.uniform(key_list[3], (NSOIL,), jnp.float32, math.log(0.1), math.log(1.0))), 0.1, 1.0),
        "soil_store": jnp.clip(jnp.exp(jax.random.uniform(key_list[4], (NSOIL,), jnp.float32, math.log(0.05), math.log(0.5))), 0.05, 0.5),
        "species": bell_draw(key_list[5], (S, NZ, NX, NY), 1.0, 6.0, ((0, 4), (2, 32)), jnp.float32),
        "mineral_zone": place_ends(jax.random.randint(key_list[6], (NZ, NX, NY), 0, NMZONE), jax.random.fold_in(key_list[6], 1), 0, NMZONE - 1).astype(jnp.int32),
        "rate_table": jnp.clip(jnp.exp(jax.random.uniform(key_list[7], (NMZONE, NM), jnp.float32, math.log(0.3), math.log(3.0))), 0.3, 3.0),
        "stoich": bell_draw(key_list[8], (S, NM), 0.5, 3.0, (), jnp.float32),
        "log_equil": jnp.clip(jax.random.uniform(key_list[9], (NM,), jnp.float32, -1.0, 1.0), -1.0, 1.0),
    }


time_step = 0.05
dispersion = 0.5
reaction_span = 0.5
newton_damping = 0.5

def harmonic(center, other):
    return 2.0 * center * other / (center + other)

def six_sides(padded):
    return [padded[..., 2:, 1:-1, 1:-1], padded[..., :-2, 1:-1, 1:-1], padded[..., 1:-1, 2:, 1:-1], padded[..., 1:-1, :-2, 1:-1], padded[..., 1:-1, 1:-1, 2:], padded[..., 1:-1, 1:-1, :-2]]

def lookup(labels, entries):
    levels = jnp.arange(entries.shape[0], dtype=jnp.int32).reshape((-1,) + (1,) * labels.ndim)
    return lax.optimization_barrier(jnp.sum(jnp.where(labels[None] == levels, entries.reshape(levels.shape), 0.0), axis=0))

def lookup_rows(labels, entries):
    levels = jnp.arange(entries.shape[0], dtype=jnp.int32)[:, None, None]
    return lax.optimization_barrier(jnp.sum(jnp.where(labels[None, None, :] == levels, entries[:, :, None], 0.0), axis=0))

def transport(concentration, conc_padded, head_padded, cond_padded):
    head_center = head_padded[1:-1, 1:-1, 1:-1]
    conduct = cond_padded[1:-1, 1:-1, 1:-1]
    change = jnp.zeros_like(concentration)
    for beside, head_beside, cond_beside in zip(six_sides(conc_padded), six_sides(head_padded), six_sides(cond_padded)):
        face_cond = harmonic(conduct, cond_beside)
        velocity = face_cond * (head_center - head_beside)
        change = change + jnp.maximum(velocity, 0.0) * concentration + jnp.minimum(velocity, 0.0) * beside
        change = change + dispersion * face_cond * (concentration - beside)
    return concentration - time_step * change

def solve_system(jacobian, mismatch):
    dimension = mismatch.shape[0]
    factor = [[None] * dimension for i in range(dimension)]
    inverse = [None] * dimension
    for j in range(dimension):
        for i in range(j, dimension):
            running = jacobian[i * dimension + j] + (1.0 if i == j else 0.0)
            for k in range(j):
                running = running - factor[i][k] * factor[j][k]
            if i == j:
                diag_root = jnp.sqrt(running)
                factor[j][j] = diag_root
                inverse[j] = 1.0 / diag_root
            else:
                factor[i][j] = running * inverse[j]
    forward = []
    for i in range(dimension):
        running = mismatch[i]
        for k in range(i):
            running = running - factor[i][k] * forward[k]
        forward.append(running * inverse[i])
    answer = [None] * dimension
    for i in reversed(range(dimension)):
        running = forward[i]
        for k in range(i + 1, dimension):
            running = running - factor[k][i] * answer[k]
        answer[i] = running * inverse[i]
    return jnp.stack(answer, 0)

def reaction(concentration, labels, rate_table, stoich, log_equil):
    rate_cells = lookup_rows(labels, rate_table)
    pair_products = (stoich[:, None, :] * stoich[None, :, :]).reshape(-1, stoich.shape[1])
    iterate = concentration
    for newton_pass in range(NEWTON):
        affinity = jnp.dot(stoich.T, iterate, precision=lax.Precision.HIGHEST, preferred_element_type=jnp.float32) - log_equil[:, None]
        tangent = jnp.tanh(affinity)
        mismatch = iterate - concentration + reaction_span * jnp.dot(stoich, rate_cells * tangent, precision=lax.Precision.HIGHEST, preferred_element_type=jnp.float32)
        jacobian = reaction_span * jnp.dot(pair_products, rate_cells * (1.0 - tangent * tangent), precision=lax.Precision.HIGHEST, preferred_element_type=jnp.float32)
        iterate = iterate - newton_damping * solve_system(jacobian, mismatch)
    return iterate

def flow_operator(field, storage, faces):
    padded = jnp.pad(field, 1)
    result = storage * field
    for face_cond, beside in zip(faces, six_sides(padded)):
        result = result + face_cond * (field - beside)
    return result

def reference(previous_head, recharge, soil_zone, soil_cond, soil_store, species, mineral_zone, rate_table, stoich, log_equil):
    conduct = lookup(soil_zone, soil_cond)
    storage = lookup(soil_zone, soil_store)
    cond_padded = jnp.pad(conduct, 1)
    faces = [harmonic(conduct, beside) for beside in six_sides(cond_padded)]
    source = storage * previous_head + recharge
    head_field = jnp.zeros_like(source)
    residual = source
    direction = source
    norm_now = jnp.sum(residual * residual)
    for iteration in range(ITERS):
        image = flow_operator(direction, storage, faces)
        alpha = norm_now / jnp.sum(direction * image)
        head_field = head_field + alpha * direction
        residual = residual - alpha * image
        norm_next = jnp.sum(residual * residual)
        direction = residual + norm_next / norm_now * direction
        norm_now = norm_next
    head_padded = jnp.pad(head_field, 1)
    moved = lax.map(lambda single: transport(single, jnp.pad(single, 1), head_padded, cond_padded), species)
    layers = moved.transpose(1, 0, 2, 3).reshape(NZ, S, NX * NY)
    labels = mineral_zone.reshape(NZ, NX * NY)
    reacted = lax.map(lambda couple: reaction(couple[0], couple[1], rate_table, stoich, log_equil), (layers, labels))
    species_out = reacted.reshape(NZ, S, NX, NY).transpose(1, 0, 2, 3)
    return (head_field, species_out)
```

```python
import functools

import jax
import jax.numpy as jnp
from jax import lax
from jax.experimental import pallas as pl
from jax.experimental.pallas import tpu as pltpu
from jax.sharding import PartitionSpec as P

NEWTON = 2
BLOCK = 3

time_step = 0.05
dispersion = 0.5
reaction_span = 0.5
newton_damping = 0.5

MESH = pl.DeviceIdType.MESH
EXACT = lax.Precision.HIGHEST


def table_lookup(labels, table):
    found = jnp.full(labels.shape, table[0], jnp.float32)
    for level in range(1, table.shape[0]):
        found = jnp.where(labels == level, table[level], found)
    return found


def harmonic_safe(center, other):
    return 2.0 * center * other / jnp.maximum(center + other, 1e-30)


def shifted(field, offset, axis):
    size = field.shape[axis]
    return pltpu.roll(field, (-offset) % size, axis)


def layer_above(field):
    return jnp.concatenate([field[1:], field[-1:]], axis=0)


def layer_below(field):
    return jnp.concatenate([field[:1], field[:-1]], axis=0)


def six_faces(conduct):
    east = harmonic_safe(conduct, shifted(conduct, 1, 2))
    south = harmonic_safe(conduct, shifted(conduct, 1, 1))
    top = harmonic_safe(conduct[:-1], conduct[1:])
    none = jnp.zeros_like(conduct[:1])
    return (
        jnp.concatenate([top, none], axis=0),
        jnp.concatenate([none, top], axis=0),
        south,
        shifted(south, -1, 1),
        east,
        shifted(east, -1, 2),
    )


def six_beside(field):
    return (
        layer_above(field),
        layer_below(field),
        shifted(field, 1, 1),
        shifted(field, -1, 1),
        shifted(field, 1, 2),
        shifted(field, -1, 2),
    )


def apply_flow(field, storage, faces):
    result = storage * field
    for face, beside in zip(faces, six_beside(field)):
        result = result + face * (field - beside)
    return result


def add_scaled(left, scale, right):
    total = dict(left)
    for key, value in right.items():
        term = scale * value
        total[key] = total[key] + term if key in total else term
    return total


def cg_block(rr, pr, pp, least, most, same):
    one = jnp.ones_like(least)
    direction = {(0, 0): one}
    residual = {(0 if same else 1, 0): one}
    change = {}
    live = None
    for step in range(BLOCK):
        alpha = (pr if step == 0 else rr)[0] / jnp.maximum(pp[1], 1e-30)
        alpha = jnp.clip(alpha, least, most)
        if live is not None:
            alpha = jnp.where(live, alpha, 0.0)
        change = add_scaled(change, alpha, direction)
        image = {(part, power + 1): value for (part, power), value in direction.items()}
        residual = add_scaled(residual, -alpha, image)
        if len(pp) < 3 or len(pr) < 2:
            break
        square = alpha * alpha
        count = min(len(rr), len(pr) - 1, len(pp) - 2)
        next_rr = [rr[k] - 2.0 * alpha * pr[k + 1] + square * pp[k + 2] for k in range(count)]
        count = min(len(pr), len(pp) - 1)
        next_pr = [pr[k] - alpha * pp[k + 1] for k in range(count)]
        above = next_rr[0] > 1e-6 * (rr[0] + square * pp[2])
        live = above if live is None else live & above
        beta = jnp.where(live, next_rr[0] / jnp.maximum(rr[0], 1e-37), 0.0)
        direction = add_scaled(residual, beta, direction)
        count = min(len(next_rr), len(next_pr))
        next_pp = [
            next_rr[k] + 2.0 * beta * next_pr[k] + beta * beta * pp[k] for k in range(count)
        ]
        pr = [next_rr[k] + beta * next_pr[k] for k in range(count)]
        rr, pp = next_rr, next_pp
    return change, residual, direction


def combine(polynomial, parts):
    total = None
    for (part, power), value in sorted(polynomial.items()):
        term = value[None] * parts[part][power]
        total = term if total is None else total + term
    return total


def flow_kernel(
    gx_count,
    sp_count,
    inner,
    previous_head,
    recharge,
    soil_zone,
    soil_cond,
    soil_store,
    head_out,
    field,
    rows_in,
    edge_out,
    edge_in,
    near_0,
    far_0,
    near_1,
    far_1,
    halo_send,
    halo_recv,
    sum_send,
    sum_recv,
):
    g = lax.axis_index("gx")
    s = lax.axis_index("sp")
    outer = gx_count // inner
    low, high = g % inner, g // inner
    plane = high * sp_count + s
    near_peers = [(high * inner + (low + k) % inner, s) for k in range(1, inner)]
    far_peers = [
        (((high + k // sp_count) % outer) * inner + low, (s + k % sp_count) % sp_count)
        for k in range(1, outer * sp_count)
    ]

    def beside(rows, columns):
        return ((g + rows + gx_count) % gx_count, (s + columns + sp_count) % sp_count)

    offsets = [(rows, columns) for rows in (-1, 0, 1) for columns in (-1, 0, 1) if (rows, columns) != (0, 0)]
    barrier = pltpu.get_barrier_semaphore()
    peers = [beside(*offset) for offset in offsets] + near_peers + far_peers
    for peer in peers:
        pl.semaphore_signal(barrier, inc=1, device_id=peer, device_id_type=MESH)

    zone = soil_zone[...]
    field[0] = table_lookup(zone, soil_store) * previous_head[...] + recharge[...]
    field[1] = zone.astype(jnp.float32)
    line = lax.broadcasted_iota(jnp.int32, (16, 128), 0)
    lane = lax.broadcasted_iota(jnp.int32, (16, 128), 1)
    pick = (lane == jnp.where(line < 8, line, line + 112)).astype(jnp.float32)
    edge_out[...] = lax.dot_general(
        pick,
        field[...].reshape(128, 128),
        (((1,), (1,)), ((), ())),
        precision=EXACT,
        preferred_element_type=jnp.float32,
    )

    pl.semaphore_wait(barrier, len(peers))
    halo = []
    for number, (rows, columns) in enumerate(offsets):
        if columns == 0:
            source, target = field, rows_in.at[0 if rows == 1 else 1]
        else:
            first = 8 if columns == 1 else 0
            source = edge_out.at[pl.ds(first, 8)]
            target = edge_in.at[1 - rows, pl.ds(first, 8)]
        copy = pltpu.make_async_remote_copy(
            src_ref=source,
            dst_ref=target,
            send_sem=halo_send.at[number],
            recv_sem=halo_recv.at[number],
            device_id=beside(rows, columns),
            device_id_type=MESH,
        )
        copy.start()
        halo.append(copy)
    for copy in halo:
        copy.wait_recv()

    row_blocks = []
    for block, center in enumerate((rows_in[0], field[...], rows_in[1])):
        side = lax.dot_general(
            edge_in[block],
            pick,
            (((0,), (0,)), ((), ())),
            precision=EXACT,
            preferred_element_type=jnp.float32,
        ).reshape(2, 8, 8, 128)
        row_blocks.append(jnp.concatenate([center, side], axis=3))
    wide = jnp.concatenate(row_blocks, axis=2)
    row = lax.broadcasted_iota(jnp.int32, (24, 256), 0)
    column = lax.broadcasted_iota(jnp.int32, (24, 256), 1)
    first_row = jnp.where(g > 0, 0, 8)
    end_row = jnp.where(g < gx_count - 1, 24, 16)
    end_right = jnp.where(s < sp_count - 1, 136, 128)
    first_left = jnp.where(s > 0, 248, 256)
    inside = (
        (row >= first_row)
        & (row < end_row)
        & ((column < end_right) | (column >= first_left))
    )[None]
    source = jnp.where(inside, wide[0], 0.0)
    conduct = jnp.where(inside, table_lookup(wide[1], soil_cond), 0.0)
    storage = jnp.where(inside, table_lookup(wide[1], soil_store), 0.0)
    faces = six_faces(conduct)

    store_least, store_most, cond_most = soil_store[0], soil_store[0], soil_cond[0]
    for level in range(1, soil_store.shape[0]):
        store_least = jnp.minimum(store_least, soil_store[level])
        store_most = jnp.maximum(store_most, soil_store[level])
        cond_most = jnp.maximum(cond_most, soil_cond[level])
    most = 1.0 / jnp.full((1, 256), store_least, jnp.float32)
    least = 1.0 / jnp.full((1, 256), store_most + 12.0 * cond_most, jnp.float32)

    sends = []

    def exchange(buffer, slot, mine, others, number):
        buffer[slot] = mine
        for peer in others:
            copy = pltpu.make_async_remote_copy(
                src_ref=buffer.at[slot],
                dst_ref=buffer.at[slot],
                send_sem=sum_send.at[number],
                recv_sem=sum_recv.at[number],
                device_id=peer,
                device_id_type=MESH,
            )
            copy.start()
        all_others = buffer.at[pl.ds(0, len(others))]
        pltpu.make_async_copy(all_others, all_others, sum_recv.at[number]).wait()
        sends.append(pltpu.make_async_copy(all_others, all_others, sum_send.at[number]))
        return jnp.sum(buffer[...], axis=0)

    def global_sums(pairs, near, far, number):
        lines = near.shape[1]
        index = lax.broadcasted_iota(jnp.int32, (lines, 128), 0)
        partial = jnp.zeros((lines, 128), jnp.float32)
        for position, (left, right) in enumerate(pairs):
            product = left[:, 8:16, :128] * right[:, 8:16, :128]
            total = jnp.sum(jnp.sum(product, axis=0), axis=0, keepdims=True)
            partial = jnp.where(index == position, total, partial)
        partial = exchange(near, low, partial, near_peers, number)
        partial = exchange(far, plane, partial, far_peers, number + 1)
        totals = jnp.broadcast_to(jnp.sum(partial, axis=1, keepdims=True), (lines, 256))
        return [totals[k : k + 1] for k in range(len(pairs))]

    powers = [source]
    for k in range(BLOCK):
        powers.append(apply_flow(powers[-1], storage, faces))
    pairs = [(powers[k // 2], powers[(k + 1) // 2]) for k in range(2 * BLOCK + 1)]
    moments = global_sums(pairs, near_0, far_0, 0)
    change, residual, direction = cg_block(moments, moments, moments, least, most, True)
    head = combine(change, [powers])
    residual = combine(residual, [powers])
    direction = combine(direction, [powers])

    p_powers = [direction]
    for k in range(BLOCK):
        p_powers.append(apply_flow(p_powers[-1], storage, faces))
    r_powers = [residual]
    for k in range(BLOCK - 1):
        r_powers.append(apply_flow(r_powers[-1], storage, faces))
    pairs = [(r_powers[k // 2], r_powers[(k + 1) // 2]) for k in range(4)]
    pairs += [(p_powers[(k + 1) // 2], r_powers[k // 2]) for k in range(5)]
    pairs += [(p_powers[k // 2], p_powers[(k + 1) // 2]) for k in range(6)]
    moments = global_sums(pairs, near_1, far_1, 2)
    change, _, _ = cg_block(moments[:4], moments[4:9], moments[9:], least, most, False)
    head = head + combine(change, [p_powers, r_powers])
    head_out[...] = head[:, 8:16, :128]

    for copy in halo:
        copy.wait_send()
    for copy in sends:
        copy.wait()


def solve_flow(mesh, previous_head, recharge, soil_zone, soil_cond, soil_store):
    gx_count, sp_count = mesh.shape["gx"], mesh.shape["sp"]
    inner = min(8, gx_count // 2)
    far_count = gx_count // inner * sp_count
    vmem = pl.BlockSpec(memory_space=pltpu.VMEM)
    smem = pl.BlockSpec(memory_space=pltpu.SMEM)
    return pl.pallas_call(
        functools.partial(flow_kernel, gx_count, sp_count, inner),
        out_shape=jax.ShapeDtypeStruct((8, 8, 128), jnp.float32),
        in_specs=[vmem, vmem, vmem, smem, smem],
        out_specs=vmem,
        scratch_shapes=[
            pltpu.VMEM((2, 8, 8, 128), jnp.float32),
            pltpu.VMEM((2, 2, 8, 8, 128), jnp.float32),
            pltpu.VMEM((16, 128), jnp.float32),
            pltpu.VMEM((3, 16, 128), jnp.float32),
            pltpu.VMEM((inner, 8, 128), jnp.float32),
            pltpu.VMEM((far_count, 8, 128), jnp.float32),
            pltpu.VMEM((inner, 16, 128), jnp.float32),
            pltpu.VMEM((far_count, 16, 128), jnp.float32),
            pltpu.SemaphoreType.DMA((8,)),
            pltpu.SemaphoreType.DMA((8,)),
            pltpu.SemaphoreType.DMA((4,)),
            pltpu.SemaphoreType.DMA((4,)),
        ],
        compiler_params=pltpu.CompilerParams(
            collective_id=0, has_side_effects=True, vmem_limit_bytes=48 * 1024 * 1024
        ),
    )(previous_head, recharge, soil_zone, soil_cond, soil_store)


def padded_2(cells, sides, width):
    for axis, dim in sides:
        count = lax.axis_size(axis)
        ends = count - 1
        head = lax.slice_in_dim(cells, 0, width, axis=dim)
        tail = lax.slice_in_dim(cells, cells.shape[dim] - width, cells.shape[dim], axis=dim)
        cells = jnp.concatenate(
            [
                lax.ppermute(tail, axis, [(i, (i + 1) % count) for i in range(ends)]),
                cells,
                lax.ppermute(head, axis, [((i + 1) % count, i) for i in range(ends)]),
            ],
            axis=dim,
        )
    return cells


def harmonic(center, other):
    return 2.0 * center * other / (center + other)


def six_sides(padded):
    return [
        padded[..., 2:, 1:-1, 1:-1],
        padded[..., :-2, 1:-1, 1:-1],
        padded[..., 1:-1, 2:, 1:-1],
        padded[..., 1:-1, :-2, 1:-1],
        padded[..., 1:-1, 1:-1, 2:],
        padded[..., 1:-1, 1:-1, :-2],
    ]


def lookup(labels, entries):
    levels = jnp.arange(entries.shape[0], dtype=jnp.int32).reshape((-1,) + (1,) * labels.ndim)
    return jnp.sum(jnp.where(labels[None] == levels, entries.reshape(levels.shape), 0.0), axis=0)


def lookup_rows(labels, entries):
    levels = jnp.arange(entries.shape[0], dtype=jnp.int32)[:, None, None]
    return jnp.sum(jnp.where(labels[None, None, :] == levels, entries[:, :, None], 0.0), axis=0)


def transport(concentration, conc_padded, head_padded, cond_padded):
    head_center = head_padded[1:-1, 1:-1, 1:-1]
    conduct = cond_padded[1:-1, 1:-1, 1:-1]
    change = jnp.zeros_like(concentration)
    for beside, head_beside, cond_beside in zip(
        six_sides(conc_padded), six_sides(head_padded), six_sides(cond_padded)
    ):
        face_cond = harmonic(conduct, cond_beside)
        velocity = face_cond * (head_center - head_beside)
        change = (
            change
            + jnp.maximum(velocity, 0.0) * concentration
            + jnp.minimum(velocity, 0.0) * beside
        )
        change = change + dispersion * face_cond * (concentration - beside)
    return concentration - time_step * change


def solve_system(jacobian, mismatch):
    dimension = mismatch.shape[0]
    factor = [[None] * dimension for i in range(dimension)]
    inverse = [None] * dimension
    for j in range(dimension):
        for i in range(j, dimension):
            running = jacobian[i * dimension + j] + (1.0 if i == j else 0.0)
            for k in range(j):
                running = running - factor[i][k] * factor[j][k]
            if i == j:
                diag_root = jnp.sqrt(running)
                factor[j][j] = diag_root
                inverse[j] = 1.0 / diag_root
            else:
                factor[i][j] = running * inverse[j]
    forward = []
    for i in range(dimension):
        running = mismatch[i]
        for k in range(i):
            running = running - factor[i][k] * forward[k]
        forward.append(running * inverse[i])
    answer = [None] * dimension
    for i in reversed(range(dimension)):
        running = forward[i]
        for k in range(i + 1, dimension):
            running = running - factor[k][i] * answer[k]
        answer[i] = running * inverse[i]
    return jnp.stack(answer, 0)


def reaction(concentration, labels, rate_table, stoich, log_equil):
    rate_cells = lookup_rows(labels, rate_table)
    pair_products = (stoich[:, None, :] * stoich[None, :, :]).reshape(-1, stoich.shape[1])
    iterate = concentration
    for newton_pass in range(NEWTON):
        affinity = (
            jnp.dot(
                stoich.T,
                iterate,
                precision=lax.Precision.HIGHEST,
                preferred_element_type=jnp.float32,
            )
            - log_equil[:, None]
        )
        tangent = jnp.tanh(affinity)
        mismatch = (
            iterate
            - concentration
            + reaction_span
            * jnp.dot(
                stoich,
                rate_cells * tangent,
                precision=lax.Precision.HIGHEST,
                preferred_element_type=jnp.float32,
            )
        )
        jacobian = reaction_span * jnp.dot(
            pair_products,
            rate_cells * (1.0 - tangent * tangent),
            precision=lax.Precision.HIGHEST,
            preferred_element_type=jnp.float32,
        )
        iterate = iterate - newton_damping * solve_system(jacobian, mismatch)
    return iterate


def pad_vertical(field):
    return jnp.pad(field, ((1, 1), (0, 0), (0, 0)))


def to_cells(block):
    return lax.all_to_all(block, "sp", split_axis=3, concat_axis=0, tiled=True)


def per_device(
    mesh,
    previous_head,
    recharge,
    soil_zone,
    soil_cond,
    soil_store,
    species,
    mineral_zone,
    rate_table,
    stoich,
    log_equil,
):
    conduct = lookup(soil_zone, soil_cond)
    head_field = solve_flow(mesh, previous_head, recharge, soil_zone, soil_cond, soil_store)
    head_rows, cond_rows = (
        lax.all_gather(head_field, "sp", axis=2, tiled=True),
        lax.all_gather(conduct, "sp", axis=2, tiled=True),
    )
    stacked = jnp.concatenate([species, head_rows[None], cond_rows[None]], 0)
    padded = padded_2(stacked, (("gx", 2),), 1)
    padded = jnp.pad(padded, ((0, 0), (1, 1), (0, 0), (1, 1)))
    moved = transport(species, padded[:-2], padded[-2], padded[-1])
    cells = to_cells(moved)
    block_shape = cells.shape
    reacted = reaction(
        cells.reshape(block_shape[0], -1), mineral_zone.reshape(-1), rate_table, stoich, log_equil
    )
    reacted = reacted.reshape(block_shape)
    species_out = lax.all_to_all(reacted, "sp", split_axis=0, concat_axis=3, tiled=True)
    return (head_field, species_out)


def solution(mesh):
    in_specs = (
        P(None, "gx", "sp"),
        P(None, "gx", "sp"),
        P(None, "gx", "sp"),
        P(),
        P(),
        P("sp", None, "gx", None),
        P(None, "gx", "sp"),
        P(),
        P(),
        P(),
    )
    out_specs = (P(None, "gx", "sp"), P("sp", None, "gx", None))
    return jax.shard_map(
        functools.partial(per_device, mesh), mesh=mesh, in_specs=in_specs, out_specs=out_specs, check_vma=False
    )
```

```python
import functools

import jax
import jax.numpy as jnp
from jax import lax
from jax.experimental import pallas as pl
from jax.experimental.pallas import tpu as pltpu
from jax.sharding import PartitionSpec as P

NEWTON = 2
BLOCK = 3

time_step = 0.05
dispersion = 0.5
reaction_span = 0.5
newton_damping = 0.5

MESH = pl.DeviceIdType.MESH
EXACT = lax.Precision.HIGHEST


def table_lookup(labels, table):
    size = table.shape[0] if hasattr(table, "shape") else len(table)
    found = jnp.full(labels.shape, table[0], jnp.float32)
    for level in range(1, size):
        found = jnp.where(labels == level, table[level], found)
    return found


def harmonic_safe(center, other):
    return 2.0 * center * other / jnp.maximum(center + other, 1e-30)


def shifted(field, offset, axis):
    size = field.shape[axis]
    return pltpu.roll(field, (-offset) % size, axis)


def layer_above(field):
    return jnp.concatenate([field[1:], field[-1:]], axis=0)


def layer_below(field):
    return jnp.concatenate([field[:1], field[:-1]], axis=0)


def six_faces(conduct):
    east = harmonic_safe(conduct, shifted(conduct, 1, 2))
    south = harmonic_safe(conduct, shifted(conduct, 1, 1))
    top = harmonic_safe(conduct[:-1], conduct[1:])
    none = jnp.zeros_like(conduct[:1])
    return (
        jnp.concatenate([top, none], axis=0),
        jnp.concatenate([none, top], axis=0),
        south,
        shifted(south, -1, 1),
        east,
        shifted(east, -1, 2),
    )


def six_beside(field):
    return (
        layer_above(field),
        layer_below(field),
        shifted(field, 1, 1),
        shifted(field, -1, 1),
        shifted(field, 1, 2),
        shifted(field, -1, 2),
    )


def apply_flow(field, storage, faces):
    result = storage * field
    for face, beside in zip(faces, six_beside(field)):
        result = result + face * (field - beside)
    return result


def add_scaled(left, scale, right):
    total = dict(left)
    for key, value in right.items():
        term = scale * value
        total[key] = total[key] + term if key in total else term
    return total


def cg_block(rr, pr, pp, least, most, same):
    one = jnp.ones_like(least)
    direction = {(0, 0): one}
    residual = {(0 if same else 1, 0): one}
    change = {}
    live = None
    for step in range(BLOCK):
        alpha = (pr if step == 0 else rr)[0] / jnp.maximum(pp[1], 1e-30)
        alpha = jnp.clip(alpha, least, most)
        if live is not None:
            alpha = jnp.where(live, alpha, 0.0)
        change = add_scaled(change, alpha, direction)
        image = {(part, power + 1): value for (part, power), value in direction.items()}
        residual = add_scaled(residual, -alpha, image)
        if len(pp) < 3 or len(pr) < 2:
            break
        square = alpha * alpha
        count = min(len(rr), len(pr) - 1, len(pp) - 2)
        next_rr = [rr[k] - 2.0 * alpha * pr[k + 1] + square * pp[k + 2] for k in range(count)]
        count = min(len(pr), len(pp) - 1)
        next_pr = [pr[k] - alpha * pp[k + 1] for k in range(count)]
        above = next_rr[0] > 1e-6 * (rr[0] + square * pp[2])
        live = above if live is None else live & above
        beta = jnp.where(live, next_rr[0] / jnp.maximum(rr[0], 1e-37), 0.0)
        direction = add_scaled(residual, beta, direction)
        count = min(len(next_rr), len(next_pr))
        next_pp = [
            next_rr[k] + 2.0 * beta * next_pr[k] + beta * beta * pp[k] for k in range(count)
        ]
        pr = [next_rr[k] + beta * next_pr[k] for k in range(count)]
        rr, pp = next_rr, next_pp
    return change, residual, direction


def combine(polynomial, parts):
    total = None
    for (part, power), value in sorted(polynomial.items()):
        term = value[None] * parts[part][power]
        total = term if total is None else total + term
    return total


def column_edges(pick, block):
    return lax.dot_general(
        pick,
        block,
        (((1,), (1,)), ((), ())),
        precision=EXACT,
        preferred_element_type=jnp.float32,
    )


def spread_edges(edges, pick):
    return lax.dot_general(
        edges,
        pick,
        (((0,), (0,)), ((), ())),
        precision=EXACT,
        preferred_element_type=jnp.float32,
    )


def weighted(scales, fields):
    total = None
    for scale, field in zip(scales, fields):
        term = scale * field
        total = term if total is None else total + term
    return total


def mineral_correction(gram, slope, start):
    count = len(start)
    right = [weighted([gram[i][k] for k in range(count)], start) for i in range(count)]
    schur = {(i, j): gram[i][j] for i in range(count) for j in range(i + 1)}
    pivot, lower = [None] * count, {}
    for k in range(count):
        pivot[k] = slope[k] / (1.0 + slope[k] * schur[k, k])
        for i in range(k + 1, count):
            lower[i, k] = schur[i, k] * pivot[k]
        for i in range(k + 1, count):
            right[i] = right[i] - lower[i, k] * right[k]
            for j in range(k + 1, i + 1):
                schur[i, j] = schur[i, j] - lower[i, k] * schur[j, k]
    answer = [None] * count
    for k in reversed(range(count)):
        value = pivot[k] * right[k]
        for i in range(k + 1, count):
            value = value - lower[i, k] * answer[i]
        answer[k] = value
    return answer


def react(moved, labels, rate_table, stoich, log_equil, gram):
    zones, minerals = rate_table.shape
    species = len(moved)
    rates = [table_lookup(labels, [rate_table[z, m] for z in range(zones)]) for m in range(minerals)]
    base = [
        weighted([stoich[c, m] for c in range(species)], moved) - log_equil[m]
        for m in range(minerals)
    ]
    extent = None
    for newton_pass in range(NEWTON):
        affinity = base
        if extent is not None:
            affinity = [base[m] + weighted(gram[m], extent) for m in range(minerals)]
        tangent = [jnp.tanh(value) for value in affinity]
        start = [reaction_span * rates[m] * tangent[m] for m in range(minerals)]
        if extent is not None:
            start = [extent[m] + start[m] for m in range(minerals)]
        slope = [
            reaction_span * rates[m] * jnp.maximum(1.0 - tangent[m] * tangent[m], 0.0)
            for m in range(minerals)
        ]
        correction = mineral_correction(gram, slope, start)
        step = [newton_damping * (start[m] - correction[m]) for m in range(minerals)]
        extent = [-step[m] if extent is None else extent[m] - step[m] for m in range(minerals)]
    return [
        moved[c] + weighted([stoich[c, m] for m in range(minerals)], extent)
        for c in range(species)
    ]


def step_kernel(
    gx_count,
    sp_count,
    inner,
    previous_head_in,
    recharge_in,
    soil_zone_in,
    soil_cond,
    soil_store,
    species_in,
    mineral_zone_in,
    rate_table,
    stoich,
    log_equil,
    head_out,
    species_out,
    previous_head,
    recharge,
    soil_zone,
    mineral_zone,
    species,
    field,
    rows_in,
    edge_out,
    edge_in,
    near_0,
    far_0,
    near_1,
    far_1,
    conc,
    ends_out,
    ends_in,
    sides_out,
    sides_in,
    beside_conc,
    weights,
    moved,
    reacted,
    gram_table,
    load_sem,
    halo_send,
    halo_recv,
    sum_send,
    sum_recv,
    spread_send,
    spread_recv,
    result_sem,
):
    g = lax.axis_index("gx")
    s = lax.axis_index("sp")
    outer = gx_count // inner
    low, high = g % inner, g // inner
    plane = high * sp_count + s
    near_peers = [(high * inner + (low + k) % inner, s) for k in range(1, inner)]
    far_peers = [
        (((high + k // sp_count) % outer) * inner + low, (s + k % sp_count) % sp_count)
        for k in range(1, outer * sp_count)
    ]
    group = species_in.shape[0]
    layers = species_in.shape[1]

    def columns_of(device):
        return pl.ds(pl.multiple_of(device * 128, 128), 128)

    def beside(rows, columns):
        return ((g + rows + gx_count) % gx_count, (s + columns) % sp_count)

    def remote(source, target, send, recv, peer):
        copy = pltpu.make_async_remote_copy(
            src_ref=source,
            dst_ref=target,
            send_sem=send,
            recv_sem=recv,
            device_id=peer,
            device_id_type=MESH,
        )
        copy.start()
        return copy

    loads = [
        pltpu.make_async_copy(source, target, load_sem.at[number])
        for number, (source, target) in enumerate(
            (
                (soil_zone_in, soil_zone),
                (previous_head_in, previous_head),
                (recharge_in, recharge),
                (species_in, species),
                (species_in.at[:, :, :, columns_of(s)], conc.at[pl.ds(group * s, group)]),
                (mineral_zone_in, mineral_zone),
            )
        )
    ]
    for copy in loads:
        copy.start()

    offsets = [(rows, columns) for rows in (-1, 0, 1) for columns in (-1, 0, 1) if (rows, columns) != (0, 0)]
    others = [k for k in range(2, sp_count - 1)]
    barrier = pltpu.get_barrier_semaphore()
    peers = [beside(*offset) for offset in offsets] + near_peers + far_peers
    peers += [beside(rows, k) for rows in (-1, 1) for k in others]
    for peer in peers:
        pl.semaphore_signal(barrier, inc=1, device_id=peer, device_id_type=MESH)

    for copy in loads[:3]:
        copy.wait()
    zone = soil_zone[...]
    field[0] = table_lookup(zone, soil_store) * previous_head[...] + recharge[...]
    field[1] = zone.astype(jnp.float32)
    line = lax.broadcasted_iota(jnp.int32, (16, 128), 0)
    lane = lax.broadcasted_iota(jnp.int32, (16, 128), 1)
    pick = (lane == jnp.where(line < 8, line, line + 112)).astype(jnp.float32)
    edge_out[...] = column_edges(pick, field[...].reshape(128, 128))

    pl.semaphore_wait(barrier, len(peers))
    halo = []
    for number, (rows, columns) in enumerate(offsets):
        if columns == 0:
            source, target = field, rows_in.at[0 if rows == 1 else 1]
        else:
            first = 8 if columns == 1 else 0
            source = edge_out.at[pl.ds(first, 8)]
            target = edge_in.at[1 - rows, pl.ds(first, 8)]
        halo.append(
            remote(source, target, halo_send.at[number], halo_recv.at[number], beside(rows, columns))
        )

    mine = pl.ds(group * s, group)
    loads[3].wait()
    for k in range(1, sp_count):
        to = (s + k) % sp_count
        remote(
            species.at[:, :, :, columns_of(to)],
            conc.at[mine],
            spread_send.at[0],
            spread_recv.at[0],
            (g, to),
        )
    width = species.shape[3]
    line = lax.broadcasted_iota(jnp.int32, (2 * sp_count, width), 0)
    lane = lax.broadcasted_iota(jnp.int32, (2 * sp_count, width), 1)
    wanted = jnp.where(line % 2 == 0, (line // 2) * 128 - 1, (line // 2) * 128 + 128)
    tiles = group * layers * 8
    sides_out[:, :tiles] = column_edges(
        (lane == wanted).astype(jnp.float32), species[...].reshape(tiles, width)
    )
    for layer in range(layers):
        ends_out[0, :, layer : layer + 1, :] = species[:, layer, 0:1, :]
        ends_out[1, :, layer : layer + 1, :] = species[:, layer, 7:8, :]
    sides_in[s] = sides_out[...]
    for k in range(1, sp_count):
        to = (s + k) % sp_count
        remote(sides_out, sides_in.at[s], spread_send.at[1], spread_recv.at[1], (g, to))
    for k in range(sp_count):
        to = (s + k) % sp_count
        for rows in (-1, 1):
            remote(
                ends_out.at[0 if rows == -1 else 1, :, :, columns_of(to)],
                ends_in.at[1 if rows == -1 else 0, mine],
                spread_send.at[2],
                spread_recv.at[2],
                beside(rows, k),
            )

    for copy in halo:
        copy.wait_recv()

    row_blocks = []
    for block, center in enumerate((rows_in[0], field[...], rows_in[1])):
        side = spread_edges(edge_in[block], pick).reshape(2, 8, 8, 128)
        row_blocks.append(jnp.concatenate([center, side], axis=3))
    wide = jnp.concatenate(row_blocks, axis=2)
    row = lax.broadcasted_iota(jnp.int32, (24, 256), 0)
    column = lax.broadcasted_iota(jnp.int32, (24, 256), 1)
    first_row = jnp.where(g > 0, 0, 8)
    end_row = jnp.where(g < gx_count - 1, 24, 16)
    end_right = jnp.where(s < sp_count - 1, 136, 128)
    first_left = jnp.where(s > 0, 248, 256)
    inside = (
        (row >= first_row)
        & (row < end_row)
        & ((column < end_right) | (column >= first_left))
    )[None]
    source = jnp.where(inside, wide[0], 0.0)
    conduct = jnp.where(inside, table_lookup(wide[1], soil_cond), 0.0)
    storage = jnp.where(inside, table_lookup(wide[1], soil_store), 0.0)
    faces = six_faces(conduct)

    store_least, store_most, cond_most = soil_store[0], soil_store[0], soil_cond[0]
    for level in range(1, soil_store.shape[0]):
        store_least = jnp.minimum(store_least, soil_store[level])
        store_most = jnp.maximum(store_most, soil_store[level])
        cond_most = jnp.maximum(cond_most, soil_cond[level])
    most = 1.0 / jnp.full((1, 256), store_least, jnp.float32)
    least = 1.0 / jnp.full((1, 256), store_most + 12.0 * cond_most, jnp.float32)

    sends = []

    def exchange(buffer, slot, value, to_peers, number, meanwhile):
        buffer[slot] = value
        for peer in to_peers:
            remote(buffer.at[slot], buffer.at[slot], sum_send.at[number], sum_recv.at[number], peer)
        if meanwhile is not None:
            meanwhile()
        all_others = buffer.at[pl.ds(0, len(to_peers))]
        pltpu.make_async_copy(all_others, all_others, sum_recv.at[number]).wait()
        sends.append(pltpu.make_async_copy(all_others, all_others, sum_send.at[number]))
        return jnp.sum(buffer[...], axis=0)

    def global_sums(pairs, near, far, number, first_work, second_work):
        lines = near.shape[1]
        index = lax.broadcasted_iota(jnp.int32, (lines, 128), 0)
        partial = jnp.zeros((lines, 128), jnp.float32)
        for position, (left, right) in enumerate(pairs):
            product = left[:, 8:16, :128] * right[:, 8:16, :128]
            total = jnp.sum(jnp.sum(product, axis=0), axis=0, keepdims=True)
            partial = jnp.where(index == position, total, partial)
        partial = exchange(near, low, partial, near_peers, number, first_work)
        partial = exchange(far, plane, partial, far_peers, number + 1, second_work)
        totals = jnp.broadcast_to(jnp.sum(partial, axis=1, keepdims=True), (lines, 256))
        return [totals[k : k + 1] for k in range(len(pairs))]

    species_count, mineral_count = stoich.shape

    def fill_gram():
        columns = [
            [stoich[c, m] for c in range(species_count)] for m in range(mineral_count)
        ]
        for i in range(mineral_count):
            for j in range(i + 1):
                terms = [a * b for a, b in zip(columns[i], columns[j])]
                while len(terms) > 1:
                    terms = [sum(terms[k : k + 2][1:], terms[k]) for k in range(0, len(terms), 2)]
                gram_table[i, j] = terms[0]

    def place_species():
        whole = conc.at[pl.ds(0, group * (sp_count - 1))]
        pltpu.make_async_copy(whole, whole, spread_recv.at[0]).wait()
        part = sides_in.at[pl.ds(0, sp_count - 1)]
        pltpu.make_async_copy(part, part, spread_recv.at[1]).wait()
        pltpu.make_async_copy(ends_in, ends_in, spread_recv.at[2]).wait()
        loads[4].wait()
        line = lax.broadcasted_iota(jnp.int32, (2 * sp_count, 128), 0)
        lane = lax.broadcasted_iota(jnp.int32, (2 * sp_count, 128), 1)
        place = (((line == 2 * s) & (lane == 0)) | ((line == 2 * s + 1) & (lane == 127))).astype(
            jnp.float32
        )
        row = lax.broadcasted_iota(jnp.int32, (1, 1, 8, 128), 2)
        lane = lax.broadcasted_iota(jnp.int32, (1, 1, 8, 128), 3)
        shape = (group, layers, 8, 128)
        for block in range(sp_count):
            part = pl.ds(group * block, group)
            center = conc[part]
            edges = spread_edges(sides_in[block][:, :tiles], place).reshape(shape)
            upper = jnp.broadcast_to(ends_in[0, part][:, :, None, :], shape)
            under = jnp.broadcast_to(ends_in[1, part][:, :, None, :], shape)
            beside_conc[0, part] = jnp.where(row == 7, under, shifted(center, 1, 2))
            beside_conc[1, part] = jnp.where(row == 0, upper, shifted(center, -1, 2))
            beside_conc[2, part] = jnp.where(lane == 127, edges, shifted(center, 1, 3))
            beside_conc[3, part] = jnp.where(lane == 0, edges, shifted(center, -1, 3))

    powers = [source]
    for k in range(BLOCK):
        powers.append(apply_flow(powers[-1], storage, faces))
    pairs = [(powers[k // 2], powers[(k + 1) // 2]) for k in range(2 * BLOCK + 1)]
    moments = global_sums(pairs, near_0, far_0, 0, fill_gram, None)
    change, residual, direction = cg_block(moments, moments, moments, least, most, True)
    head = combine(change, [powers])
    residual = combine(residual, [powers])
    direction = combine(direction, [powers])

    p_powers = [direction]
    for k in range(BLOCK):
        p_powers.append(apply_flow(p_powers[-1], storage, faces))
    r_powers = [residual]
    for k in range(BLOCK - 1):
        r_powers.append(apply_flow(r_powers[-1], storage, faces))
    pairs = [(r_powers[k // 2], r_powers[(k + 1) // 2]) for k in range(4)]
    pairs += [(p_powers[(k + 1) // 2], r_powers[k // 2]) for k in range(5)]
    pairs += [(p_powers[k // 2], p_powers[(k + 1) // 2]) for k in range(6)]
    moments = global_sums(pairs, near_1, far_1, 2, place_species, None)
    change, _, _ = cg_block(moments[:4], moments[4:9], moments[9:], least, most, False)
    head = head + combine(change, [p_powers, r_powers])

    def own(values):
        return values[:, 8:16, :128]

    head_out[...] = own(head)
    kept = jnp.ones_like(own(head))
    for number, (face, head_beside) in enumerate(zip(faces, six_beside(head))):
        face = own(face)
        velocity = face * (own(head) - own(head_beside))
        kept = kept - time_step * (jnp.maximum(velocity, 0.0) + dispersion * face)
        weights[number] = time_step * (dispersion * face - jnp.minimum(velocity, 0.0))
    for number in range(species_count):
        center = conc[number]
        total = kept * center
        total = total + weights[0] * layer_above(center)
        total = total + weights[1] * layer_below(center)
        for side in range(4):
            total = total + weights[2 + side] * beside_conc[side, number]
        moved[number] = total

    loads[5].wait()
    chunk = 2

    def react_chunk(step, carry):
        span = pl.ds(step * chunk, chunk)
        gram = [
            [gram_table[max(i, j), min(i, j)] for j in range(mineral_count)]
            for i in range(mineral_count)
        ]
        result = react(
            [moved[c, span] for c in range(species_count)],
            mineral_zone[span],
            rate_table,
            stoich,
            log_equil,
            gram,
        )
        for c in range(species_count):
            reacted[c, span] = result[c]
        for k in range(1, sp_count):
            to = (s + k) % sp_count
            remote(
                reacted.at[pl.ds(group * to, group), span],
                species_out.at[:, span, :, columns_of(s)],
                result_sem.at[0],
                result_sem.at[1],
                (g, to),
            )
        pltpu.make_async_copy(
            reacted.at[mine, span], species_out.at[:, span, :, columns_of(s)], result_sem.at[2]
        ).start()
        return carry

    lax.fori_loop(0, layers // chunk, react_chunk, 0)

    for copy in halo:
        copy.wait_send()
    for copy in sends:
        copy.wait()
    three = conc.at[pl.ds(0, group * (sp_count - 1))]
    pltpu.make_async_copy(three, three, spread_send.at[0]).wait()
    part = sides_in.at[pl.ds(0, sp_count - 1)]
    pltpu.make_async_copy(part, part, spread_send.at[1]).wait()
    pltpu.make_async_copy(ends_in, ends_in, spread_send.at[2]).wait()
    pltpu.make_async_copy(three, three, result_sem.at[0]).wait()
    pltpu.make_async_copy(three, three, result_sem.at[1]).wait()
    once = reacted.at[pl.ds(0, group)]
    pltpu.make_async_copy(once, once, result_sem.at[2]).wait()


def per_device(mesh, *arrays):
    gx_count, sp_count = mesh.shape["gx"], mesh.shape["sp"]
    inner = min(8, gx_count // 2)
    far_count = gx_count // inner * sp_count
    species = arrays[5]
    group, layers, _, width = species.shape
    total = group * sp_count
    minerals = arrays[8].shape[1]
    vmem = pl.BlockSpec(memory_space=pltpu.VMEM)
    smem = pl.BlockSpec(memory_space=pltpu.SMEM)
    hbm = pl.BlockSpec(memory_space=pltpu.HBM)
    cells = (layers, 8, 128)

    def floats(*shape):
        return pltpu.VMEM(shape, jnp.float32)

    return tuple(
        pl.pallas_call(
            functools.partial(step_kernel, gx_count, sp_count, inner),
            out_shape=(
                jax.ShapeDtypeStruct(cells, jnp.float32),
                jax.ShapeDtypeStruct(species.shape, jnp.float32),
            ),
            in_specs=[hbm, hbm, hbm, smem, smem, hbm, hbm, smem, smem, smem],
            out_specs=(vmem, hbm),
            scratch_shapes=[
                floats(*cells),
                floats(*cells),
                pltpu.VMEM(cells, jnp.int32),
                pltpu.VMEM(cells, jnp.int32),
                floats(*species.shape),
                floats(2, *cells),
                floats(2, 2, *cells),
                floats(16, 128),
                floats(3, 16, 128),
                floats(inner, 8, 128),
                floats(far_count, 8, 128),
                floats(inner, 16, 128),
                floats(far_count, 16, 128),
                floats(total, *cells),
                floats(2, group, layers, width),
                floats(2, total, layers, 128),
                floats(2 * sp_count, 256),
                floats(sp_count, 2 * sp_count, 256),
                floats(4, total, *cells),
                floats(6, *cells),
                floats(total, *cells),
                floats(total, *cells),
                pltpu.SMEM((minerals, minerals), jnp.float32),
                pltpu.SemaphoreType.DMA((6,)),
                pltpu.SemaphoreType.DMA((8,)),
                pltpu.SemaphoreType.DMA((8,)),
                pltpu.SemaphoreType.DMA((4,)),
                pltpu.SemaphoreType.DMA((4,)),
                pltpu.SemaphoreType.DMA((3,)),
                pltpu.SemaphoreType.DMA((3,)),
                pltpu.SemaphoreType.DMA((3,)),
            ],
            compiler_params=pltpu.CompilerParams(
                collective_id=0, has_side_effects=True, vmem_limit_bytes=48 * 1024 * 1024
            ),
        )(*arrays)
    )


def solution(mesh):
    cells = P(None, "gx", "sp")
    groups = P("sp", None, "gx", None)
    return jax.shard_map(
        functools.partial(per_device, mesh),
        mesh=mesh,
        in_specs=(cells, cells, cells, P(), P(), groups, cells, P(), P(), P()),
        out_specs=(cells, groups),
        check_vma=False,
    )
```

```python
import functools

import jax
import jax.numpy as jnp
from jax import lax
from jax.experimental import pallas as pl
from jax.experimental.pallas import tpu as pltpu
from jax.sharding import PartitionSpec as P

NEWTON = 2
BLOCK = 3

time_step = 0.05
dispersion = 0.5
reaction_span = 0.5
newton_damping = 0.5

MESH = pl.DeviceIdType.MESH
EXACT = lax.Precision.HIGHEST


def table_lookup(labels, table):
    size = table.shape[0] if hasattr(table, "shape") else len(table)
    found = jnp.full(labels.shape, table[0], jnp.float32)
    for level in range(1, size):
        found = jnp.where(labels == level, table[level], found)
    return found


def harmonic_safe(center, other):
    return 2.0 * center * other / jnp.maximum(center + other, 1e-30)


def shifted(field, offset, axis):
    size = field.shape[axis]
    return pltpu.roll(field, (-offset) % size, axis)


def layer_above(field):
    return jnp.concatenate([field[1:], field[-1:]], axis=0)


def layer_below(field):
    return jnp.concatenate([field[:1], field[:-1]], axis=0)


def six_faces(conduct):
    east = harmonic_safe(conduct, shifted(conduct, 1, 2))
    south = harmonic_safe(conduct, shifted(conduct, 1, 1))
    top = harmonic_safe(conduct[:-1], conduct[1:])
    none = jnp.zeros_like(conduct[:1])
    return (
        jnp.concatenate([top, none], axis=0),
        jnp.concatenate([none, top], axis=0),
        south,
        shifted(south, -1, 1),
        east,
        shifted(east, -1, 2),
    )


def six_beside(field):
    return (
        layer_above(field),
        layer_below(field),
        shifted(field, 1, 1),
        shifted(field, -1, 1),
        shifted(field, 1, 2),
        shifted(field, -1, 2),
    )


def apply_flow(field, storage, faces):
    result = storage * field
    for face, beside in zip(faces, six_beside(field)):
        result = result + face * (field - beside)
    return result


def add_scaled(left, scale, right):
    total = dict(left)
    for key, value in right.items():
        term = scale * value
        total[key] = total[key] + term if key in total else term
    return total


def cg_block(rr, pr, pp, least, most, same):
    one = jnp.ones_like(least)
    direction = {(0, 0): one}
    residual = {(0 if same else 1, 0): one}
    change = {}
    live = None
    for step in range(BLOCK):
        alpha = (pr if step == 0 else rr)[0] / jnp.maximum(pp[1], 1e-30)
        alpha = jnp.clip(alpha, least, most)
        if live is not None:
            alpha = jnp.where(live, alpha, 0.0)
        change = add_scaled(change, alpha, direction)
        image = {(part, power + 1): value for (part, power), value in direction.items()}
        residual = add_scaled(residual, -alpha, image)
        if len(pp) < 3 or len(pr) < 2:
            break
        square = alpha * alpha
        count = min(len(rr), len(pr) - 1, len(pp) - 2)
        next_rr = [rr[k] - 2.0 * alpha * pr[k + 1] + square * pp[k + 2] for k in range(count)]
        count = min(len(pr), len(pp) - 1)
        next_pr = [pr[k] - alpha * pp[k + 1] for k in range(count)]
        above = next_rr[0] > 1e-6 * (rr[0] + square * pp[2])
        live = above if live is None else live & above
        beta = jnp.where(live, next_rr[0] / jnp.maximum(rr[0], 1e-37), 0.0)
        direction = add_scaled(residual, beta, direction)
        count = min(len(next_rr), len(next_pr))
        next_pp = [
            next_rr[k] + 2.0 * beta * next_pr[k] + beta * beta * pp[k] for k in range(count)
        ]
        pr = [next_rr[k] + beta * next_pr[k] for k in range(count)]
        rr, pp = next_rr, next_pp
    return change, residual, direction


def combine(polynomial, parts):
    total = None
    for (part, power), value in sorted(polynomial.items()):
        term = value[None] * parts[part][power]
        total = term if total is None else total + term
    return total


def column_edges(pick, block):
    return lax.dot_general(
        pick,
        block,
        (((1,), (1,)), ((), ())),
        precision=EXACT,
        preferred_element_type=jnp.float32,
    )


def spread_edges(edges, pick):
    return lax.dot_general(
        edges,
        pick,
        (((0,), (0,)), ((), ())),
        precision=EXACT,
        preferred_element_type=jnp.float32,
    )


def weighted(scales, fields):
    total = None
    for scale, field in zip(scales, fields):
        term = scale * field
        total = term if total is None else total + term
    return total


def mineral_correction(gram, slope, start):
    count = len(start)
    right = [weighted([gram[i][k] for k in range(count)], start) for i in range(count)]
    schur = {(i, j): gram[i][j] for i in range(count) for j in range(i + 1)}
    pivot, lower = [None] * count, {}
    for k in range(count):
        pivot[k] = slope[k] / (1.0 + slope[k] * schur[k, k])
        for i in range(k + 1, count):
            lower[i, k] = schur[i, k] * pivot[k]
        for i in range(k + 1, count):
            right[i] = right[i] - lower[i, k] * right[k]
            for j in range(k + 1, i + 1):
                schur[i, j] = schur[i, j] - lower[i, k] * schur[j, k]
    answer = [None] * count
    for k in reversed(range(count)):
        value = pivot[k] * right[k]
        for i in range(k + 1, count):
            value = value - lower[i, k] * answer[i]
        answer[k] = value
    return answer


def react(moved, labels, rate_table, stoich, log_equil, gram):
    zones, minerals = rate_table.shape
    species = len(moved)
    rates = [table_lookup(labels, [rate_table[z, m] for z in range(zones)]) for m in range(minerals)]
    base = [
        weighted([stoich[m, c] for c in range(species)], moved) - log_equil[m]
        for m in range(minerals)
    ]
    extent = None
    for newton_pass in range(NEWTON):
        affinity = base
        if extent is not None:
            affinity = [base[m] + weighted(gram[m], extent) for m in range(minerals)]
        tangent = [jnp.tanh(value) for value in affinity]
        start = [reaction_span * rates[m] * tangent[m] for m in range(minerals)]
        if extent is not None:
            start = [extent[m] + start[m] for m in range(minerals)]
        slope = [
            reaction_span * rates[m] * jnp.maximum(1.0 - tangent[m] * tangent[m], 0.0)
            for m in range(minerals)
        ]
        correction = mineral_correction(gram, slope, start)
        step = [newton_damping * (start[m] - correction[m]) for m in range(minerals)]
        extent = [-step[m] if extent is None else extent[m] - step[m] for m in range(minerals)]
    return [
        moved[c] + weighted([stoich[m, c] for m in range(minerals)], extent)
        for c in range(species)
    ]


def step_kernel(
    gx_count,
    sp_count,
    inner,
    previous_head_in,
    recharge_in,
    soil_zone_in,
    soil_cond_in,
    soil_store_in,
    species_in,
    mineral_zone_in,
    rate_table_in,
    stoich_in,
    log_equil_in,
    head_out,
    species_out,
    soil_cond,
    soil_store,
    rate_table,
    stoich,
    log_equil,
    previous_head,
    recharge,
    soil_zone,
    mineral_zone,
    species,
    field,
    rows_in,
    edge_out,
    edge_in,
    near_0,
    far_0,
    near_1,
    far_1,
    conc,
    ends_out,
    ends_in,
    sides_out,
    sides_in,
    beside_conc,
    weights,
    moved,
    reacted,
    gram_table,
    load_sem,
    halo_send,
    halo_recv,
    sum_send,
    sum_recv,
    spread_send,
    spread_recv,
    result_sem,
):
    g = lax.axis_index("gx")
    s = lax.axis_index("sp")
    outer = gx_count // inner
    low, high = g % inner, g // inner
    plane = high * sp_count + s
    near_peers = [(high * inner + (low + k) % inner, s) for k in range(1, inner)]
    far_peers = [
        (((high + k // sp_count) % outer) * inner + low, (s + k % sp_count) % sp_count)
        for k in range(1, outer * sp_count)
    ]
    group = species_in.shape[0]
    layers = species_in.shape[1]

    def columns_of(device):
        return pl.ds(pl.multiple_of(device * 128, 128), 128)

    def beside(rows, columns):
        return ((g + rows + gx_count) % gx_count, (s + columns) % sp_count)

    def remote(source, target, send, recv, peer):
        copy = pltpu.make_async_remote_copy(
            src_ref=source,
            dst_ref=target,
            send_sem=send,
            recv_sem=recv,
            device_id=peer,
            device_id_type=MESH,
        )
        copy.start()
        return copy

    loads = [
        pltpu.make_async_copy(source, target, load_sem.at[number])
        for number, (source, target) in enumerate(
            (
                (soil_zone_in, soil_zone),
                (previous_head_in, previous_head),
                (recharge_in, recharge),
                (species_in, species),
                (species_in.at[:, :, :, columns_of(s)], conc.at[pl.ds(group * s, group)]),
                (mineral_zone_in, mineral_zone),
                (soil_store_in, soil_store),
                (soil_cond_in, soil_cond),
                (rate_table_in, rate_table),
                (stoich_in, stoich),
                (log_equil_in, log_equil),
            )
        )
    ]
    for copy in loads:
        copy.start()

    offsets = [(rows, columns) for rows in (-1, 0, 1) for columns in (-1, 0, 1) if (rows, columns) != (0, 0)]
    others = [k for k in range(2, sp_count - 1)]
    barrier = pltpu.get_barrier_semaphore()
    peers = [beside(*offset) for offset in offsets] + near_peers + far_peers
    peers += [beside(rows, k) for rows in (-1, 1) for k in others]
    for peer in peers:
        pl.semaphore_signal(barrier, inc=1, device_id=peer, device_id_type=MESH)

    for copy in loads[:3] + loads[6:7]:
        copy.wait()
    zone = soil_zone[...]
    field[0] = table_lookup(zone, soil_store) * previous_head[...] + recharge[...]
    field[1] = zone.astype(jnp.float32)
    line = lax.broadcasted_iota(jnp.int32, (16, 128), 0)
    lane = lax.broadcasted_iota(jnp.int32, (16, 128), 1)
    pick = (lane == jnp.where(line < 8, line, line + 112)).astype(jnp.float32)
    edge_out[...] = column_edges(pick, field[...].reshape(128, 128))

    pl.semaphore_wait(barrier, len(peers))
    halo = []
    for number, (rows, columns) in enumerate(offsets):
        if columns == 0:
            source, target = field, rows_in.at[0 if rows == 1 else 1]
        else:
            first = 8 if columns == 1 else 0
            source = edge_out.at[pl.ds(first, 8)]
            target = edge_in.at[1 - rows, pl.ds(first, 8)]
        halo.append(
            remote(source, target, halo_send.at[number], halo_recv.at[number], beside(rows, columns))
        )

    mine = pl.ds(group * s, group)
    loads[3].wait()
    for k in range(1, sp_count):
        to = (s + k) % sp_count
        remote(
            species.at[:, :, :, columns_of(to)],
            conc.at[mine],
            spread_send.at[0],
            spread_recv.at[0],
            (g, to),
        )
    width = species.shape[3]
    line = lax.broadcasted_iota(jnp.int32, (2 * sp_count, width), 0)
    lane = lax.broadcasted_iota(jnp.int32, (2 * sp_count, width), 1)
    wanted = jnp.where(line % 2 == 0, (line // 2) * 128 - 1, (line // 2) * 128 + 128)
    tiles = group * layers * 8
    sides_out[:, :tiles] = column_edges(
        (lane == wanted).astype(jnp.float32), species[...].reshape(tiles, width)
    )
    for layer in range(layers):
        ends_out[0, :, layer : layer + 1, :] = species[:, layer, 0:1, :]
        ends_out[1, :, layer : layer + 1, :] = species[:, layer, 7:8, :]
    sides_in[s] = sides_out[...]
    for k in range(1, sp_count):
        to = (s + k) % sp_count
        remote(sides_out, sides_in.at[s], spread_send.at[1], spread_recv.at[1], (g, to))
    for k in range(sp_count):
        to = (s + k) % sp_count
        for rows in (-1, 1):
            remote(
                ends_out.at[0 if rows == -1 else 1, :, :, columns_of(to)],
                ends_in.at[1 if rows == -1 else 0, mine],
                spread_send.at[2],
                spread_recv.at[2],
                beside(rows, k),
            )

    for copy in loads[7:]:
        copy.wait()
    for copy in halo:
        copy.wait_recv()

    row_blocks = []
    for block, center in enumerate((rows_in[0], field[...], rows_in[1])):
        side = spread_edges(edge_in[block], pick).reshape(2, 8, 8, 128)
        row_blocks.append(jnp.concatenate([center, side], axis=3))
    wide = jnp.concatenate(row_blocks, axis=2)
    row = lax.broadcasted_iota(jnp.int32, (24, 256), 0)
    column = lax.broadcasted_iota(jnp.int32, (24, 256), 1)
    first_row = jnp.where(g > 0, 0, 8)
    end_row = jnp.where(g < gx_count - 1, 24, 16)
    end_right = jnp.where(s < sp_count - 1, 136, 128)
    first_left = jnp.where(s > 0, 248, 256)
    inside = (
        (row >= first_row)
        & (row < end_row)
        & ((column < end_right) | (column >= first_left))
    )[None]
    source = jnp.where(inside, wide[0], 0.0)
    conduct = jnp.where(inside, table_lookup(wide[1], soil_cond), 0.0)
    storage = jnp.where(inside, table_lookup(wide[1], soil_store), 0.0)
    faces = six_faces(conduct)

    store_least, store_most, cond_most = soil_store[0], soil_store[0], soil_cond[0]
    for level in range(1, soil_store.shape[0]):
        store_least = jnp.minimum(store_least, soil_store[level])
        store_most = jnp.maximum(store_most, soil_store[level])
        cond_most = jnp.maximum(cond_most, soil_cond[level])
    most = 1.0 / jnp.full((1, 256), store_least, jnp.float32)
    least = 1.0 / jnp.full((1, 256), store_most + 12.0 * cond_most, jnp.float32)

    sends = []

    def exchange(buffer, slot, value, to_peers, number, meanwhile):
        buffer[slot] = value
        for peer in to_peers:
            remote(buffer.at[slot], buffer.at[slot], sum_send.at[number], sum_recv.at[number], peer)
        if meanwhile is not None:
            meanwhile()
        all_others = buffer.at[pl.ds(0, len(to_peers))]
        pltpu.make_async_copy(all_others, all_others, sum_recv.at[number]).wait()
        sends.append(pltpu.make_async_copy(all_others, all_others, sum_send.at[number]))
        return jnp.sum(buffer[...], axis=0)

    def global_sums(pairs, near, far, number, first_work, second_work):
        lines = near.shape[1]
        index = lax.broadcasted_iota(jnp.int32, (lines, 128), 0)
        partial = jnp.zeros((lines, 128), jnp.float32)
        for position, (left, right) in enumerate(pairs):
            product = left[:, 8:16, :128] * right[:, 8:16, :128]
            total = jnp.sum(jnp.sum(product, axis=0), axis=0, keepdims=True)
            partial = jnp.where(index == position, total, partial)
        partial = exchange(near, low, partial, near_peers, number, first_work)
        partial = exchange(far, plane, partial, far_peers, number + 1, second_work)
        totals = jnp.broadcast_to(jnp.sum(partial, axis=1, keepdims=True), (lines, 256))
        return [totals[k : k + 1] for k in range(len(pairs))]

    mineral_count, species_count = stoich.shape

    def fill_gram():
        columns = [
            [stoich[m, c] for c in range(species_count)] for m in range(mineral_count)
        ]
        for i in range(mineral_count):
            for j in range(i + 1):
                terms = [a * b for a, b in zip(columns[i], columns[j])]
                while len(terms) > 1:
                    terms = [sum(terms[k : k + 2][1:], terms[k]) for k in range(0, len(terms), 2)]
                gram_table[i, j] = terms[0]

    def place_species():
        whole = conc.at[pl.ds(0, group * (sp_count - 1))]
        pltpu.make_async_copy(whole, whole, spread_recv.at[0]).wait()
        part = sides_in.at[pl.ds(0, sp_count - 1)]
        pltpu.make_async_copy(part, part, spread_recv.at[1]).wait()
        pltpu.make_async_copy(ends_in, ends_in, spread_recv.at[2]).wait()
        loads[4].wait()
        line = lax.broadcasted_iota(jnp.int32, (2 * sp_count, 128), 0)
        lane = lax.broadcasted_iota(jnp.int32, (2 * sp_count, 128), 1)
        place = (((line == 2 * s) & (lane == 0)) | ((line == 2 * s + 1) & (lane == 127))).astype(
            jnp.float32
        )
        row = lax.broadcasted_iota(jnp.int32, (1, 1, 8, 128), 2)
        lane = lax.broadcasted_iota(jnp.int32, (1, 1, 8, 128), 3)
        shape = (group, layers, 8, 128)
        for block in range(sp_count):
            part = pl.ds(group * block, group)
            center = conc[part]
            edges = spread_edges(sides_in[block][:, :tiles], place).reshape(shape)
            upper = jnp.broadcast_to(ends_in[0, part][:, :, None, :], shape)
            under = jnp.broadcast_to(ends_in[1, part][:, :, None, :], shape)
            beside_conc[0, part] = jnp.where(row == 7, under, shifted(center, 1, 2))
            beside_conc[1, part] = jnp.where(row == 0, upper, shifted(center, -1, 2))
            beside_conc[2, part] = jnp.where(lane == 127, edges, shifted(center, 1, 3))
            beside_conc[3, part] = jnp.where(lane == 0, edges, shifted(center, -1, 3))

    powers = [source]
    for k in range(BLOCK):
        powers.append(apply_flow(powers[-1], storage, faces))
    pairs = [(powers[k // 2], powers[(k + 1) // 2]) for k in range(2 * BLOCK + 1)]
    moments = global_sums(pairs, near_0, far_0, 0, fill_gram, None)
    change, residual, direction = cg_block(moments, moments, moments, least, most, True)
    head = combine(change, [powers])
    residual = combine(residual, [powers])
    direction = combine(direction, [powers])

    p_powers = [direction]
    for k in range(BLOCK):
        p_powers.append(apply_flow(p_powers[-1], storage, faces))
    r_powers = [residual]
    for k in range(BLOCK - 1):
        r_powers.append(apply_flow(r_powers[-1], storage, faces))
    pairs = [(r_powers[k // 2], r_powers[(k + 1) // 2]) for k in range(4)]
    pairs += [(p_powers[(k + 1) // 2], r_powers[k // 2]) for k in range(5)]
    pairs += [(p_powers[k // 2], p_powers[(k + 1) // 2]) for k in range(6)]
    moments = global_sums(pairs, near_1, far_1, 2, place_species, None)
    change, _, _ = cg_block(moments[:4], moments[4:9], moments[9:], least, most, False)
    head = head + combine(change, [p_powers, r_powers])

    def own(values):
        return values[:, 8:16, :128]

    head_out[...] = own(head)
    kept = jnp.ones_like(own(head))
    for number, (face, head_beside) in enumerate(zip(faces, six_beside(head))):
        face = own(face)
        velocity = face * (own(head) - own(head_beside))
        kept = kept - time_step * (jnp.maximum(velocity, 0.0) + dispersion * face)
        weights[number] = time_step * (dispersion * face - jnp.minimum(velocity, 0.0))
    for number in range(species_count):
        center = conc[number]
        total = kept * center
        total = total + weights[0] * layer_above(center)
        total = total + weights[1] * layer_below(center)
        for side in range(4):
            total = total + weights[2 + side] * beside_conc[side, number]
        moved[number] = total

    loads[5].wait()
    chunk = 2

    def react_chunk(step, carry):
        span = pl.ds(step * chunk, chunk)
        gram = [
            [gram_table[max(i, j), min(i, j)] for j in range(mineral_count)]
            for i in range(mineral_count)
        ]
        result = react(
            [moved[c, span] for c in range(species_count)],
            mineral_zone[span],
            rate_table,
            stoich,
            log_equil,
            gram,
        )
        for c in range(species_count):
            reacted[c, span] = result[c]
        for k in range(1, sp_count):
            to = (s + k) % sp_count
            remote(
                reacted.at[pl.ds(group * to, group), span],
                species_out.at[:, span, :, columns_of(s)],
                result_sem.at[0],
                result_sem.at[1],
                (g, to),
            )
        pltpu.make_async_copy(
            reacted.at[mine, span], species_out.at[:, span, :, columns_of(s)], result_sem.at[2]
        ).start()
        return carry

    lax.fori_loop(0, layers // chunk, react_chunk, 0)

    for copy in halo:
        copy.wait_send()
    for copy in sends:
        copy.wait()
    three = conc.at[pl.ds(0, group * (sp_count - 1))]
    pltpu.make_async_copy(three, three, spread_send.at[0]).wait()
    part = sides_in.at[pl.ds(0, sp_count - 1)]
    pltpu.make_async_copy(part, part, spread_send.at[1]).wait()
    pltpu.make_async_copy(ends_in, ends_in, spread_send.at[2]).wait()
    pltpu.make_async_copy(three, three, result_sem.at[0]).wait()
    pltpu.make_async_copy(three, three, result_sem.at[1]).wait()
    once = reacted.at[pl.ds(0, group)]
    pltpu.make_async_copy(once, once, result_sem.at[2]).wait()


def per_device(mesh, *arrays):
    gx_count, sp_count = mesh.shape["gx"], mesh.shape["sp"]
    inner = min(8, gx_count // 2)
    far_count = gx_count // inner * sp_count
    species = arrays[5]
    group, layers, _, width = species.shape
    total = group * sp_count
    minerals = arrays[8].shape[1]
    arrays = arrays[:8] + (arrays[8].T,) + arrays[9:]
    tables = arrays[3:5] + arrays[7:]
    vmem = pl.BlockSpec(memory_space=pltpu.VMEM)
    hbm = pl.BlockSpec(memory_space=pltpu.HBM)
    cells = (layers, 8, 128)

    def floats(*shape):
        return pltpu.VMEM(shape, jnp.float32)

    return tuple(
        pl.pallas_call(
            functools.partial(step_kernel, gx_count, sp_count, inner),
            out_shape=(
                jax.ShapeDtypeStruct(cells, jnp.float32),
                jax.ShapeDtypeStruct(species.shape, jnp.float32),
            ),
            in_specs=[hbm] * 10,
            out_specs=(vmem, hbm),
            scratch_shapes=[
                *[pltpu.SMEM(table.shape, jnp.float32) for table in tables],
                floats(*cells),
                floats(*cells),
                pltpu.VMEM(cells, jnp.int32),
                pltpu.VMEM(cells, jnp.int32),
                floats(*species.shape),
                floats(2, *cells),
                floats(2, 2, *cells),
                floats(16, 128),
                floats(3, 16, 128),
                floats(inner, 8, 128),
                floats(far_count, 8, 128),
                floats(inner, 16, 128),
                floats(far_count, 16, 128),
                floats(total, *cells),
                floats(2, group, layers, width),
                floats(2, total, layers, 128),
                floats(2 * sp_count, 256),
                floats(sp_count, 2 * sp_count, 256),
                floats(4, total, *cells),
                floats(6, *cells),
                floats(total, *cells),
                floats(total, *cells),
                pltpu.SMEM((minerals, minerals), jnp.float32),
                pltpu.SemaphoreType.DMA((11,)),
                pltpu.SemaphoreType.DMA((8,)),
                pltpu.SemaphoreType.DMA((8,)),
                pltpu.SemaphoreType.DMA((4,)),
                pltpu.SemaphoreType.DMA((4,)),
                pltpu.SemaphoreType.DMA((3,)),
                pltpu.SemaphoreType.DMA((3,)),
                pltpu.SemaphoreType.DMA((3,)),
            ],
            compiler_params=pltpu.CompilerParams(
                collective_id=0, has_side_effects=True, vmem_limit_bytes=60 * 1024 * 1024
            ),
        )(*arrays)
    )


def solution(mesh):
    cells = P(None, "gx", "sp")
    groups = P("sp", None, "gx", None)
    return jax.shard_map(
        functools.partial(per_device, mesh),
        mesh=mesh,
        in_specs=(cells, cells, cells, P(), P(), groups, cells, P(), P(), P()),
        out_specs=(cells, groups),
        check_vma=False,
    )
```

```python
import functools

import jax
import jax.numpy as jnp
from jax import lax
from jax.experimental import pallas as pl
from jax.experimental.pallas import tpu as pltpu
from jax.sharding import PartitionSpec as P

NEWTON = 2
BLOCK = 3

time_step = 0.05
dispersion = 0.5
reaction_span = 0.5
newton_damping = 0.5

MESH = pl.DeviceIdType.MESH
EXACT = lax.Precision.HIGHEST


def table_lookup(labels, table):
    size = table.shape[0] if hasattr(table, "shape") else len(table)
    found = jnp.full(labels.shape, table[0], jnp.float32)
    for level in range(1, size):
        found = jnp.where(labels == level, table[level], found)
    return found


def harmonic_safe(center, other):
    return 2.0 * center * other / jnp.maximum(center + other, 1e-30)


def shifted(field, offset, axis):
    size = field.shape[axis]
    return pltpu.roll(field, (-offset) % size, axis)


def layer_above(field):
    return jnp.concatenate([field[1:], field[-1:]], axis=0)


def layer_below(field):
    return jnp.concatenate([field[:1], field[:-1]], axis=0)


def six_faces(conduct):
    east = harmonic_safe(conduct, shifted(conduct, 1, 2))
    south = harmonic_safe(conduct, shifted(conduct, 1, 1))
    top = harmonic_safe(conduct[:-1], conduct[1:])
    none = jnp.zeros_like(conduct[:1])
    return (
        jnp.concatenate([top, none], axis=0),
        jnp.concatenate([none, top], axis=0),
        south,
        shifted(south, -1, 1),
        east,
        shifted(east, -1, 2),
    )


def six_beside(field):
    return (
        layer_above(field),
        layer_below(field),
        shifted(field, 1, 1),
        shifted(field, -1, 1),
        shifted(field, 1, 2),
        shifted(field, -1, 2),
    )


def apply_flow(field, storage, faces):
    result = storage * field
    for face, beside in zip(faces, six_beside(field)):
        result = result + face * (field - beside)
    return result


def add_scaled(left, scale, right):
    total = dict(left)
    for key, value in right.items():
        term = scale * value
        total[key] = total[key] + term if key in total else term
    return total


def cg_block(rr, pr, pp, least, most, same):
    one = jnp.ones_like(least)
    direction = {(0, 0): one}
    residual = {(0 if same else 1, 0): one}
    change = {}
    live = None
    for step in range(BLOCK):
        alpha = (pr if step == 0 else rr)[0] / jnp.maximum(pp[1], 1e-30)
        alpha = jnp.clip(alpha, least, most)
        if live is not None:
            alpha = jnp.where(live, alpha, 0.0)
        change = add_scaled(change, alpha, direction)
        image = {(part, power + 1): value for (part, power), value in direction.items()}
        residual = add_scaled(residual, -alpha, image)
        if len(pp) < 3 or len(pr) < 2:
            break
        square = alpha * alpha
        count = min(len(rr), len(pr) - 1, len(pp) - 2)
        next_rr = [rr[k] - 2.0 * alpha * pr[k + 1] + square * pp[k + 2] for k in range(count)]
        count = min(len(pr), len(pp) - 1)
        next_pr = [pr[k] - alpha * pp[k + 1] for k in range(count)]
        above = next_rr[0] > 1e-6 * (rr[0] + square * pp[2])
        live = above if live is None else live & above
        beta = jnp.where(live, next_rr[0] / jnp.maximum(rr[0], 1e-37), 0.0)
        direction = add_scaled(residual, beta, direction)
        count = min(len(next_rr), len(next_pr))
        next_pp = [
            next_rr[k] + 2.0 * beta * next_pr[k] + beta * beta * pp[k] for k in range(count)
        ]
        pr = [next_rr[k] + beta * next_pr[k] for k in range(count)]
        rr, pp = next_rr, next_pp
    return change, residual, direction


def combine(polynomial, parts):
    total = None
    for (part, power), value in sorted(polynomial.items()):
        term = value[None] * parts[part][power]
        total = term if total is None else total + term
    return total


def column_edges(pick, block):
    return lax.dot_general(
        pick,
        block,
        (((1,), (1,)), ((), ())),
        precision=EXACT,
        preferred_element_type=jnp.float32,
    )


def spread_edges(edges, pick):
    return lax.dot_general(
        edges,
        pick,
        (((0,), (0,)), ((), ())),
        precision=EXACT,
        preferred_element_type=jnp.float32,
    )


def weighted(scales, fields):
    total = None
    for scale, field in zip(scales, fields):
        term = scale * field
        total = term if total is None else total + term
    return total


def mineral_correction(gram, slope, start):
    count = len(start)
    right = [weighted([gram[i][k] for k in range(count)], start) for i in range(count)]
    schur = {(i, j): gram[i][j] for i in range(count) for j in range(i + 1)}
    pivot, lower = [None] * count, {}
    for k in range(count):
        pivot[k] = slope[k] / (1.0 + slope[k] * schur[k, k])
        for i in range(k + 1, count):
            lower[i, k] = schur[i, k] * pivot[k]
        for i in range(k + 1, count):
            right[i] = right[i] - lower[i, k] * right[k]
            for j in range(k + 1, i + 1):
                schur[i, j] = schur[i, j] - lower[i, k] * schur[j, k]
    answer = [None] * count
    for k in reversed(range(count)):
        value = pivot[k] * right[k]
        for i in range(k + 1, count):
            value = value - lower[i, k] * answer[i]
        answer[k] = value
    return answer


def react(moved, labels, rate_table, stoich, log_equil, gram):
    zones, minerals = rate_table.shape
    species = len(moved)
    rates = [table_lookup(labels, [rate_table[z, m] for z in range(zones)]) for m in range(minerals)]
    base = [
        weighted([stoich[m, c] for c in range(species)], moved) - log_equil[m]
        for m in range(minerals)
    ]
    extent = None
    for newton_pass in range(NEWTON):
        affinity = base
        if extent is not None:
            affinity = [base[m] + weighted(gram[m], extent) for m in range(minerals)]
        tangent = [jnp.tanh(value) for value in affinity]
        start = [reaction_span * rates[m] * tangent[m] for m in range(minerals)]
        if extent is not None:
            start = [extent[m] + start[m] for m in range(minerals)]
        slope = [
            reaction_span * rates[m] * jnp.maximum(1.0 - tangent[m] * tangent[m], 0.0)
            for m in range(minerals)
        ]
        correction = mineral_correction(gram, slope, start)
        step = [newton_damping * (start[m] - correction[m]) for m in range(minerals)]
        extent = [-step[m] if extent is None else extent[m] - step[m] for m in range(minerals)]
    return [
        moved[c] + weighted([stoich[m, c] for m in range(minerals)], extent)
        for c in range(species)
    ]


def step_kernel(
    gx_count,
    sp_count,
    inner,
    previous_head_in,
    recharge_in,
    soil_zone_in,
    soil_cond_in,
    soil_store_in,
    species_in,
    mineral_zone_in,
    rate_table_in,
    stoich_in,
    log_equil_in,
    head_out,
    species_out,
    soil_cond,
    soil_store,
    rate_table,
    stoich,
    log_equil,
    previous_head,
    recharge,
    soil_zone,
    mineral_zone,
    species,
    field,
    rows_in,
    edge_out,
    edge_in,
    gathered_0,
    gathered_1,
    conc,
    ends_out,
    ends_in,
    sides_out,
    sides_in,
    beside_conc,
    weights,
    moved,
    reacted,
    gram_table,
    load_sem,
    halo_send,
    halo_recv,
    sum_send,
    sum_recv,
    spread_send,
    spread_recv,
    result_sem,
):
    g = lax.axis_index("gx")
    s = lax.axis_index("sp")
    cores, across = 2, inner // 2
    down = gx_count // inner
    core, x, y = lax.rem(g, cores), lax.rem(lax.div(g, cores), across), lax.div(g, inner)
    at_core = [lax.rem(core + k, cores) for k in range(cores)]
    at_x = [lax.rem(x + k, across) * cores for k in range(across)]
    at_y = [lax.rem(y + k, down) * inner for k in range(down)]
    at_z = [lax.rem(s + k, sp_count) for k in range(sp_count)]
    at_gx = [[[a + b + c for c in at_core] for b in at_x] for a in at_y]

    def hops(k, count):
        return min(k, count - k)

    steps = [
        (hops(i, down) + hops(j, across) + hops(m, sp_count), k, i, j, m)
        for i in range(down)
        for j in range(across)
        for k in range(cores)
        for m in range(sp_count)
    ][1:]
    everyone = [
        (at_gx[i][j][k], at_z[m]) for _, k, i, j, m in sorted(steps, reverse=True)
    ]
    slot = g * sp_count + s
    group = species_in.shape[0]
    layers = species_in.shape[1]

    def columns_of(device):
        return pl.ds(pl.multiple_of(device * 128, 128), 128)

    def beside(rows, columns):
        return ((g + rows + gx_count) % gx_count, (s + columns) % sp_count)

    def remote(source, target, send, recv, peer):
        copy = pltpu.make_async_remote_copy(
            src_ref=source,
            dst_ref=target,
            send_sem=send,
            recv_sem=recv,
            device_id=peer,
            device_id_type=MESH,
        )
        copy.start()
        return copy

    loads = [
        pltpu.make_async_copy(source, target, load_sem.at[number])
        for number, (source, target) in enumerate(
            (
                (soil_zone_in, soil_zone),
                (previous_head_in, previous_head),
                (recharge_in, recharge),
                (species_in, species),
                (species_in.at[:, :, :, columns_of(s)], conc.at[pl.ds(group * s, group)]),
                (mineral_zone_in, mineral_zone),
                (soil_store_in, soil_store),
                (soil_cond_in, soil_cond),
                (rate_table_in, rate_table),
                (stoich_in, stoich),
                (log_equil_in, log_equil),
            )
        )
    ]
    for copy in loads:
        copy.start()

    offsets = [(rows, columns) for rows in (-1, 0, 1) for columns in (-1, 0, 1) if (rows, columns) != (0, 0)]
    barrier = pltpu.get_barrier_semaphore()
    for peer in everyone:
        pl.semaphore_signal(barrier, inc=1, device_id=peer, device_id_type=MESH)

    for copy in loads[:3] + loads[6:7]:
        copy.wait()
    zone = soil_zone[...]
    field[0] = table_lookup(zone, soil_store) * previous_head[...] + recharge[...]
    field[1] = zone.astype(jnp.float32)
    line = lax.broadcasted_iota(jnp.int32, (16, 128), 0)
    lane = lax.broadcasted_iota(jnp.int32, (16, 128), 1)
    pick = (lane == jnp.where(line < 8, line, line + 112)).astype(jnp.float32)
    edge_out[...] = column_edges(pick, field[...].reshape(128, 128))

    pl.semaphore_wait(barrier, len(everyone))
    halo = []
    for number, (rows, columns) in enumerate(offsets):
        if columns == 0:
            source, target = field, rows_in.at[0 if rows == 1 else 1]
        else:
            first = 8 if columns == 1 else 0
            source = edge_out.at[pl.ds(first, 8)]
            target = edge_in.at[1 - rows, pl.ds(first, 8)]
        halo.append(
            remote(source, target, halo_send.at[number], halo_recv.at[number], beside(rows, columns))
        )

    mine = pl.ds(group * s, group)
    loads[3].wait()
    for k in range(1, sp_count):
        to = (s + k) % sp_count
        remote(
            species.at[:, :, :, columns_of(to)],
            conc.at[mine],
            spread_send.at[0],
            spread_recv.at[0],
            (g, to),
        )
    width = species.shape[3]
    line = lax.broadcasted_iota(jnp.int32, (2 * sp_count, width), 0)
    lane = lax.broadcasted_iota(jnp.int32, (2 * sp_count, width), 1)
    wanted = jnp.where(line % 2 == 0, (line // 2) * 128 - 1, (line // 2) * 128 + 128)
    tiles = group * layers * 8
    sides_out[:, :tiles] = column_edges(
        (lane == wanted).astype(jnp.float32), species[...].reshape(tiles, width)
    )
    for layer in range(layers):
        ends_out[0, :, layer : layer + 1, :] = species[:, layer, 0:1, :]
        ends_out[1, :, layer : layer + 1, :] = species[:, layer, 7:8, :]
    sides_in[s] = sides_out[...]
    for k in range(1, sp_count):
        to = (s + k) % sp_count
        remote(sides_out, sides_in.at[s], spread_send.at[1], spread_recv.at[1], (g, to))
    for k in range(sp_count):
        to = (s + k) % sp_count
        for rows in (-1, 1):
            remote(
                ends_out.at[0 if rows == -1 else 1, :, :, columns_of(to)],
                ends_in.at[1 if rows == -1 else 0, mine],
                spread_send.at[2],
                spread_recv.at[2],
                beside(rows, k),
            )

    for copy in loads[7:]:
        copy.wait()
    for copy in halo:
        copy.wait_recv()

    row_blocks = []
    for block, center in enumerate((rows_in[0], field[...], rows_in[1])):
        side = spread_edges(edge_in[block], pick).reshape(2, 8, 8, 128)
        row_blocks.append(jnp.concatenate([center, side], axis=3))
    wide = jnp.concatenate(row_blocks, axis=2)
    row = lax.broadcasted_iota(jnp.int32, (24, 256), 0)
    column = lax.broadcasted_iota(jnp.int32, (24, 256), 1)
    first_row = jnp.where(g > 0, 0, 8)
    end_row = jnp.where(g < gx_count - 1, 24, 16)
    end_right = jnp.where(s < sp_count - 1, 136, 128)
    first_left = jnp.where(s > 0, 248, 256)
    inside = (
        (row >= first_row)
        & (row < end_row)
        & ((column < end_right) | (column >= first_left))
    )[None]
    source = jnp.where(inside, wide[0], 0.0)
    conduct = jnp.where(inside, table_lookup(wide[1], soil_cond), 0.0)
    storage = jnp.where(inside, table_lookup(wide[1], soil_store), 0.0)
    faces = six_faces(conduct)

    store_least, store_most, cond_most = soil_store[0], soil_store[0], soil_cond[0]
    for level in range(1, soil_store.shape[0]):
        store_least = jnp.minimum(store_least, soil_store[level])
        store_most = jnp.maximum(store_most, soil_store[level])
        cond_most = jnp.maximum(cond_most, soil_cond[level])
    most = 1.0 / jnp.full((1, 256), store_least, jnp.float32)
    least = 1.0 / jnp.full((1, 256), store_most + 12.0 * cond_most, jnp.float32)

    sends = []

    def global_sums(pairs, gathered, number, meanwhile):
        lines = -(-len(pairs) // 8) * 8
        row = lax.broadcasted_iota(jnp.int32, (lines, 128), 0)
        lane = lax.broadcasted_iota(jnp.int32, (lines, 128), 1)
        partial = jnp.zeros((lines, 128), jnp.float32)
        for position, (left, right) in enumerate(pairs):
            product = left[:, 8:16, :128] * right[:, 8:16, :128]
            total = jnp.sum(jnp.sum(product, axis=0), axis=0, keepdims=True)
            partial = jnp.where(row == position, total, partial)
        totals = jnp.sum(partial, axis=1, keepdims=True)
        gathered[slot] = jnp.sum(jnp.where(row == lane, totals, 0.0), axis=0, keepdims=True)
        for peer in everyone:
            remote(
                gathered.at[slot], gathered.at[slot], sum_send.at[number], sum_recv.at[number], peer
            )
        meanwhile()
        all_others = gathered.at[pl.ds(0, len(everyone))]
        pltpu.make_async_copy(all_others, all_others, sum_recv.at[number]).wait()
        sends.append(pltpu.make_async_copy(all_others, all_others, sum_send.at[number]))
        total = jnp.sum(gathered[...], axis=0)
        return [jnp.broadcast_to(total[:, k : k + 1], (1, 256)) for k in range(len(pairs))]

    mineral_count, species_count = stoich.shape

    def fill_gram():
        columns = [
            [stoich[m, c] for c in range(species_count)] for m in range(mineral_count)
        ]
        for i in range(mineral_count):
            for j in range(i + 1):
                terms = [a * b for a, b in zip(columns[i], columns[j])]
                while len(terms) > 1:
                    terms = [sum(terms[k : k + 2][1:], terms[k]) for k in range(0, len(terms), 2)]
                gram_table[i, j] = terms[0]

    def place_species():
        whole = conc.at[pl.ds(0, group * (sp_count - 1))]
        pltpu.make_async_copy(whole, whole, spread_recv.at[0]).wait()
        part = sides_in.at[pl.ds(0, sp_count - 1)]
        pltpu.make_async_copy(part, part, spread_recv.at[1]).wait()
        pltpu.make_async_copy(ends_in, ends_in, spread_recv.at[2]).wait()
        loads[4].wait()
        line = lax.broadcasted_iota(jnp.int32, (2 * sp_count, 128), 0)
        lane = lax.broadcasted_iota(jnp.int32, (2 * sp_count, 128), 1)
        place = (((line == 2 * s) & (lane == 0)) | ((line == 2 * s + 1) & (lane == 127))).astype(
            jnp.float32
        )
        row = lax.broadcasted_iota(jnp.int32, (1, 1, 8, 128), 2)
        lane = lax.broadcasted_iota(jnp.int32, (1, 1, 8, 128), 3)
        shape = (group, layers, 8, 128)
        for block in range(sp_count):
            part = pl.ds(group * block, group)
            center = conc[part]
            edges = spread_edges(sides_in[block][:, :tiles], place).reshape(shape)
            upper = jnp.broadcast_to(ends_in[0, part][:, :, None, :], shape)
            under = jnp.broadcast_to(ends_in[1, part][:, :, None, :], shape)
            beside_conc[0, part] = jnp.where(row == 7, under, shifted(center, 1, 2))
            beside_conc[1, part] = jnp.where(row == 0, upper, shifted(center, -1, 2))
            beside_conc[2, part] = jnp.where(lane == 127, edges, shifted(center, 1, 3))
            beside_conc[3, part] = jnp.where(lane == 0, edges, shifted(center, -1, 3))

    powers = [source]
    for k in range(BLOCK):
        powers.append(apply_flow(powers[-1], storage, faces))
    pairs = [(powers[k // 2], powers[(k + 1) // 2]) for k in range(2 * BLOCK + 1)]
    moments = global_sums(pairs, gathered_0, 0, fill_gram)
    change, residual, direction = cg_block(moments, moments, moments, least, most, True)
    head = combine(change, [powers])
    residual = combine(residual, [powers])
    direction = combine(direction, [powers])

    p_powers = [direction]
    for k in range(BLOCK):
        p_powers.append(apply_flow(p_powers[-1], storage, faces))
    r_powers = [residual]
    for k in range(BLOCK - 1):
        r_powers.append(apply_flow(r_powers[-1], storage, faces))
    pairs = [(r_powers[k // 2], r_powers[(k + 1) // 2]) for k in range(4)]
    pairs += [(p_powers[(k + 1) // 2], r_powers[k // 2]) for k in range(5)]
    pairs += [(p_powers[k // 2], p_powers[(k + 1) // 2]) for k in range(6)]
    moments = global_sums(pairs, gathered_1, 1, place_species)
    change, _, _ = cg_block(moments[:4], moments[4:9], moments[9:], least, most, False)
    head = head + combine(change, [p_powers, r_powers])

    def own(values):
        return values[:, 8:16, :128]

    head_out[...] = own(head)
    kept = jnp.ones_like(own(head))
    for number, (face, head_beside) in enumerate(zip(faces, six_beside(head))):
        face = own(face)
        velocity = face * (own(head) - own(head_beside))
        kept = kept - time_step * (jnp.maximum(velocity, 0.0) + dispersion * face)
        weights[number] = time_step * (dispersion * face - jnp.minimum(velocity, 0.0))
    for number in range(species_count):
        center = conc[number]
        total = kept * center
        total = total + weights[0] * layer_above(center)
        total = total + weights[1] * layer_below(center)
        for side in range(4):
            total = total + weights[2 + side] * beside_conc[side, number]
        moved[number] = total

    loads[5].wait()
    chunk = 2

    def react_chunk(step, carry):
        span = pl.ds(step * chunk, chunk)
        gram = [
            [gram_table[max(i, j), min(i, j)] for j in range(mineral_count)]
            for i in range(mineral_count)
        ]
        result = react(
            [moved[c, span] for c in range(species_count)],
            mineral_zone[span],
            rate_table,
            stoich,
            log_equil,
            gram,
        )
        for c in range(species_count):
            reacted[c, span] = result[c]
        for k in range(1, sp_count):
            to = (s + k) % sp_count
            remote(
                reacted.at[pl.ds(group * to, group), span],
                species_out.at[:, span, :, columns_of(s)],
                result_sem.at[0],
                result_sem.at[1],
                (g, to),
            )
        pltpu.make_async_copy(
            reacted.at[mine, span], species_out.at[:, span, :, columns_of(s)], result_sem.at[2]
        ).start()
        return carry

    lax.fori_loop(0, layers // chunk, react_chunk, 0)

    for copy in halo:
        copy.wait_send()
    for copy in sends:
        copy.wait()
    three = conc.at[pl.ds(0, group * (sp_count - 1))]
    pltpu.make_async_copy(three, three, spread_send.at[0]).wait()
    part = sides_in.at[pl.ds(0, sp_count - 1)]
    pltpu.make_async_copy(part, part, spread_send.at[1]).wait()
    pltpu.make_async_copy(ends_in, ends_in, spread_send.at[2]).wait()
    pltpu.make_async_copy(three, three, result_sem.at[0]).wait()
    pltpu.make_async_copy(three, three, result_sem.at[1]).wait()
    once = reacted.at[pl.ds(0, group)]
    pltpu.make_async_copy(once, once, result_sem.at[2]).wait()


def per_device(mesh, *arrays):
    gx_count, sp_count = mesh.shape["gx"], mesh.shape["sp"]
    inner = min(8, gx_count // 2)
    species = arrays[5]
    group, layers, _, width = species.shape
    total = group * sp_count
    minerals = arrays[8].shape[1]
    arrays = arrays[:8] + (arrays[8].T,) + arrays[9:]
    tables = arrays[3:5] + arrays[7:]
    vmem = pl.BlockSpec(memory_space=pltpu.VMEM)
    hbm = pl.BlockSpec(memory_space=pltpu.HBM)
    cells = (layers, 8, 128)

    def floats(*shape):
        return pltpu.VMEM(shape, jnp.float32)

    return tuple(
        pl.pallas_call(
            functools.partial(step_kernel, gx_count, sp_count, inner),
            out_shape=(
                jax.ShapeDtypeStruct(cells, jnp.float32),
                jax.ShapeDtypeStruct(species.shape, jnp.float32),
            ),
            in_specs=[hbm] * 10,
            out_specs=(vmem, hbm),
            scratch_shapes=[
                *[pltpu.SMEM(table.shape, jnp.float32) for table in tables],
                floats(*cells),
                floats(*cells),
                pltpu.VMEM(cells, jnp.int32),
                pltpu.VMEM(cells, jnp.int32),
                floats(*species.shape),
                floats(2, *cells),
                floats(2, 2, *cells),
                floats(16, 128),
                floats(3, 16, 128),
                floats(gx_count * sp_count, 1, 128),
                floats(gx_count * sp_count, 1, 128),
                floats(total, *cells),
                floats(2, group, layers, width),
                floats(2, total, layers, 128),
                floats(2 * sp_count, 256),
                floats(sp_count, 2 * sp_count, 256),
                floats(4, total, *cells),
                floats(6, *cells),
                floats(total, *cells),
                floats(total, *cells),
                pltpu.SMEM((minerals, minerals), jnp.float32),
                pltpu.SemaphoreType.DMA((11,)),
                pltpu.SemaphoreType.DMA((8,)),
                pltpu.SemaphoreType.DMA((8,)),
                pltpu.SemaphoreType.DMA((2,)),
                pltpu.SemaphoreType.DMA((2,)),
                pltpu.SemaphoreType.DMA((3,)),
                pltpu.SemaphoreType.DMA((3,)),
                pltpu.SemaphoreType.DMA((3,)),
            ],
            compiler_params=pltpu.CompilerParams(
                collective_id=0, has_side_effects=True, vmem_limit_bytes=60 * 1024 * 1024
            ),
        )(*arrays)
    )


def solution(mesh):
    cells = P(None, "gx", "sp")
    groups = P("sp", None, "gx", None)
    return jax.shard_map(
        functools.partial(per_device, mesh),
        mesh=mesh,
        in_specs=(cells, cells, cells, P(), P(), groups, cells, P(), P(), P()),
        out_specs=(cells, groups),
        check_vma=False,
    )
```

```python
import functools

import jax
import jax.numpy as jnp
from jax import lax
from jax.experimental import pallas as pl
from jax.experimental.pallas import tpu as pltpu
from jax.sharding import PartitionSpec as P

NEWTON = 2
BLOCK = 3

time_step = 0.05
dispersion = 0.5
reaction_span = 0.5
newton_damping = 0.5

MESH = pl.DeviceIdType.MESH
EXACT = lax.Precision.HIGHEST


def table_lookup(labels, table):
    size = table.shape[0] if hasattr(table, "shape") else len(table)
    found = jnp.full(labels.shape, table[0], jnp.float32)
    for level in range(1, size):
        found = jnp.where(labels == level, table[level], found)
    return found


def harmonic_safe(center, other):
    return 2.0 * center * other / jnp.maximum(center + other, 1e-30)


def shifted(field, offset, axis):
    size = field.shape[axis]
    return pltpu.roll(field, (-offset) % size, axis)


def layer_above(field):
    return jnp.concatenate([field[1:], field[-1:]], axis=0)


def layer_below(field):
    return jnp.concatenate([field[:1], field[:-1]], axis=0)


def six_faces(conduct):
    east = harmonic_safe(conduct, shifted(conduct, 1, 2))
    south = harmonic_safe(conduct, shifted(conduct, 1, 1))
    top = harmonic_safe(conduct[:-1], conduct[1:])
    none = jnp.zeros_like(conduct[:1])
    return (
        jnp.concatenate([top, none], axis=0),
        jnp.concatenate([none, top], axis=0),
        south,
        shifted(south, -1, 1),
        east,
        shifted(east, -1, 2),
    )


def six_beside(field):
    return (
        layer_above(field),
        layer_below(field),
        shifted(field, 1, 1),
        shifted(field, -1, 1),
        shifted(field, 1, 2),
        shifted(field, -1, 2),
    )


def apply_flow(field, storage, faces):
    result = storage * field
    for face, beside in zip(faces, six_beside(field)):
        result = result + face * (field - beside)
    return result


def add_scaled(left, scale, right):
    total = dict(left)
    for key, value in right.items():
        term = scale * value
        total[key] = total[key] + term if key in total else term
    return total


def cg_block(rr, pr, pp, least, most, same):
    one = jnp.ones_like(least)
    direction = {(0, 0): one}
    residual = {(0 if same else 1, 0): one}
    change = {}
    live = None
    for step in range(BLOCK):
        alpha = (pr if step == 0 else rr)[0] / jnp.maximum(pp[1], 1e-30)
        alpha = jnp.clip(alpha, least, most)
        if live is not None:
            alpha = jnp.where(live, alpha, 0.0)
        change = add_scaled(change, alpha, direction)
        image = {(part, power + 1): value for (part, power), value in direction.items()}
        residual = add_scaled(residual, -alpha, image)
        if len(pp) < 3 or len(pr) < 2:
            break
        square = alpha * alpha
        count = min(len(rr), len(pr) - 1, len(pp) - 2)
        next_rr = [rr[k] - 2.0 * alpha * pr[k + 1] + square * pp[k + 2] for k in range(count)]
        count = min(len(pr), len(pp) - 1)
        next_pr = [pr[k] - alpha * pp[k + 1] for k in range(count)]
        above = next_rr[0] > 1e-6 * (rr[0] + square * pp[2])
        live = above if live is None else live & above
        beta = jnp.where(live, next_rr[0] / jnp.maximum(rr[0], 1e-37), 0.0)
        direction = add_scaled(residual, beta, direction)
        count = min(len(next_rr), len(next_pr))
        next_pp = [
            next_rr[k] + 2.0 * beta * next_pr[k] + beta * beta * pp[k] for k in range(count)
        ]
        pr = [next_rr[k] + beta * next_pr[k] for k in range(count)]
        rr, pp = next_rr, next_pp
    return change, residual, direction


def combine(polynomial, parts):
    total = None
    for (part, power), value in sorted(polynomial.items()):
        term = value[None] * parts[part][power]
        total = term if total is None else total + term
    return total


def column_edges(pick, block):
    return lax.dot_general(
        pick,
        block,
        (((1,), (1,)), ((), ())),
        precision=EXACT,
        preferred_element_type=jnp.float32,
    )


def spread_edges(edges, pick):
    return lax.dot_general(
        edges,
        pick,
        (((0,), (0,)), ((), ())),
        precision=EXACT,
        preferred_element_type=jnp.float32,
    )


def weighted(scales, fields):
    total = None
    for scale, field in zip(scales, fields):
        term = scale * field
        total = term if total is None else total + term
    return total


def mineral_correction(gram, slope, start):
    count = len(start)
    right = [weighted([gram[i][k] for k in range(count)], start) for i in range(count)]
    schur = {(i, j): gram[i][j] for i in range(count) for j in range(i + 1)}
    pivot, lower = [None] * count, {}
    for k in range(count):
        pivot[k] = slope[k] / (1.0 + slope[k] * schur[k, k])
        for i in range(k + 1, count):
            lower[i, k] = schur[i, k] * pivot[k]
        for i in range(k + 1, count):
            right[i] = right[i] - lower[i, k] * right[k]
            for j in range(k + 1, i + 1):
                schur[i, j] = schur[i, j] - lower[i, k] * schur[j, k]
    answer = [None] * count
    for k in reversed(range(count)):
        value = pivot[k] * right[k]
        for i in range(k + 1, count):
            value = value - lower[i, k] * answer[i]
        answer[k] = value
    return answer


def react(moved, labels, rate_table, stoich, log_equil, gram):
    zones, minerals = rate_table.shape
    species = len(moved)
    rates = [table_lookup(labels, [rate_table[z, m] for z in range(zones)]) for m in range(minerals)]
    base = [
        weighted([stoich[m, c] for c in range(species)], moved) - log_equil[m]
        for m in range(minerals)
    ]
    extent = None
    for newton_pass in range(NEWTON):
        affinity = base
        if extent is not None:
            affinity = [base[m] + weighted(gram[m], extent) for m in range(minerals)]
        tangent = [jnp.tanh(value) for value in affinity]
        start = [reaction_span * rates[m] * tangent[m] for m in range(minerals)]
        if extent is not None:
            start = [extent[m] + start[m] for m in range(minerals)]
        slope = [
            reaction_span * rates[m] * jnp.maximum(1.0 - tangent[m] * tangent[m], 0.0)
            for m in range(minerals)
        ]
        correction = mineral_correction(gram, slope, start)
        step = [newton_damping * (start[m] - correction[m]) for m in range(minerals)]
        extent = [-step[m] if extent is None else extent[m] - step[m] for m in range(minerals)]
    return [
        moved[c] + weighted([stoich[m, c] for m in range(minerals)], extent)
        for c in range(species)
    ]


def step_kernel(
    gx_count,
    sp_count,
    inner,
    previous_head_in,
    recharge_in,
    soil_zone_in,
    soil_cond_in,
    soil_store_in,
    species_in,
    mineral_zone_in,
    rate_table_in,
    stoich_in,
    log_equil_in,
    head_out,
    species_out,
    soil_cond,
    soil_store,
    rate_table,
    stoich,
    log_equil,
    previous_head,
    recharge,
    soil_zone,
    mineral_zone,
    species,
    field,
    rows_in,
    edge_out,
    edge_in,
    gathered_0,
    gathered_1,
    conc,
    ends_out,
    ends_in,
    sides_out,
    sides_in,
    beside_conc,
    weights,
    moved,
    reacted,
    gram_table,
    load_sem,
    halo_send,
    halo_recv,
    sum_send,
    sum_recv,
    spread_send,
    spread_recv,
    result_sem,
):
    g = lax.axis_index("gx")
    s = lax.axis_index("sp")
    cores, across = 2, inner // 2
    down = gx_count // inner
    core, x, y = lax.rem(g, cores), lax.rem(lax.div(g, cores), across), lax.div(g, inner)
    at_core = [lax.rem(core + k, cores) for k in range(cores)]
    at_x = [lax.rem(x + k, across) * cores for k in range(across)]
    at_y = [lax.rem(y + k, down) * inner for k in range(down)]
    at_z = [lax.rem(s + k, sp_count) for k in range(sp_count)]
    at_gx = [[[a + b + c for c in at_core] for b in at_x] for a in at_y]

    def hops(k, count):
        return min(k, count - k)

    steps = [
        (hops(i, down) + hops(j, across) + hops(m, sp_count), k, i, j, m)
        for i in range(down)
        for j in range(across)
        for k in range(cores)
        for m in range(sp_count)
    ][1:]
    everyone = [
        (at_gx[i][j][k], at_z[m]) for _, k, i, j, m in sorted(steps, reverse=True)
    ]
    slot = g * sp_count + s
    group = species_in.shape[0]
    layers = species_in.shape[1]

    def columns_of(device):
        return pl.ds(pl.multiple_of(device * 128, 128), 128)

    def beside(rows, columns):
        return ((g + rows + gx_count) % gx_count, (s + columns) % sp_count)

    def remote(source, target, send, recv, peer):
        copy = pltpu.make_async_remote_copy(
            src_ref=source,
            dst_ref=target,
            send_sem=send,
            recv_sem=recv,
            device_id=peer,
            device_id_type=MESH,
        )
        copy.start()
        return copy

    loads = [
        pltpu.make_async_copy(source, target, load_sem.at[number])
        for number, (source, target) in enumerate(
            (
                (soil_zone_in, soil_zone),
                (previous_head_in, previous_head),
                (recharge_in, recharge),
                (species_in, species),
                (species_in.at[:, :, :, columns_of(s)], conc.at[pl.ds(group * s, group)]),
                (mineral_zone_in, mineral_zone),
                (soil_store_in, soil_store),
                (soil_cond_in, soil_cond),
                (rate_table_in, rate_table),
                (stoich_in, stoich),
                (log_equil_in, log_equil),
            )
        )
    ]
    for copy in loads:
        copy.start()

    offsets = [(rows, columns) for rows in (-1, 0, 1) for columns in (-1, 0, 1) if (rows, columns) != (0, 0)]
    barrier = pltpu.get_barrier_semaphore()
    for peer in everyone:
        pl.semaphore_signal(barrier, inc=1, device_id=peer, device_id_type=MESH)

    for copy in loads[:3] + loads[6:7]:
        copy.wait()
    zone = soil_zone[...]
    field[0] = table_lookup(zone, soil_store) * previous_head[...] + recharge[...]
    field[1] = zone.astype(jnp.float32)
    line = lax.broadcasted_iota(jnp.int32, (16, 128), 0)
    lane = lax.broadcasted_iota(jnp.int32, (16, 128), 1)
    pick = (lane == jnp.where(line < 8, line, line + 112)).astype(jnp.float32)
    edge_out[...] = column_edges(pick, field[...].reshape(128, 128))

    pl.semaphore_wait(barrier, len(everyone))
    halo = []
    for number, (rows, columns) in enumerate(offsets):
        if columns == 0:
            source, target = field, rows_in.at[0 if rows == 1 else 1]
        else:
            first = 8 if columns == 1 else 0
            source = edge_out.at[pl.ds(first, 8)]
            target = edge_in.at[1 - rows, pl.ds(first, 8)]
        halo.append(
            remote(source, target, halo_send.at[number], halo_recv.at[number], beside(rows, columns))
        )

    mine = pl.ds(group * s, group)
    loads[3].wait()
    for k in range(1, sp_count):
        to = (s + k) % sp_count
        remote(
            species.at[:, :, :, columns_of(to)],
            conc.at[mine],
            spread_send.at[0],
            spread_recv.at[0],
            (g, to),
        )
    width = species.shape[3]
    line = lax.broadcasted_iota(jnp.int32, (2 * sp_count, width), 0)
    lane = lax.broadcasted_iota(jnp.int32, (2 * sp_count, width), 1)
    wanted = jnp.where(line % 2 == 0, (line // 2) * 128 - 1, (line // 2) * 128 + 128)
    tiles = group * layers * 8
    sides_out[:, :tiles] = column_edges(
        (lane == wanted).astype(jnp.float32), species[...].reshape(tiles, width)
    )
    for layer in range(layers):
        ends_out[0, :, layer : layer + 1, :] = species[:, layer, 0:1, :]
        ends_out[1, :, layer : layer + 1, :] = species[:, layer, 7:8, :]
    sides_in[s] = sides_out[...]
    for k in range(1, sp_count):
        to = (s + k) % sp_count
        remote(sides_out, sides_in.at[s], spread_send.at[1], spread_recv.at[1], (g, to))
    for k in range(sp_count):
        to = (s + k) % sp_count
        for rows in (-1, 1):
            remote(
                ends_out.at[0 if rows == -1 else 1, :, :, columns_of(to)],
                ends_in.at[1 if rows == -1 else 0, mine],
                spread_send.at[2],
                spread_recv.at[2],
                beside(rows, k),
            )

    for copy in loads[7:]:
        copy.wait()
    for copy in halo:
        copy.wait_recv()

    row_blocks = []
    for block, center in enumerate((rows_in[0], field[...], rows_in[1])):
        side = spread_edges(edge_in[block], pick).reshape(2, 8, 8, 128)
        row_blocks.append(jnp.concatenate([center, side], axis=3))
    wide = jnp.concatenate(row_blocks, axis=2)
    row = lax.broadcasted_iota(jnp.int32, (24, 256), 0)
    column = lax.broadcasted_iota(jnp.int32, (24, 256), 1)
    first_row = jnp.where(g > 0, 0, 8)
    end_row = jnp.where(g < gx_count - 1, 24, 16)
    end_right = jnp.where(s < sp_count - 1, 136, 128)
    first_left = jnp.where(s > 0, 248, 256)
    inside = (
        (row >= first_row)
        & (row < end_row)
        & ((column < end_right) | (column >= first_left))
    )[None]
    source = jnp.where(inside, wide[0], 0.0)
    conduct = jnp.where(inside, table_lookup(wide[1], soil_cond), 0.0)
    storage = jnp.where(inside, table_lookup(wide[1], soil_store), 0.0)
    faces = six_faces(conduct)

    store_least, store_most, cond_most = soil_store[0], soil_store[0], soil_cond[0]
    for level in range(1, soil_store.shape[0]):
        store_least = jnp.minimum(store_least, soil_store[level])
        store_most = jnp.maximum(store_most, soil_store[level])
        cond_most = jnp.maximum(cond_most, soil_cond[level])
    most = 1.0 / jnp.full((1, 256), store_least, jnp.float32)
    least = 1.0 / jnp.full((1, 256), store_most + 12.0 * cond_most, jnp.float32)

    sends = []

    def global_sums(pairs, gathered, number, meanwhile):
        lines = -(-len(pairs) // 8) * 8
        row = lax.broadcasted_iota(jnp.int32, (lines, 128), 0)
        lane = lax.broadcasted_iota(jnp.int32, (lines, 128), 1)
        partial = jnp.zeros((lines, 128), jnp.float32)
        for position, (left, right) in enumerate(pairs):
            product = left[:, 8:16, :128] * right[:, 8:16, :128]
            total = jnp.sum(jnp.sum(product, axis=0), axis=0, keepdims=True)
            partial = jnp.where(row == position, total, partial)
        totals = jnp.sum(partial, axis=1, keepdims=True)
        gathered[slot] = jnp.sum(jnp.where(row == lane, totals, 0.0), axis=0, keepdims=True)
        for peer in everyone:
            remote(
                gathered.at[slot], gathered.at[slot], sum_send.at[number], sum_recv.at[number], peer
            )
        meanwhile()
        all_others = gathered.at[pl.ds(0, len(everyone))]
        pltpu.make_async_copy(all_others, all_others, sum_recv.at[number]).wait()
        sends.append(pltpu.make_async_copy(all_others, all_others, sum_send.at[number]))
        total = gathered[...]
        while total.shape[0] > 1:
            half = total.shape[0] // 2
            total = total[:half] + total[half:]
        total = total[0]
        return [jnp.broadcast_to(total[:, k : k + 1], (1, 256)) for k in range(len(pairs))]

    mineral_count, species_count = stoich.shape

    def fill_gram():
        columns = [
            [stoich[m, c] for c in range(species_count)] for m in range(mineral_count)
        ]
        for i in range(mineral_count):
            for j in range(i + 1):
                terms = [a * b for a, b in zip(columns[i], columns[j])]
                while len(terms) > 1:
                    terms = [sum(terms[k : k + 2][1:], terms[k]) for k in range(0, len(terms), 2)]
                gram_table[i, j] = terms[0]

    def place_species():
        whole = conc.at[pl.ds(0, group * (sp_count - 1))]
        pltpu.make_async_copy(whole, whole, spread_recv.at[0]).wait()
        part = sides_in.at[pl.ds(0, sp_count - 1)]
        pltpu.make_async_copy(part, part, spread_recv.at[1]).wait()
        pltpu.make_async_copy(ends_in, ends_in, spread_recv.at[2]).wait()
        loads[4].wait()
        line = lax.broadcasted_iota(jnp.int32, (2 * sp_count, 128), 0)
        lane = lax.broadcasted_iota(jnp.int32, (2 * sp_count, 128), 1)
        place = (((line == 2 * s) & (lane == 0)) | ((line == 2 * s + 1) & (lane == 127))).astype(
            jnp.float32
        )
        row = lax.broadcasted_iota(jnp.int32, (1, 1, 8, 128), 2)
        lane = lax.broadcasted_iota(jnp.int32, (1, 1, 8, 128), 3)
        shape = (group, layers, 8, 128)
        for block in range(sp_count):
            part = pl.ds(group * block, group)
            center = conc[part]
            edges = spread_edges(sides_in[block][:, :tiles], place).reshape(shape)
            upper = jnp.broadcast_to(ends_in[0, part][:, :, None, :], shape)
            under = jnp.broadcast_to(ends_in[1, part][:, :, None, :], shape)
            beside_conc[0, part] = jnp.where(row == 7, under, shifted(center, 1, 2))
            beside_conc[1, part] = jnp.where(row == 0, upper, shifted(center, -1, 2))
            beside_conc[2, part] = jnp.where(lane == 127, edges, shifted(center, 1, 3))
            beside_conc[3, part] = jnp.where(lane == 0, edges, shifted(center, -1, 3))

    powers = [source]
    for k in range(BLOCK):
        powers.append(apply_flow(powers[-1], storage, faces))
    pairs = [(powers[k // 2], powers[(k + 1) // 2]) for k in range(2 * BLOCK + 1)]
    moments = global_sums(pairs, gathered_0, 0, fill_gram)
    change, residual, direction = cg_block(moments, moments, moments, least, most, True)
    head = combine(change, [powers])
    residual = combine(residual, [powers])
    direction = combine(direction, [powers])

    p_powers = [direction]
    for k in range(BLOCK):
        p_powers.append(apply_flow(p_powers[-1], storage, faces))
    r_powers = [residual]
    for k in range(BLOCK - 1):
        r_powers.append(apply_flow(r_powers[-1], storage, faces))
    pairs = [(r_powers[k // 2], r_powers[(k + 1) // 2]) for k in range(4)]
    pairs += [(p_powers[(k + 1) // 2], r_powers[k // 2]) for k in range(5)]
    pairs += [(p_powers[k // 2], p_powers[(k + 1) // 2]) for k in range(6)]
    moments = global_sums(pairs, gathered_1, 1, place_species)
    change, _, _ = cg_block(moments[:4], moments[4:9], moments[9:], least, most, False)
    head = head + combine(change, [p_powers, r_powers])

    def own(values):
        return values[:, 8:16, :128]

    head_out[...] = own(head)
    kept = jnp.ones_like(own(head))
    for number, (face, head_beside) in enumerate(zip(faces, six_beside(head))):
        face = own(face)
        velocity = face * (own(head) - own(head_beside))
        kept = kept - time_step * (jnp.maximum(velocity, 0.0) + dispersion * face)
        weights[number] = time_step * (dispersion * face - jnp.minimum(velocity, 0.0))
    for number in range(species_count):
        center = conc[number]
        total = kept * center
        total = total + weights[0] * layer_above(center)
        total = total + weights[1] * layer_below(center)
        for side in range(4):
            total = total + weights[2 + side] * beside_conc[side, number]
        moved[number] = total

    loads[5].wait()
    chunk = 2

    def react_chunk(step, carry):
        span = pl.ds(step * chunk, chunk)
        gram = [
            [gram_table[max(i, j), min(i, j)] for j in range(mineral_count)]
            for i in range(mineral_count)
        ]
        result = react(
            [moved[c, span] for c in range(species_count)],
            mineral_zone[span],
            rate_table,
            stoich,
            log_equil,
            gram,
        )
        for c in range(species_count):
            reacted[c, span] = result[c]
        for k in range(1, sp_count):
            to = (s + k) % sp_count
            remote(
                reacted.at[pl.ds(group * to, group), span],
                species_out.at[:, span, :, columns_of(s)],
                result_sem.at[0],
                result_sem.at[1],
                (g, to),
            )
        pltpu.make_async_copy(
            reacted.at[mine, span], species_out.at[:, span, :, columns_of(s)], result_sem.at[2]
        ).start()
        return carry

    lax.fori_loop(0, layers // chunk, react_chunk, 0)

    for copy in halo:
        copy.wait_send()
    for copy in sends:
        copy.wait()
    three = conc.at[pl.ds(0, group * (sp_count - 1))]
    pltpu.make_async_copy(three, three, spread_send.at[0]).wait()
    part = sides_in.at[pl.ds(0, sp_count - 1)]
    pltpu.make_async_copy(part, part, spread_send.at[1]).wait()
    pltpu.make_async_copy(ends_in, ends_in, spread_send.at[2]).wait()
    pltpu.make_async_copy(three, three, result_sem.at[0]).wait()
    pltpu.make_async_copy(three, three, result_sem.at[1]).wait()
    once = reacted.at[pl.ds(0, group)]
    pltpu.make_async_copy(once, once, result_sem.at[2]).wait()


def hand_over(head, species, head_out, species_out, head_held, species_held, load_sem, store_sem):
    parts = [(head, head_held, head_out)]
    for k in range(species.shape[0]):
        parts.append((species.at[k], species_held.at[k], species_out.at[k]))
    loads, stores = [], []
    for number, (source, held, target) in enumerate(parts):
        loads.append(pltpu.make_async_copy(source, held, load_sem.at[number]))
        stores.append(pltpu.make_async_copy(held, target, store_sem.at[number]))
    for copy in loads:
        copy.start()
    for load, store in zip(loads, stores):
        load.wait()
        store.start()
    for copy in stores:
        copy.wait()


def per_device(mesh, *arrays):
    gx_count, sp_count = mesh.shape["gx"], mesh.shape["sp"]
    inner = min(8, gx_count // 2)
    species = arrays[5]
    group, layers, _, width = species.shape
    total = group * sp_count
    minerals = arrays[8].shape[1]
    arrays = arrays[:8] + (arrays[8].T,) + arrays[9:]
    tables = arrays[3:5] + arrays[7:]
    vmem = pl.BlockSpec(memory_space=pltpu.VMEM)
    hbm = pl.BlockSpec(memory_space=pltpu.HBM)
    cells = (layers, 8, 128)

    def floats(*shape):
        return pltpu.VMEM(shape, jnp.float32)

    results = (
        pl.pallas_call(
            functools.partial(step_kernel, gx_count, sp_count, inner),
            out_shape=(
                jax.ShapeDtypeStruct(cells, jnp.float32),
                jax.ShapeDtypeStruct(species.shape, jnp.float32),
            ),
            in_specs=[hbm] * 10,
            out_specs=(vmem, hbm),
            scratch_shapes=[
                *[pltpu.SMEM(table.shape, jnp.float32) for table in tables],
                floats(*cells),
                floats(*cells),
                pltpu.VMEM(cells, jnp.int32),
                pltpu.VMEM(cells, jnp.int32),
                floats(*species.shape),
                floats(2, *cells),
                floats(2, 2, *cells),
                floats(16, 128),
                floats(3, 16, 128),
                floats(gx_count * sp_count, 1, 128),
                floats(gx_count * sp_count, 1, 128),
                floats(total, *cells),
                floats(2, group, layers, width),
                floats(2, total, layers, 128),
                floats(2 * sp_count, 256),
                floats(sp_count, 2 * sp_count, 256),
                floats(4, total, *cells),
                floats(6, *cells),
                floats(total, *cells),
                floats(total, *cells),
                pltpu.SMEM((minerals, minerals), jnp.float32),
                pltpu.SemaphoreType.DMA((11,)),
                pltpu.SemaphoreType.DMA((8,)),
                pltpu.SemaphoreType.DMA((8,)),
                pltpu.SemaphoreType.DMA((2,)),
                pltpu.SemaphoreType.DMA((2,)),
                pltpu.SemaphoreType.DMA((3,)),
                pltpu.SemaphoreType.DMA((3,)),
                pltpu.SemaphoreType.DMA((3,)),
            ],
            compiler_params=pltpu.CompilerParams(
                collective_id=0, has_side_effects=True, vmem_limit_bytes=60 * 1024 * 1024
            ),
        )(*arrays)
    )

    return tuple(
        pl.pallas_call(
            hand_over,
            out_shape=tuple(jax.ShapeDtypeStruct(r.shape, r.dtype) for r in results),
            in_specs=[hbm, hbm],
            out_specs=(hbm, hbm),
            scratch_shapes=[
                *[floats(*r.shape) for r in results],
                pltpu.SemaphoreType.DMA((1 + group,)),
                pltpu.SemaphoreType.DMA((1 + group,)),
            ],
            compiler_params=pltpu.CompilerParams(vmem_limit_bytes=60 * 1024 * 1024),
        )(*results)
    )


def solution(mesh):
    cells = P(None, "gx", "sp")
    groups = P("sp", None, "gx", None)
    return jax.shard_map(
        functools.partial(per_device, mesh),
        mesh=mesh,
        in_specs=(cells, cells, cells, P(), P(), groups, cells, P(), P(), P()),
        out_specs=(cells, groups),
        check_vma=False,
    )
```

```python
import functools

import jax
import jax.numpy as jnp
from jax import lax
from jax.experimental import pallas as pl
from jax.experimental.pallas import tpu as pltpu
from jax.sharding import PartitionSpec as P

NEWTON = 2
SHIFTS = (0.5, 0.125, 1.0, 0.25, 1.0, 0.0625)
CHUNK = 2
PIECE = 2

time_step = 0.05
dispersion = 0.5
reaction_span = 0.5
newton_damping = 0.5

MESH = pl.DeviceIdType.MESH
EXACT = lax.Precision.HIGHEST


def table_lookup(labels, table):
    size = table.shape[0] if hasattr(table, "shape") else len(table)
    found = jnp.full(labels.shape, table[0], jnp.float32)
    for level in range(1, size):
        found = jnp.where(labels == level, table[level], found)
    return found


def harmonic_safe(center, other):
    return 2.0 * center * other / jnp.maximum(center + other, 1e-30)


def shifted(field, offset, axis):
    size = field.shape[axis]
    return pltpu.roll(field, (-offset) % size, axis)


def layer_above(field):
    return jnp.concatenate([field[1:], field[-1:]], axis=0)


def layer_below(field):
    return jnp.concatenate([field[:1], field[:-1]], axis=0)


def six_faces(conduct):
    east = harmonic_safe(conduct, shifted(conduct, 1, 2))
    south = harmonic_safe(conduct, shifted(conduct, 1, 1))
    top = harmonic_safe(conduct[:-1], conduct[1:])
    none = jnp.zeros_like(conduct[:1])
    return (
        jnp.concatenate([top, none], axis=0),
        jnp.concatenate([none, top], axis=0),
        south,
        shifted(south, -1, 1),
        east,
        shifted(east, -1, 2),
    )


def six_beside(field):
    return (
        layer_above(field),
        layer_below(field),
        shifted(field, 1, 1),
        shifted(field, -1, 1),
        shifted(field, 1, 2),
        shifted(field, -1, 2),
    )


def apply_flow(field, storage, faces):
    result = storage * field
    for face, beside in zip(faces, six_beside(field)):
        result = result + face * (field - beside)
    return result


def exact_sum(left, right):
    total = left + right
    part = total - left
    return total, (left - (total - part)) + (right - part)


def split(value):
    wide = 4097.0 * value
    high = wide - (wide - value)
    return high, value - high


def paired(high, low):
    total = high + low
    return total, low - (total - high)


def pair_add(left, right):
    total, error = exact_sum(left[0], right[0])
    return paired(total, error + (left[1] + right[1]))


def pair_minus(left, right):
    return pair_add(left, (-right[0], -right[1]))


def pair_times(left, right):
    left_high, left_low = split(left[0])
    right_high, right_low = split(right[0])
    product = left[0] * right[0]
    error = left_high * right_high - product
    error = error + left_high * right_low + left_low * right_high + left_low * right_low
    return paired(product, error + (left[0] * right[1] + left[1] * right[0]))


def pair_inverse(value):
    guess = 1.0 / value[0]
    none = jnp.zeros_like(guess)
    rest = pair_minus((none + 1.0, none), pair_times(value, (guess, none)))
    return paired(guess, guess * (rest[0] + rest[1]))


def halved(total, error):
    half = total.shape[0] // 2
    total, more = exact_sum(total[:half], total[half:])
    return total, error[:half] + error[half:] + more


def inner_product(left, right):
    total = left[0] * right[0]
    error = left[0] * right[1] + left[1] * right[0] + left[1] * right[1]
    while total.shape[0] > 1:
        total, error = halved(total, error)
    return total[0], error[0]


def merge_rows(pairs):
    row = lax.broadcasted_iota(jnp.int32, (8, 128), 0)
    for shift in (4, 2, 1):
        keep = (row % (2 * shift)) < shift
        merged = []
        for left, right in zip(pairs[:shift], pairs[shift:]):
            ends = []
            for part in range(2):
                ends.append(
                    (
                        jnp.where(keep, left[part], pltpu.roll(right[part], shift, 0)),
                        jnp.where(keep, pltpu.roll(left[part], 8 - shift, 0), right[part]),
                    )
                )
            total, error = exact_sum(*ends[0])
            merged.append((total, error + (ends[1][0] + ends[1][1])))
        pairs = merged
    return pairs[0]


def solve_krylov(gram):
    size = len(SHIFTS)
    matrix = {}
    for i in range(size):
        for j in range(i, size):
            after = pair_add(gram[i, j + 1], gram[min(i + 1, j), max(i + 1, j)])
            for shift in (SHIFTS[i], SHIFTS[j]):
                after = pair_add(after, (shift * gram[i, j][0], shift * gram[i, j][1]))
            matrix[j, i] = after
    right = [gram[0, i] for i in range(size)]
    first = [gram[k, k][0] for k in range(size)]
    inverse, lower = [None] * size, {}
    for k in range(size):
        pivot = matrix[k, k]
        usable = pivot[0] > 8e-12 * first[k]
        inverse[k] = tuple(jnp.where(usable, part, 0.0) for part in pair_inverse(pivot))
        for i in range(k + 1, size):
            lower[i, k] = pair_times(matrix[i, k], inverse[k])
        for i in range(k + 1, size):
            right[i] = pair_minus(right[i], pair_times(lower[i, k], right[k]))
            for j in range(k + 1, i + 1):
                matrix[i, j] = pair_minus(
                    matrix[i, j], pair_times(lower[i, k], matrix[j, k])
                )
    answer = [None] * size
    for k in reversed(range(size)):
        value = pair_times(right[k], inverse[k])[0]
        for i in range(k + 1, size):
            value = value - lower[i, k][0] * answer[i]
        answer[k] = value
    return [2.0 * value for value in answer]


def column_edges(pick, block):
    return lax.dot_general(
        pick,
        block,
        (((1,), (1,)), ((), ())),
        precision=EXACT,
        preferred_element_type=jnp.float32,
    )


def spread_edges(edges, pick):
    return lax.dot_general(
        edges,
        pick,
        (((0,), (0,)), ((), ())),
        precision=EXACT,
        preferred_element_type=jnp.float32,
    )


def weighted(scales, fields):
    total = None
    for scale, field in zip(scales, fields):
        term = scale * field
        total = term if total is None else total + term
    return total


def mineral_correction(gram, slope, start):
    count = len(start)
    right = [weighted([gram[i][k] for k in range(count)], start) for i in range(count)]
    schur = {(i, j): gram[i][j] for i in range(count) for j in range(i + 1)}
    pivot, lower = [None] * count, {}
    for k in range(count):
        pivot[k] = slope[k] / (1.0 + slope[k] * schur[k, k])
        for i in range(k + 1, count):
            lower[i, k] = schur[i, k] * pivot[k]
        for i in range(k + 1, count):
            right[i] = right[i] - lower[i, k] * right[k]
            for j in range(k + 1, i + 1):
                schur[i, j] = schur[i, j] - lower[i, k] * schur[j, k]
    answer = [None] * count
    for k in reversed(range(count)):
        value = pivot[k] * right[k]
        for i in range(k + 1, count):
            value = value - lower[i, k] * answer[i]
        answer[k] = value
    return answer


def react(moved, labels, rate_table, stoich, log_equil, gram):
    zones, minerals = rate_table.shape
    species = len(moved)
    rates = [table_lookup(labels, [rate_table[z, m] for z in range(zones)]) for m in range(minerals)]
    base = [
        weighted([stoich[m, c] for c in range(species)], moved) - log_equil[m]
        for m in range(minerals)
    ]
    extent = None
    for newton_pass in range(NEWTON):
        affinity = base
        if extent is not None:
            affinity = [base[m] + weighted(gram[m], extent) for m in range(minerals)]
        tangent = [jnp.tanh(value) for value in affinity]
        start = [reaction_span * rates[m] * tangent[m] for m in range(minerals)]
        if extent is not None:
            start = [extent[m] + start[m] for m in range(minerals)]
        slope = [
            reaction_span * rates[m] * jnp.maximum(1.0 - tangent[m] * tangent[m], 0.0)
            for m in range(minerals)
        ]
        correction = mineral_correction(gram, slope, start)
        step = [newton_damping * (start[m] - correction[m]) for m in range(minerals)]
        extent = [-step[m] if extent is None else extent[m] - step[m] for m in range(minerals)]
    return [
        moved[c] + weighted([stoich[m, c] for m in range(minerals)], extent)
        for c in range(species)
    ]


def step_kernel(
    gx_count,
    sp_count,
    inner,
    previous_head_in,
    recharge_in,
    soil_zone_in,
    soil_cond_in,
    soil_store_in,
    species_in,
    mineral_zone_in,
    rate_table_in,
    stoich_in,
    log_equil_in,
    head_out,
    species_out,
    soil_cond,
    soil_store,
    rate_table,
    stoich,
    log_equil,
    previous_head,
    recharge,
    soil_zone,
    mineral_zone,
    species,
    field,
    rows_in,
    edge_out,
    edge_in,
    gathered,
    conc,
    ends_out,
    ends_in,
    sides_out,
    sides_in,
    beside_conc,
    weights,
    reacted,
    gram_table,
    load_sem,
    halo_send,
    halo_recv,
    sum_send,
    sum_recv,
    spread_send,
    spread_recv,
    result_sem,
):
    g = lax.axis_index("gx")
    s = lax.axis_index("sp")
    cores, across = 2, inner // 2
    down = gx_count // inner
    core, x, y = lax.rem(g, cores), lax.rem(lax.div(g, cores), across), lax.div(g, inner)
    at_core = [lax.rem(core + k, cores) for k in range(cores)]
    at_x = [lax.rem(x + k, across) * cores for k in range(across)]
    at_y = [lax.rem(y + k, down) * inner for k in range(down)]
    at_z = [lax.rem(s + k, sp_count) for k in range(sp_count)]
    at_gx = [[[a + b + c for c in at_core] for b in at_x] for a in at_y]

    def hops(k, count):
        return min(k, count - k)

    steps = [
        (hops(i, down) + hops(j, across) + hops(m, sp_count), k, i, j, m)
        for i in range(down)
        for j in range(across)
        for k in range(cores)
        for m in range(sp_count)
    ][1:]
    everyone = [
        (at_gx[i][j][k], at_z[m]) for _, k, i, j, m in sorted(steps, reverse=True)
    ]
    slot = g * sp_count + s
    group = species_in.shape[0]
    layers = species_in.shape[1]

    def columns_of(device):
        return pl.ds(pl.multiple_of(device * 128, 128), 128)

    def beside(rows, columns):
        return ((g + rows + gx_count) % gx_count, (s + columns) % sp_count)

    def remote(source, target, send, recv, peer):
        copy = pltpu.make_async_remote_copy(
            src_ref=source,
            dst_ref=target,
            send_sem=send,
            recv_sem=recv,
            device_id=peer,
            device_id_type=MESH,
        )
        copy.start()
        return copy

    middle = pl.ds(1, layers)
    loads = [
        pltpu.make_async_copy(source, target, load_sem.at[number])
        for number, (source, target) in enumerate(
            (
                (soil_zone_in, soil_zone),
                (previous_head_in, previous_head),
                (recharge_in, recharge),
                (species_in, species),
                (species_in.at[:, :, :, columns_of(s)], conc.at[pl.ds(group * s, group), middle]),
                (mineral_zone_in, mineral_zone),
                (soil_store_in, soil_store),
                (soil_cond_in, soil_cond),
                (rate_table_in, rate_table),
                (stoich_in, stoich),
                (log_equil_in, log_equil),
            )
        )
    ]
    for copy in loads:
        copy.start()

    offsets = [(rows, columns) for rows in (-1, 0, 1) for columns in (-1, 0, 1) if (rows, columns) != (0, 0)]
    barrier = pltpu.get_barrier_semaphore()
    for peer in everyone:
        pl.semaphore_signal(barrier, inc=1, device_id=peer, device_id_type=MESH)

    for copy in loads[:3] + loads[6:7]:
        copy.wait()
    for number in range(group * sp_count):
        conc[number, 0] = jnp.zeros((8, 128), jnp.float32)
        conc[number, layers + 1] = jnp.zeros((8, 128), jnp.float32)
    zone = soil_zone[...]
    field[0] = table_lookup(zone, soil_store) * previous_head[...] + recharge[...]
    field[1] = zone.astype(jnp.float32)
    line = lax.broadcasted_iota(jnp.int32, (16, 128), 0)
    lane = lax.broadcasted_iota(jnp.int32, (16, 128), 1)
    pick = (lane == jnp.where(line < 8, line, line + 112)).astype(jnp.float32)
    edge_out[...] = column_edges(pick, field[...].reshape(128, 128))

    pl.semaphore_wait(barrier, len(everyone))
    halo = []
    for number, (rows, columns) in enumerate(offsets):
        if columns == 0:
            source, target = field, rows_in.at[0 if rows == 1 else 1]
        else:
            first = 8 if columns == 1 else 0
            source = edge_out.at[pl.ds(first, 8)]
            target = edge_in.at[1 - rows, pl.ds(first, 8)]
        halo.append(
            remote(source, target, halo_send.at[number], halo_recv.at[number], beside(rows, columns))
        )

    mine = pl.ds(group * s, group)
    loads[3].wait()
    for k in range(1, sp_count):
        to = (s + k) % sp_count
        remote(
            species.at[:, :, :, columns_of(to)],
            conc.at[mine, middle],
            spread_send.at[0],
            spread_recv.at[0],
            (g, to),
        )
    width = species.shape[3]
    line = lax.broadcasted_iota(jnp.int32, (2 * sp_count, width), 0)
    lane = lax.broadcasted_iota(jnp.int32, (2 * sp_count, width), 1)
    wanted = jnp.where(line % 2 == 0, (line // 2) * 128 - 1, (line // 2) * 128 + 128)
    tiles = group * layers * 8
    sides_out[:, :tiles] = column_edges(
        (lane == wanted).astype(jnp.float32), species[...].reshape(tiles, width)
    )
    for layer in range(layers):
        ends_out[0, :, layer : layer + 1, :] = species[:, layer, 0:1, :]
        ends_out[1, :, layer : layer + 1, :] = species[:, layer, 7:8, :]
    sides_in[s] = sides_out[...]
    for k in range(1, sp_count):
        to = (s + k) % sp_count
        remote(sides_out, sides_in.at[s], spread_send.at[1], spread_recv.at[1], (g, to))
    for k in range(sp_count):
        to = (s + k) % sp_count
        for rows in (-1, 1):
            remote(
                ends_out.at[0 if rows == -1 else 1, :, :, columns_of(to)],
                ends_in.at[1 if rows == -1 else 0, mine],
                spread_send.at[2],
                spread_recv.at[2],
                beside(rows, k),
            )

    for copy in loads[7:]:
        copy.wait()
    for copy in halo:
        copy.wait_recv()

    row_blocks = []
    for block, center in enumerate((rows_in[0], field[...], rows_in[1])):
        side = spread_edges(edge_in[block], pick).reshape(2, 8, 8, 128)
        row_blocks.append(jnp.concatenate([center, side], axis=3))
    wide = jnp.concatenate(row_blocks, axis=2)
    row = lax.broadcasted_iota(jnp.int32, (24, 256), 0)
    column = lax.broadcasted_iota(jnp.int32, (24, 256), 1)
    first_row = jnp.where(g > 0, 0, 8)
    end_row = jnp.where(g < gx_count - 1, 24, 16)
    end_right = jnp.where(s < sp_count - 1, 136, 128)
    first_left = jnp.where(s > 0, 248, 256)
    inside = (
        (row >= first_row)
        & (row < end_row)
        & ((column < end_right) | (column >= first_left))
    )[None]
    source = jnp.where(inside, wide[0], 0.0)
    conduct = jnp.where(inside, table_lookup(wide[1], soil_cond), 0.0)
    storage = jnp.where(inside, table_lookup(wide[1], soil_store), 0.0)
    faces = six_faces(conduct)

    store_most, cond_most = soil_store[0], soil_cond[0]
    for level in range(1, soil_store.shape[0]):
        store_most = jnp.maximum(store_most, soil_store[level])
        cond_most = jnp.maximum(cond_most, soil_cond[level])
    scale = 2.0 / jnp.full((1, 256), store_most + 12.0 * cond_most, jnp.float32)

    mineral_count, species_count = stoich.shape

    def fill_gram():
        columns = [
            [stoich[m, c] for c in range(species_count)] for m in range(mineral_count)
        ]
        for i in range(mineral_count):
            for j in range(i + 1):
                terms = [a * b for a, b in zip(columns[i], columns[j])]
                while len(terms) > 1:
                    terms = [sum(terms[k : k + 2][1:], terms[k]) for k in range(0, len(terms), 2)]
                gram_table[i, j] = terms[0]

    def place_species():
        whole = conc.at[pl.ds(0, group * (sp_count - 1)), middle]
        pltpu.make_async_copy(whole, whole, spread_recv.at[0]).wait()
        part = sides_in.at[pl.ds(0, sp_count - 1)]
        pltpu.make_async_copy(part, part, spread_recv.at[1]).wait()
        pltpu.make_async_copy(ends_in, ends_in, spread_recv.at[2]).wait()
        loads[4].wait()
        line = lax.broadcasted_iota(jnp.int32, (2 * sp_count, 128), 0)
        lane = lax.broadcasted_iota(jnp.int32, (2 * sp_count, 128), 1)
        place = (((line == 2 * s) & (lane == 0)) | ((line == 2 * s + 1) & (lane == 127))).astype(
            jnp.float32
        )
        row = lax.broadcasted_iota(jnp.int32, (1, 1, 8, 128), 2)
        lane = lax.broadcasted_iota(jnp.int32, (1, 1, 8, 128), 3)
        shape = (group, layers, 8, 128)
        for block in range(sp_count):
            part = pl.ds(group * block, group)
            center = conc[part, middle]
            edges = spread_edges(sides_in[block][:, :tiles], place).reshape(shape)
            upper = jnp.broadcast_to(ends_in[0, part][:, :, None, :], shape)
            under = jnp.broadcast_to(ends_in[1, part][:, :, None, :], shape)
            beside_conc[0, part] = jnp.where(row == 7, under, shifted(center, 1, 2))
            beside_conc[1, part] = jnp.where(row == 0, upper, shifted(center, -1, 2))
            beside_conc[2, part] = jnp.where(lane == 127, edges, shifted(center, 1, 3))
            beside_conc[3, part] = jnp.where(lane == 0, edges, shifted(center, -1, 3))

    def own(values):
        return values[:, 8:16, :128]

    basis = [source]
    for shift in SHIFTS:
        image = scale[None] * apply_flow(basis[-1], storage, faces)
        basis.append(image - shift * basis[-1])
    parts = [split(own(vector)) for vector in basis]
    size = len(SHIFTS)
    places = [(i, j) for i in range(size) for j in range(i, size + 1)]
    products = [inner_product(parts[i], parts[j]) for i, j in places]
    lines = 32
    blank = jnp.zeros((8, 128), jnp.float32)
    products += [(blank, blank)] * (lines - len(products))
    rows = [merge_rows(products[first : first + 8]) for first in range(0, lines, 8)]
    rows = [row[0] for row in rows] + [row[1] for row in rows]
    table = jnp.concatenate(rows + [blank] * (16 - len(rows)), axis=0).T
    error = jnp.zeros_like(table)
    while table.shape[0] > 8:
        table, error = halved(table, error)
    for shift in (4, 2, 1):
        table, more = exact_sum(table, pltpu.roll(table, shift, 0))
        error = error + pltpu.roll(error, shift, 0) + more
    lane = lax.broadcasted_iota(jnp.int32, (8, 128), 1)
    table = jnp.where(lane < 2 * lines, table, pltpu.roll(error, 2 * lines, 1))
    gathered[slot] = table[:1]
    for peer in everyone:
        remote(gathered.at[slot], gathered.at[slot], sum_send.at[0], sum_recv.at[0], peer)
    fill_gram()
    place_species()
    all_others = gathered.at[pl.ds(0, len(everyone))]
    pltpu.make_async_copy(all_others, all_others, sum_recv.at[0]).wait()
    table = gathered[...]
    error = jnp.zeros_like(table)
    while table.shape[0] > 1:
        table, error = halved(table, error)
    table = jnp.broadcast_to(table[0], (8, 128))
    error = jnp.broadcast_to(error[0], (8, 128))
    error = error + pltpu.roll(table, 128 - 2 * lines, 1) + pltpu.roll(table, 128 - lines, 1)
    high, low = paired(table, error)
    entries = {
        place: tuple(
            jnp.broadcast_to(part[:1, k : k + 1], (1, 128)) for part in (high, low)
        )
        for k, place in enumerate(places)
    }
    answer = solve_krylov(entries)
    head = None
    for value, vector in zip(answer, basis):
        term = (scale * jnp.concatenate([value, value], axis=1))[None] * vector
        head = term if head is None else head + term

    head_out[...] = own(head)
    kept = jnp.ones_like(own(head))
    for number, (face, head_beside) in enumerate(zip(faces, six_beside(head))):
        face = own(face)
        velocity = face * (own(head) - own(head_beside))
        kept = kept - time_step * (jnp.maximum(velocity, 0.0) + dispersion * face)
        weights[number] = time_step * (dispersion * face - jnp.minimum(velocity, 0.0))
    weights[6] = kept

    loads[5].wait()
    chunk = CHUNK

    def react_chunk(step, carry):
        span = pl.ds(step * chunk, chunk)
        gram = [
            [gram_table[max(i, j), min(i, j)] for j in range(mineral_count)]
            for i in range(mineral_count)
        ]
        scales = [weights[number, span] for number in range(7)]
        moved = []
        for c in range(species_count):
            fields = [conc[c, pl.ds(step * chunk + shift, chunk)] for shift in (2, 0)]
            fields += [beside_conc[side, c, span] for side in range(4)]
            fields.append(conc[c, pl.ds(step * chunk + 1, chunk)])
            moved.append(weighted(scales, fields))
        result = react(
            moved,
            mineral_zone[span],
            rate_table,
            stoich,
            log_equil,
            gram,
        )
        for c in range(species_count):
            reacted[c, span] = result[c]
        for k in range(1, sp_count):
            to = (s + k) % sp_count
            remote(
                reacted.at[pl.ds(group * to, group), span],
                species_out.at[:, span, :, columns_of(s)],
                result_sem.at[0],
                result_sem.at[1],
                (g, to),
            )
        pltpu.make_async_copy(
            reacted.at[mine, span], species_out.at[:, span, :, columns_of(s)], result_sem.at[2]
        ).start()
        return carry

    lax.fori_loop(0, layers // chunk, react_chunk, 0)

    for copy in halo:
        copy.wait_send()
    pltpu.make_async_copy(all_others, all_others, sum_send.at[0]).wait()
    three = conc.at[pl.ds(0, group * (sp_count - 1)), middle]
    pltpu.make_async_copy(three, three, spread_send.at[0]).wait()
    part = sides_in.at[pl.ds(0, sp_count - 1)]
    pltpu.make_async_copy(part, part, spread_send.at[1]).wait()
    pltpu.make_async_copy(ends_in, ends_in, spread_send.at[2]).wait()
    pltpu.make_async_copy(three, three, result_sem.at[0]).wait()
    pltpu.make_async_copy(three, three, result_sem.at[1]).wait()
    once = reacted.at[pl.ds(0, group)]
    pltpu.make_async_copy(once, once, result_sem.at[2]).wait()


def hand_over(head, species, head_out, species_out, head_held, species_held, load_sem, store_sem):
    parts = [(head, head_held, head_out)]
    for k in range(species.shape[0]):
        for first in range(0, species.shape[1], PIECE):
            part = (k, pl.ds(first, PIECE))
            parts.append((species.at[part], species_held.at[part], species_out.at[part]))
    loads, stores = [], []
    for number, (source, held, target) in enumerate(parts):
        loads.append(pltpu.make_async_copy(source, held, load_sem.at[number]))
        stores.append(pltpu.make_async_copy(held, target, store_sem.at[number]))
    for copy in loads:
        copy.start()
    for load, store in zip(loads, stores):
        load.wait()
        store.start()
    for copy in stores:
        copy.wait()


def per_device(mesh, *arrays):
    gx_count, sp_count = mesh.shape["gx"], mesh.shape["sp"]
    inner = min(8, gx_count // 2)
    species = arrays[5]
    group, layers, _, width = species.shape
    total = group * sp_count
    minerals = arrays[8].shape[1]
    arrays = arrays[:8] + (arrays[8].T,) + arrays[9:]
    tables = arrays[3:5] + arrays[7:]
    vmem = pl.BlockSpec(memory_space=pltpu.VMEM)
    hbm = pl.BlockSpec(memory_space=pltpu.HBM)
    cells = (layers, 8, 128)

    def floats(*shape):
        return pltpu.VMEM(shape, jnp.float32)

    results = (
        pl.pallas_call(
            functools.partial(step_kernel, gx_count, sp_count, inner),
            out_shape=(
                jax.ShapeDtypeStruct(cells, jnp.float32),
                jax.ShapeDtypeStruct(species.shape, jnp.float32),
            ),
            in_specs=[hbm] * 10,
            out_specs=(vmem, hbm),
            scratch_shapes=[
                *[pltpu.SMEM(table.shape, jnp.float32) for table in tables],
                floats(*cells),
                floats(*cells),
                pltpu.VMEM(cells, jnp.int32),
                pltpu.VMEM(cells, jnp.int32),
                floats(*species.shape),
                floats(2, *cells),
                floats(2, 2, *cells),
                floats(16, 128),
                floats(3, 16, 128),
                floats(gx_count * sp_count, 1, 128),
                floats(total, layers + 2, 8, 128),
                floats(2, group, layers, width),
                floats(2, total, layers, 128),
                floats(2 * sp_count, 256),
                floats(sp_count, 2 * sp_count, 256),
                floats(4, total, *cells),
                floats(7, *cells),
                floats(total, *cells),
                pltpu.SMEM((minerals, minerals), jnp.float32),
                pltpu.SemaphoreType.DMA((11,)),
                pltpu.SemaphoreType.DMA((8,)),
                pltpu.SemaphoreType.DMA((8,)),
                pltpu.SemaphoreType.DMA((1,)),
                pltpu.SemaphoreType.DMA((1,)),
                pltpu.SemaphoreType.DMA((3,)),
                pltpu.SemaphoreType.DMA((3,)),
                pltpu.SemaphoreType.DMA((3,)),
            ],
            compiler_params=pltpu.CompilerParams(
                collective_id=0, has_side_effects=True, vmem_limit_bytes=60 * 1024 * 1024
            ),
        )(*arrays)
    )

    return tuple(
        pl.pallas_call(
            hand_over,
            out_shape=tuple(jax.ShapeDtypeStruct(r.shape, r.dtype) for r in results),
            in_specs=[hbm, hbm],
            out_specs=(hbm, hbm),
            scratch_shapes=[
                *[floats(*r.shape) for r in results],
                pltpu.SemaphoreType.DMA((1 + group * layers // PIECE,)),
                pltpu.SemaphoreType.DMA((1 + group * layers // PIECE,)),
            ],
            compiler_params=pltpu.CompilerParams(vmem_limit_bytes=60 * 1024 * 1024),
        )(*results)
    )


def solution(mesh):
    cells = P(None, "gx", "sp")
    groups = P("sp", None, "gx", None)
    return jax.shard_map(
        functools.partial(per_device, mesh),
        mesh=mesh,
        in_specs=(cells, cells, cells, P(), P(), groups, cells, P(), P(), P()),
        out_specs=(cells, groups),
        check_vma=False,
    )
```

```python
import functools

import jax
import jax.numpy as jnp
from jax import lax
from jax.experimental import pallas as pl
from jax.experimental.pallas import tpu as pltpu
from jax.sharding import PartitionSpec as P

NEWTON = 2
ROUNDING = 4.3e-12
SHIFTS = (0.5, 0.125, 1.0, 0.25, 1.0, 0.0625)
CHUNK = 2
PIECE = 2

time_step = 0.05
dispersion = 0.5
reaction_span = 0.5
newton_damping = 0.5

MESH = pl.DeviceIdType.MESH
EXACT = lax.Precision.HIGHEST


def table_lookup(labels, table):
    size = table.shape[0] if hasattr(table, "shape") else len(table)
    found = jnp.full(labels.shape, table[0], jnp.float32)
    for level in range(1, size):
        found = jnp.where(labels == level, table[level], found)
    return found


def harmonic_safe(center, other):
    return 2.0 * center * other / jnp.maximum(center + other, 1e-30)


def shifted(field, offset, axis):
    size = field.shape[axis]
    return pltpu.roll(field, (-offset) % size, axis)


def layer_above(field):
    return jnp.concatenate([field[1:], field[-1:]], axis=0)


def layer_below(field):
    return jnp.concatenate([field[:1], field[:-1]], axis=0)


def six_faces(conduct):
    east = harmonic_safe(conduct, shifted(conduct, 1, 2))
    south = harmonic_safe(conduct, shifted(conduct, 1, 1))
    top = harmonic_safe(conduct[:-1], conduct[1:])
    none = jnp.zeros_like(conduct[:1])
    return (
        jnp.concatenate([top, none], axis=0),
        jnp.concatenate([none, top], axis=0),
        south,
        shifted(south, -1, 1),
        east,
        shifted(east, -1, 2),
    )


def six_beside(field):
    return (
        layer_above(field),
        layer_below(field),
        shifted(field, 1, 1),
        shifted(field, -1, 1),
        shifted(field, 1, 2),
        shifted(field, -1, 2),
    )


def apply_flow(field, storage, faces):
    result = storage * field
    for face, beside in zip(faces, six_beside(field)):
        result = result + face * (field - beside)
    return result


def exact_sum(left, right):
    total = left + right
    part = total - left
    return total, (left - (total - part)) + (right - part)


def split(value):
    wide = 4097.0 * value
    high = wide - (wide - value)
    return high, value - high


def paired(high, low):
    total = high + low
    return total, low - (total - high)


def pair_add(left, right):
    total, error = exact_sum(left[0], right[0])
    return paired(total, error + (left[1] + right[1]))


def pair_minus(left, right):
    return pair_add(left, (-right[0], -right[1]))


def pair_times(left, right):
    left_high, left_low = split(left[0])
    right_high, right_low = split(right[0])
    product = left[0] * right[0]
    error = left_high * right_high - product
    error = error + left_high * right_low + left_low * right_high + left_low * right_low
    return paired(product, error + (left[0] * right[1] + left[1] * right[0]))


def pair_inverse(value):
    guess = 1.0 / value[0]
    none = jnp.zeros_like(guess)
    rest = pair_minus((none + 1.0, none), pair_times(value, (guess, none)))
    return paired(guess, guess * (rest[0] + rest[1]))


def halved(total, error):
    half = total.shape[0] // 2
    total, more = exact_sum(total[:half], total[half:])
    return total, error[:half] + error[half:] + more


def inner_product(left, right):
    total = left[0] * right[0]
    error = left[0] * right[1] + left[1] * right[0] + left[1] * right[1]
    while total.shape[0] > 1:
        total, error = halved(total, error)
    return total[0], error[0]


def merge_rows(pairs):
    row = lax.broadcasted_iota(jnp.int32, (8, 128), 0)
    for shift in (4, 2, 1):
        keep = (row % (2 * shift)) < shift
        merged = []
        for left, right in zip(pairs[:shift], pairs[shift:]):
            ends = []
            for part in range(2):
                ends.append(
                    (
                        jnp.where(keep, left[part], pltpu.roll(right[part], shift, 0)),
                        jnp.where(keep, pltpu.roll(left[part], 8 - shift, 0), right[part]),
                    )
                )
            total, error = exact_sum(*ends[0])
            merged.append((total, error + (ends[1][0] + ends[1][1])))
        pairs = merged
    return pairs[0]


def solve_krylov(gram):
    size = len(SHIFTS)
    matrix = {}
    for i in range(size):
        for j in range(i, size):
            after = pair_add(gram[i, j + 1], gram[min(i + 1, j), max(i + 1, j)])
            for shift in (SHIFTS[i], SHIFTS[j]):
                after = pair_add(after, (shift * gram[i, j][0], shift * gram[i, j][1]))
            matrix[j, i] = after
    right = [gram[0, i] for i in range(size)]
    squares = [gram[k, k][0] for k in range(size)]
    mixes = []
    inverse, lower = [None] * size, {}
    for k in range(size):
        pivot = matrix[k, k]
        mix = [jnp.zeros_like(squares[0])] * k + [jnp.ones_like(squares[0])]
        for i in range(k):
            for j in range(i + 1):
                mix[j] = mix[j] - lower[k, i][0] * mixes[i][j]
        mixes.append(mix)
        noise = weighted([value * value for value in mix], squares)
        usable = pivot[0] > ROUNDING * noise
        inverse[k] = tuple(jnp.where(usable, part, 0.0) for part in pair_inverse(pivot))
        for i in range(k + 1, size):
            lower[i, k] = pair_times(matrix[i, k], inverse[k])
        for i in range(k + 1, size):
            right[i] = pair_minus(right[i], pair_times(lower[i, k], right[k]))
            for j in range(k + 1, i + 1):
                matrix[i, j] = pair_minus(
                    matrix[i, j], pair_times(lower[i, k], matrix[j, k])
                )
    answer = [None] * size
    for k in reversed(range(size)):
        value = pair_times(right[k], inverse[k])[0]
        for i in range(k + 1, size):
            value = value - lower[i, k][0] * answer[i]
        answer[k] = value
    return [2.0 * value for value in answer]


def column_edges(pick, block):
    return lax.dot_general(
        pick,
        block,
        (((1,), (1,)), ((), ())),
        precision=EXACT,
        preferred_element_type=jnp.float32,
    )


def spread_edges(edges, pick):
    return lax.dot_general(
        edges,
        pick,
        (((0,), (0,)), ((), ())),
        precision=EXACT,
        preferred_element_type=jnp.float32,
    )


def weighted(scales, fields):
    total = None
    for scale, field in zip(scales, fields):
        term = scale * field
        total = term if total is None else total + term
    return total


def mineral_correction(gram, slope, start):
    count = len(start)
    right = [weighted([gram[i][k] for k in range(count)], start) for i in range(count)]
    schur = {(i, j): gram[i][j] for i in range(count) for j in range(i + 1)}
    pivot, lower = [None] * count, {}
    for k in range(count):
        pivot[k] = slope[k] / (1.0 + slope[k] * schur[k, k])
        for i in range(k + 1, count):
            lower[i, k] = schur[i, k] * pivot[k]
        for i in range(k + 1, count):
            right[i] = right[i] - lower[i, k] * right[k]
            for j in range(k + 1, i + 1):
                schur[i, j] = schur[i, j] - lower[i, k] * schur[j, k]
    answer = [None] * count
    for k in reversed(range(count)):
        value = pivot[k] * right[k]
        for i in range(k + 1, count):
            value = value - lower[i, k] * answer[i]
        answer[k] = value
    return answer


def react(moved, labels, rate_table, stoich, log_equil, gram):
    zones, minerals = rate_table.shape
    species = len(moved)
    rates = [table_lookup(labels, [rate_table[z, m] for z in range(zones)]) for m in range(minerals)]
    base = [
        weighted([stoich[m, c] for c in range(species)], moved) - log_equil[m]
        for m in range(minerals)
    ]
    extent = None
    for newton_pass in range(NEWTON):
        affinity = base
        if extent is not None:
            affinity = [base[m] + weighted(gram[m], extent) for m in range(minerals)]
        tangent = [jnp.tanh(value) for value in affinity]
        start = [reaction_span * rates[m] * tangent[m] for m in range(minerals)]
        if extent is not None:
            start = [extent[m] + start[m] for m in range(minerals)]
        slope = [
            reaction_span * rates[m] * jnp.maximum(1.0 - tangent[m] * tangent[m], 0.0)
            for m in range(minerals)
        ]
        correction = mineral_correction(gram, slope, start)
        step = [newton_damping * (start[m] - correction[m]) for m in range(minerals)]
        extent = [-step[m] if extent is None else extent[m] - step[m] for m in range(minerals)]
    return [
        moved[c] + weighted([stoich[m, c] for m in range(minerals)], extent)
        for c in range(species)
    ]


def step_kernel(
    gx_count,
    sp_count,
    inner,
    previous_head_in,
    recharge_in,
    soil_zone_in,
    soil_cond_in,
    soil_store_in,
    species_in,
    mineral_zone_in,
    rate_table_in,
    stoich_in,
    log_equil_in,
    head_out,
    species_out,
    soil_cond,
    soil_store,
    rate_table,
    stoich,
    log_equil,
    previous_head,
    recharge,
    soil_zone,
    mineral_zone,
    species,
    field,
    rows_in,
    edge_out,
    edge_in,
    gathered,
    conc,
    ends_out,
    ends_in,
    sides_out,
    sides_in,
    beside_conc,
    weights,
    reacted,
    gram_table,
    load_sem,
    halo_send,
    halo_recv,
    sum_send,
    sum_recv,
    spread_send,
    spread_recv,
    result_sem,
):
    g = lax.axis_index("gx")
    s = lax.axis_index("sp")
    cores, across = 2, inner // 2
    down = gx_count // inner
    core, x, y = lax.rem(g, cores), lax.rem(lax.div(g, cores), across), lax.div(g, inner)
    at_core = [lax.rem(core + k, cores) for k in range(cores)]
    at_x = [lax.rem(x + k, across) * cores for k in range(across)]
    at_y = [lax.rem(y + k, down) * inner for k in range(down)]
    at_z = [lax.rem(s + k, sp_count) for k in range(sp_count)]
    at_gx = [[[a + b + c for c in at_core] for b in at_x] for a in at_y]

    def hops(k, count):
        return min(k, count - k)

    steps = [
        (hops(i, down) + hops(j, across) + hops(m, sp_count), k, i, j, m)
        for i in range(down)
        for j in range(across)
        for k in range(cores)
        for m in range(sp_count)
    ][1:]
    everyone = [
        (at_gx[i][j][k], at_z[m]) for _, k, i, j, m in sorted(steps, reverse=True)
    ]
    slot = g * sp_count + s
    group = species_in.shape[0]
    layers = species_in.shape[1]

    def columns_of(device):
        return pl.ds(pl.multiple_of(device * 128, 128), 128)

    def beside(rows, columns):
        return ((g + rows + gx_count) % gx_count, (s + columns) % sp_count)

    def remote(source, target, send, recv, peer):
        copy = pltpu.make_async_remote_copy(
            src_ref=source,
            dst_ref=target,
            send_sem=send,
            recv_sem=recv,
            device_id=peer,
            device_id_type=MESH,
        )
        copy.start()
        return copy

    middle = pl.ds(1, layers)
    loads = [
        pltpu.make_async_copy(source, target, load_sem.at[number])
        for number, (source, target) in enumerate(
            (
                (soil_zone_in, soil_zone),
                (previous_head_in, previous_head),
                (recharge_in, recharge),
                (species_in, species),
                (species_in.at[:, :, :, columns_of(s)], conc.at[pl.ds(group * s, group), middle]),
                (mineral_zone_in, mineral_zone),
                (soil_store_in, soil_store),
                (soil_cond_in, soil_cond),
                (rate_table_in, rate_table),
                (stoich_in, stoich),
                (log_equil_in, log_equil),
            )
        )
    ]
    for copy in loads:
        copy.start()

    offsets = [(rows, columns) for rows in (-1, 0, 1) for columns in (-1, 0, 1) if (rows, columns) != (0, 0)]
    barrier = pltpu.get_barrier_semaphore()
    for peer in everyone:
        pl.semaphore_signal(barrier, inc=1, device_id=peer, device_id_type=MESH)

    for copy in loads[:3] + loads[6:7]:
        copy.wait()
    for number in range(group * sp_count):
        conc[number, 0] = jnp.zeros((8, 128), jnp.float32)
        conc[number, layers + 1] = jnp.zeros((8, 128), jnp.float32)
    zone = soil_zone[...]
    field[0] = table_lookup(zone, soil_store) * previous_head[...] + recharge[...]
    field[1] = zone.astype(jnp.float32)
    line = lax.broadcasted_iota(jnp.int32, (16, 128), 0)
    lane = lax.broadcasted_iota(jnp.int32, (16, 128), 1)
    pick = (lane == jnp.where(line < 8, line, line + 112)).astype(jnp.float32)
    edge_out[...] = column_edges(pick, field[...].reshape(128, 128))

    pl.semaphore_wait(barrier, len(everyone))
    halo = []
    for number, (rows, columns) in enumerate(offsets):
        if columns == 0:
            source, target = field, rows_in.at[0 if rows == 1 else 1]
        else:
            first = 8 if columns == 1 else 0
            source = edge_out.at[pl.ds(first, 8)]
            target = edge_in.at[1 - rows, pl.ds(first, 8)]
        halo.append(
            remote(source, target, halo_send.at[number], halo_recv.at[number], beside(rows, columns))
        )

    mine = pl.ds(group * s, group)
    loads[3].wait()
    for k in range(1, sp_count):
        to = (s + k) % sp_count
        remote(
            species.at[:, :, :, columns_of(to)],
            conc.at[mine, middle],
            spread_send.at[0],
            spread_recv.at[0],
            (g, to),
        )
    width = species.shape[3]
    line = lax.broadcasted_iota(jnp.int32, (2 * sp_count, width), 0)
    lane = lax.broadcasted_iota(jnp.int32, (2 * sp_count, width), 1)
    wanted = jnp.where(line % 2 == 0, (line // 2) * 128 - 1, (line // 2) * 128 + 128)
    tiles = group * layers * 8
    sides_out[:, :tiles] = column_edges(
        (lane == wanted).astype(jnp.float32), species[...].reshape(tiles, width)
    )
    for layer in range(layers):
        ends_out[0, :, layer : layer + 1, :] = species[:, layer, 0:1, :]
        ends_out[1, :, layer : layer + 1, :] = species[:, layer, 7:8, :]
    sides_in[s] = sides_out[...]
    for k in range(1, sp_count):
        to = (s + k) % sp_count
        remote(sides_out, sides_in.at[s], spread_send.at[1], spread_recv.at[1], (g, to))
    for k in range(sp_count):
        to = (s + k) % sp_count
        for rows in (-1, 1):
            remote(
                ends_out.at[0 if rows == -1 else 1, :, :, columns_of(to)],
                ends_in.at[1 if rows == -1 else 0, mine],
                spread_send.at[2],
                spread_recv.at[2],
                beside(rows, k),
            )

    for copy in loads[7:]:
        copy.wait()
    for copy in halo:
        copy.wait_recv()

    row_blocks = []
    for block, center in enumerate((rows_in[0], field[...], rows_in[1])):
        side = spread_edges(edge_in[block], pick).reshape(2, 8, 8, 128)
        row_blocks.append(jnp.concatenate([center, side], axis=3))
    wide = jnp.concatenate(row_blocks, axis=2)
    row = lax.broadcasted_iota(jnp.int32, (24, 256), 0)
    column = lax.broadcasted_iota(jnp.int32, (24, 256), 1)
    first_row = jnp.where(g > 0, 0, 8)
    end_row = jnp.where(g < gx_count - 1, 24, 16)
    end_right = jnp.where(s < sp_count - 1, 136, 128)
    first_left = jnp.where(s > 0, 248, 256)
    inside = (
        (row >= first_row)
        & (row < end_row)
        & ((column < end_right) | (column >= first_left))
    )[None]
    source = jnp.where(inside, wide[0], 0.0)
    conduct = jnp.where(inside, table_lookup(wide[1], soil_cond), 0.0)
    storage = jnp.where(inside, table_lookup(wide[1], soil_store), 0.0)
    faces = six_faces(conduct)

    store_most, cond_most = soil_store[0], soil_cond[0]
    for level in range(1, soil_store.shape[0]):
        store_most = jnp.maximum(store_most, soil_store[level])
        cond_most = jnp.maximum(cond_most, soil_cond[level])
    scale = 2.0 / jnp.full((1, 256), store_most + 12.0 * cond_most, jnp.float32)

    mineral_count, species_count = stoich.shape

    def fill_gram():
        columns = [
            [stoich[m, c] for c in range(species_count)] for m in range(mineral_count)
        ]
        for i in range(mineral_count):
            for j in range(i + 1):
                terms = [a * b for a, b in zip(columns[i], columns[j])]
                while len(terms) > 1:
                    terms = [sum(terms[k : k + 2][1:], terms[k]) for k in range(0, len(terms), 2)]
                gram_table[i, j] = terms[0]

    def place_species():
        whole = conc.at[pl.ds(0, group * (sp_count - 1)), middle]
        pltpu.make_async_copy(whole, whole, spread_recv.at[0]).wait()
        part = sides_in.at[pl.ds(0, sp_count - 1)]
        pltpu.make_async_copy(part, part, spread_recv.at[1]).wait()
        pltpu.make_async_copy(ends_in, ends_in, spread_recv.at[2]).wait()
        loads[4].wait()
        line = lax.broadcasted_iota(jnp.int32, (2 * sp_count, 128), 0)
        lane = lax.broadcasted_iota(jnp.int32, (2 * sp_count, 128), 1)
        place = (((line == 2 * s) & (lane == 0)) | ((line == 2 * s + 1) & (lane == 127))).astype(
            jnp.float32
        )
        row = lax.broadcasted_iota(jnp.int32, (1, 1, 8, 128), 2)
        lane = lax.broadcasted_iota(jnp.int32, (1, 1, 8, 128), 3)
        shape = (group, layers, 8, 128)
        for block in range(sp_count):
            part = pl.ds(group * block, group)
            center = conc[part, middle]
            edges = spread_edges(sides_in[block][:, :tiles], place).reshape(shape)
            upper = jnp.broadcast_to(ends_in[0, part][:, :, None, :], shape)
            under = jnp.broadcast_to(ends_in[1, part][:, :, None, :], shape)
            beside_conc[0, part] = jnp.where(row == 7, under, shifted(center, 1, 2))
            beside_conc[1, part] = jnp.where(row == 0, upper, shifted(center, -1, 2))
            beside_conc[2, part] = jnp.where(lane == 127, edges, shifted(center, 1, 3))
            beside_conc[3, part] = jnp.where(lane == 0, edges, shifted(center, -1, 3))

    def own(values):
        return values[:, 8:16, :128]

    basis = [source]
    for shift in SHIFTS:
        image = scale[None] * apply_flow(basis[-1], storage, faces)
        basis.append(image - shift * basis[-1])
    parts = [split(own(vector)) for vector in basis]
    size = len(SHIFTS)
    places = [(i, j) for i in range(size) for j in range(i, size + 1)]
    products = [inner_product(parts[i], parts[j]) for i, j in places]
    lines = 32
    blank = jnp.zeros((8, 128), jnp.float32)
    products += [(blank, blank)] * (lines - len(products))
    rows = [merge_rows(products[first : first + 8]) for first in range(0, lines, 8)]
    rows = [row[0] for row in rows] + [row[1] for row in rows]
    table = jnp.concatenate(rows + [blank] * (16 - len(rows)), axis=0).T
    error = jnp.zeros_like(table)
    while table.shape[0] > 8:
        table, error = halved(table, error)
    for shift in (4, 2, 1):
        table, more = exact_sum(table, pltpu.roll(table, shift, 0))
        error = error + pltpu.roll(error, shift, 0) + more
    lane = lax.broadcasted_iota(jnp.int32, (8, 128), 1)
    table = jnp.where(lane < 2 * lines, table, pltpu.roll(error, 2 * lines, 1))
    gathered[slot] = table[:1]
    for peer in everyone:
        remote(gathered.at[slot], gathered.at[slot], sum_send.at[0], sum_recv.at[0], peer)
    fill_gram()
    place_species()
    all_others = gathered.at[pl.ds(0, len(everyone))]
    pltpu.make_async_copy(all_others, all_others, sum_recv.at[0]).wait()
    table = gathered[...]
    error = jnp.zeros_like(table)
    while table.shape[0] > 1:
        table, error = halved(table, error)
    table = jnp.broadcast_to(table[0], (8, 128))
    error = jnp.broadcast_to(error[0], (8, 128))
    error = error + pltpu.roll(table, 128 - 2 * lines, 1) + pltpu.roll(table, 128 - lines, 1)
    high, low = paired(table, error)
    entries = {
        place: tuple(
            jnp.broadcast_to(part[:1, k : k + 1], (1, 128)) for part in (high, low)
        )
        for k, place in enumerate(places)
    }
    answer = solve_krylov(entries)
    head = None
    for value, vector in zip(answer, basis):
        term = (scale * jnp.concatenate([value, value], axis=1))[None] * vector
        head = term if head is None else head + term

    head_out[...] = own(head)
    kept = jnp.ones_like(own(head))
    for number, (face, head_beside) in enumerate(zip(faces, six_beside(head))):
        face = own(face)
        velocity = face * (own(head) - own(head_beside))
        kept = kept - time_step * (jnp.maximum(velocity, 0.0) + dispersion * face)
        weights[number] = time_step * (dispersion * face - jnp.minimum(velocity, 0.0))
    weights[6] = kept

    loads[5].wait()
    chunk = CHUNK

    def react_chunk(step, carry):
        span = pl.ds(step * chunk, chunk)
        gram = [
            [gram_table[max(i, j), min(i, j)] for j in range(mineral_count)]
            for i in range(mineral_count)
        ]
        scales = [weights[number, span] for number in range(7)]
        moved = []
        for c in range(species_count):
            fields = [conc[c, pl.ds(step * chunk + shift, chunk)] for shift in (2, 0)]
            fields += [beside_conc[side, c, span] for side in range(4)]
            fields.append(conc[c, pl.ds(step * chunk + 1, chunk)])
            moved.append(weighted(scales, fields))
        result = react(
            moved,
            mineral_zone[span],
            rate_table,
            stoich,
            log_equil,
            gram,
        )
        for c in range(species_count):
            reacted[c, span] = result[c]
        for k in range(1, sp_count):
            to = (s + k) % sp_count
            remote(
                reacted.at[pl.ds(group * to, group), span],
                species_out.at[:, span, :, columns_of(s)],
                result_sem.at[0],
                result_sem.at[1],
                (g, to),
            )
        pltpu.make_async_copy(
            reacted.at[mine, span], species_out.at[:, span, :, columns_of(s)], result_sem.at[2]
        ).start()
        return carry

    lax.fori_loop(0, layers // chunk, react_chunk, 0)

    for copy in halo:
        copy.wait_send()
    pltpu.make_async_copy(all_others, all_others, sum_send.at[0]).wait()
    three = conc.at[pl.ds(0, group * (sp_count - 1)), middle]
    pltpu.make_async_copy(three, three, spread_send.at[0]).wait()
    part = sides_in.at[pl.ds(0, sp_count - 1)]
    pltpu.make_async_copy(part, part, spread_send.at[1]).wait()
    pltpu.make_async_copy(ends_in, ends_in, spread_send.at[2]).wait()
    pltpu.make_async_copy(three, three, result_sem.at[0]).wait()
    pltpu.make_async_copy(three, three, result_sem.at[1]).wait()
    once = reacted.at[pl.ds(0, group)]
    pltpu.make_async_copy(once, once, result_sem.at[2]).wait()


def hand_over(head, species, head_out, species_out, head_held, species_held, load_sem, store_sem):
    parts = [(head, head_held, head_out)]
    for k in range(species.shape[0]):
        for first in range(0, species.shape[1], PIECE):
            part = (k, pl.ds(first, PIECE))
            parts.append((species.at[part], species_held.at[part], species_out.at[part]))
    loads, stores = [], []
    for number, (source, held, target) in enumerate(parts):
        loads.append(pltpu.make_async_copy(source, held, load_sem.at[number]))
        stores.append(pltpu.make_async_copy(held, target, store_sem.at[number]))
    for copy in loads:
        copy.start()
    for load, store in zip(loads, stores):
        load.wait()
        store.start()
    for copy in stores:
        copy.wait()


def per_device(mesh, *arrays):
    gx_count, sp_count = mesh.shape["gx"], mesh.shape["sp"]
    inner = min(8, gx_count // 2)
    species = arrays[5]
    group, layers, _, width = species.shape
    total = group * sp_count
    minerals = arrays[8].shape[1]
    arrays = arrays[:8] + (arrays[8].T,) + arrays[9:]
    tables = arrays[3:5] + arrays[7:]
    vmem = pl.BlockSpec(memory_space=pltpu.VMEM)
    hbm = pl.BlockSpec(memory_space=pltpu.HBM)
    cells = (layers, 8, 128)

    def floats(*shape):
        return pltpu.VMEM(shape, jnp.float32)

    results = (
        pl.pallas_call(
            functools.partial(step_kernel, gx_count, sp_count, inner),
            out_shape=(
                jax.ShapeDtypeStruct(cells, jnp.float32),
                jax.ShapeDtypeStruct(species.shape, jnp.float32),
            ),
            in_specs=[hbm] * 10,
            out_specs=(vmem, hbm),
            scratch_shapes=[
                *[pltpu.SMEM(table.shape, jnp.float32) for table in tables],
                floats(*cells),
                floats(*cells),
                pltpu.VMEM(cells, jnp.int32),
                pltpu.VMEM(cells, jnp.int32),
                floats(*species.shape),
                floats(2, *cells),
                floats(2, 2, *cells),
                floats(16, 128),
                floats(3, 16, 128),
                floats(gx_count * sp_count, 1, 128),
                floats(total, layers + 2, 8, 128),
                floats(2, group, layers, width),
                floats(2, total, layers, 128),
                floats(2 * sp_count, 256),
                floats(sp_count, 2 * sp_count, 256),
                floats(4, total, *cells),
                floats(7, *cells),
                floats(total, *cells),
                pltpu.SMEM((minerals, minerals), jnp.float32),
                pltpu.SemaphoreType.DMA((11,)),
                pltpu.SemaphoreType.DMA((8,)),
                pltpu.SemaphoreType.DMA((8,)),
                pltpu.SemaphoreType.DMA((1,)),
                pltpu.SemaphoreType.DMA((1,)),
                pltpu.SemaphoreType.DMA((3,)),
                pltpu.SemaphoreType.DMA((3,)),
                pltpu.SemaphoreType.DMA((3,)),
            ],
            compiler_params=pltpu.CompilerParams(
                collective_id=0, has_side_effects=True, vmem_limit_bytes=60 * 1024 * 1024
            ),
        )(*arrays)
    )

    return tuple(
        pl.pallas_call(
            hand_over,
            out_shape=tuple(jax.ShapeDtypeStruct(r.shape, r.dtype) for r in results),
            in_specs=[hbm, hbm],
            out_specs=(hbm, hbm),
            scratch_shapes=[
                *[floats(*r.shape) for r in results],
                pltpu.SemaphoreType.DMA((1 + group * layers // PIECE,)),
                pltpu.SemaphoreType.DMA((1 + group * layers // PIECE,)),
            ],
            compiler_params=pltpu.CompilerParams(vmem_limit_bytes=60 * 1024 * 1024),
        )(*results)
    )


def solution(mesh):
    cells = P(None, "gx", "sp")
    groups = P("sp", None, "gx", None)
    return jax.shard_map(
        functools.partial(per_device, mesh),
        mesh=mesh,
        in_specs=(cells, cells, cells, P(), P(), groups, cells, P(), P(), P()),
        out_specs=(cells, groups),
        check_vma=False,
    )
```

```python
import functools

import jax
import jax.numpy as jnp
from jax import lax
from jax.experimental import pallas as pl
from jax.experimental.pallas import tpu as pltpu
from jax.sharding import PartitionSpec as P

NEWTON = 2
ROUNDING = 1.7e-13
SHIFTS = (0.5, 0.125, 1.0, 0.25, 1.0, 0.0625)
CHUNK = 2
PIECE = 2

time_step = 0.05
dispersion = 0.5
reaction_span = 0.5
newton_damping = 0.5

MESH = pl.DeviceIdType.MESH
EXACT = lax.Precision.HIGHEST


def table_lookup(labels, table):
    size = table.shape[0] if hasattr(table, "shape") else len(table)
    found = jnp.full(labels.shape, table[0], jnp.float32)
    for level in range(1, size):
        found = jnp.where(labels == level, table[level], found)
    return found


def harmonic_safe(center, other):
    return 2.0 * center * other / jnp.maximum(center + other, 1e-30)


def shifted(field, offset, axis):
    size = field.shape[axis]
    return pltpu.roll(field, (-offset) % size, axis)


def layer_above(field):
    return jnp.concatenate([field[1:], field[-1:]], axis=0)


def layer_below(field):
    return jnp.concatenate([field[:1], field[:-1]], axis=0)


def six_faces(conduct):
    east = harmonic_safe(conduct, shifted(conduct, 1, 2))
    south = harmonic_safe(conduct, shifted(conduct, 1, 1))
    top = harmonic_safe(conduct[:-1], conduct[1:])
    none = jnp.zeros_like(conduct[:1])
    return (
        jnp.concatenate([top, none], axis=0),
        jnp.concatenate([none, top], axis=0),
        south,
        shifted(south, -1, 1),
        east,
        shifted(east, -1, 2),
    )


def six_beside(field):
    return (
        layer_above(field),
        layer_below(field),
        shifted(field, 1, 1),
        shifted(field, -1, 1),
        shifted(field, 1, 2),
        shifted(field, -1, 2),
    )


def apply_flow(field, storage, faces):
    result = storage * field
    for face, beside in zip(faces, six_beside(field)):
        result = result + face * (field - beside)
    return result


def exact_sum(left, right):
    total = left + right
    part = total - left
    return total, (left - (total - part)) + (right - part)


def split(value):
    wide = 4097.0 * value
    high = wide - (wide - value)
    return high, value - high


def paired(high, low):
    total = high + low
    return total, low - (total - high)


def pair_add(left, right):
    total, error = exact_sum(left[0], right[0])
    return paired(total, error + (left[1] + right[1]))


def pair_minus(left, right):
    return pair_add(left, (-right[0], -right[1]))


def pair_times(left, right):
    left_high, left_low = split(left[0])
    right_high, right_low = split(right[0])
    product = left[0] * right[0]
    error = left_high * right_high - product
    error = error + left_high * right_low + left_low * right_high + left_low * right_low
    return paired(product, error + (left[0] * right[1] + left[1] * right[0]))


def pair_inverse(value):
    guess = 1.0 / value[0]
    none = jnp.zeros_like(guess)
    rest = pair_minus((none + 1.0, none), pair_times(value, (guess, none)))
    return paired(guess, guess * (rest[0] + rest[1]))


def halved(total, error):
    half = total.shape[0] // 2
    total, more = exact_sum(total[:half], total[half:])
    return total, error[:half] + error[half:] + more


def exact_product(left, left_parts, right):
    high, low = split(right)
    product = left * right
    error = left_parts[0] * high - product
    error = error + left_parts[0] * low + left_parts[1] * high + left_parts[1] * low
    return product, error


def rounding_left(field, following, shift, scale, factors, beside):
    total, error = exact_product(*factors[0], field)
    for factor, other in zip(factors[1:], beside):
        gap, lost = exact_sum(field, -other)
        flow, more = exact_product(*factor, gap)
        total, rest = exact_sum(total, flow)
        error = error + (rest + (more + factor[0] * lost))
    scaled, more = exact_product(*scale, total)
    more = more + scale[0] * error
    scaled, rest = exact_sum(scaled, -shift * field)
    left, last = exact_sum(scaled, -following)
    return left + (last + (rest + more))


def inner_product(left, right):
    total = left[0] * right[0]
    error = left[0] * right[1] + left[1] * right[0] + left[1] * right[1]
    while total.shape[0] > 1:
        total, error = halved(total, error)
    return total[0], error[0]


def merge_rows(pairs):
    row = lax.broadcasted_iota(jnp.int32, (8, 128), 0)
    for shift in (4, 2, 1):
        keep = (row % (2 * shift)) < shift
        merged = []
        for left, right in zip(pairs[:shift], pairs[shift:]):
            ends = []
            for part in range(2):
                ends.append(
                    (
                        jnp.where(keep, left[part], pltpu.roll(right[part], shift, 0)),
                        jnp.where(keep, pltpu.roll(left[part], 8 - shift, 0), right[part]),
                    )
                )
            total, error = exact_sum(*ends[0])
            merged.append((total, error + (ends[1][0] + ends[1][1])))
        pairs = merged
    return pairs[0]


def solve_krylov(gram, rounding):
    size = len(SHIFTS)
    matrix = {}
    for i in range(size):
        for j in range(i, size):
            after = pair_add(gram[i, j + 1], gram[min(i + 1, j), max(i + 1, j)])
            for shift in (SHIFTS[i], SHIFTS[j]):
                after = pair_add(after, (shift * gram[i, j][0], shift * gram[i, j][1]))
            after = pair_add(after, (rounding[i, j], jnp.zeros_like(after[0])))
            matrix[j, i] = after
    right = [gram[0, i] for i in range(size)]
    squares = [gram[k, k][0] for k in range(size)]
    mixes = []
    inverse, lower = [None] * size, {}
    for k in range(size):
        pivot = matrix[k, k]
        mix = [jnp.zeros_like(squares[0])] * k + [jnp.ones_like(squares[0])]
        for i in range(k):
            for j in range(i + 1):
                mix[j] = mix[j] - lower[k, i][0] * mixes[i][j]
        mixes.append(mix)
        noise = weighted([value * value for value in mix], squares)
        usable = pivot[0] > ROUNDING * noise
        inverse[k] = tuple(jnp.where(usable, part, 0.0) for part in pair_inverse(pivot))
        for i in range(k + 1, size):
            lower[i, k] = pair_times(matrix[i, k], inverse[k])
        for i in range(k + 1, size):
            right[i] = pair_minus(right[i], pair_times(lower[i, k], right[k]))
            for j in range(k + 1, i + 1):
                matrix[i, j] = pair_minus(
                    matrix[i, j], pair_times(lower[i, k], matrix[j, k])
                )
    answer = [None] * size
    for k in reversed(range(size)):
        value = pair_times(right[k], inverse[k])[0]
        for i in range(k + 1, size):
            value = value - lower[i, k][0] * answer[i]
        answer[k] = value
    return [2.0 * value for value in answer]


def column_edges(pick, block):
    return lax.dot_general(
        pick,
        block,
        (((1,), (1,)), ((), ())),
        precision=EXACT,
        preferred_element_type=jnp.float32,
    )


def spread_edges(edges, pick):
    return lax.dot_general(
        edges,
        pick,
        (((0,), (0,)), ((), ())),
        precision=EXACT,
        preferred_element_type=jnp.float32,
    )


def weighted(scales, fields):
    total = None
    for scale, field in zip(scales, fields):
        term = scale * field
        total = term if total is None else total + term
    return total


def mineral_correction(gram, slope, start):
    count = len(start)
    right = [weighted([gram[i][k] for k in range(count)], start) for i in range(count)]
    schur = {(i, j): gram[i][j] for i in range(count) for j in range(i + 1)}
    pivot, lower = [None] * count, {}
    for k in range(count):
        pivot[k] = slope[k] / (1.0 + slope[k] * schur[k, k])
        for i in range(k + 1, count):
            lower[i, k] = schur[i, k] * pivot[k]
        for i in range(k + 1, count):
            right[i] = right[i] - lower[i, k] * right[k]
            for j in range(k + 1, i + 1):
                schur[i, j] = schur[i, j] - lower[i, k] * schur[j, k]
    answer = [None] * count
    for k in reversed(range(count)):
        value = pivot[k] * right[k]
        for i in range(k + 1, count):
            value = value - lower[i, k] * answer[i]
        answer[k] = value
    return answer


def react(moved, labels, rate_table, stoich, log_equil, gram):
    zones, minerals = rate_table.shape
    species = len(moved)
    rates = [table_lookup(labels, [rate_table[z, m] for z in range(zones)]) for m in range(minerals)]
    base = [
        weighted([stoich[m, c] for c in range(species)], moved) - log_equil[m]
        for m in range(minerals)
    ]
    extent = None
    for newton_pass in range(NEWTON):
        affinity = base
        if extent is not None:
            affinity = [base[m] + weighted(gram[m], extent) for m in range(minerals)]
        tangent = [jnp.tanh(value) for value in affinity]
        start = [reaction_span * rates[m] * tangent[m] for m in range(minerals)]
        if extent is not None:
            start = [extent[m] + start[m] for m in range(minerals)]
        slope = [
            reaction_span * rates[m] * jnp.maximum(1.0 - tangent[m] * tangent[m], 0.0)
            for m in range(minerals)
        ]
        correction = mineral_correction(gram, slope, start)
        step = [newton_damping * (start[m] - correction[m]) for m in range(minerals)]
        extent = [-step[m] if extent is None else extent[m] - step[m] for m in range(minerals)]
    return [
        moved[c] + weighted([stoich[m, c] for m in range(minerals)], extent)
        for c in range(species)
    ]


def step_kernel(
    gx_count,
    sp_count,
    inner,
    previous_head_in,
    recharge_in,
    soil_zone_in,
    soil_cond_in,
    soil_store_in,
    species_in,
    mineral_zone_in,
    rate_table_in,
    stoich_in,
    log_equil_in,
    head_out,
    species_out,
    soil_cond,
    soil_store,
    rate_table,
    stoich,
    log_equil,
    previous_head,
    recharge,
    soil_zone,
    mineral_zone,
    species,
    field,
    rows_in,
    edge_out,
    edge_in,
    gathered,
    conc,
    ends_out,
    ends_in,
    sides_out,
    sides_in,
    beside_conc,
    weights,
    reacted,
    gram_table,
    load_sem,
    halo_send,
    halo_recv,
    sum_send,
    sum_recv,
    spread_send,
    spread_recv,
    result_sem,
):
    g = lax.axis_index("gx")
    s = lax.axis_index("sp")
    cores, across = 2, inner // 2
    down = gx_count // inner
    core, x, y = lax.rem(g, cores), lax.rem(lax.div(g, cores), across), lax.div(g, inner)
    at_core = [lax.rem(core + k, cores) for k in range(cores)]
    at_x = [lax.rem(x + k, across) * cores for k in range(across)]
    at_y = [lax.rem(y + k, down) * inner for k in range(down)]
    at_z = [lax.rem(s + k, sp_count) for k in range(sp_count)]
    at_gx = [[[a + b + c for c in at_core] for b in at_x] for a in at_y]

    def hops(k, count):
        return min(k, count - k)

    steps = [
        (hops(i, down) + hops(j, across) + hops(m, sp_count), k, i, j, m)
        for i in range(down)
        for j in range(across)
        for k in range(cores)
        for m in range(sp_count)
    ][1:]
    everyone = [
        (at_gx[i][j][k], at_z[m]) for _, k, i, j, m in sorted(steps, reverse=True)
    ]
    slot = g * sp_count + s
    group = species_in.shape[0]
    layers = species_in.shape[1]

    def columns_of(device):
        return pl.ds(pl.multiple_of(device * 128, 128), 128)

    def beside(rows, columns):
        return ((g + rows + gx_count) % gx_count, (s + columns) % sp_count)

    def remote(source, target, send, recv, peer):
        copy = pltpu.make_async_remote_copy(
            src_ref=source,
            dst_ref=target,
            send_sem=send,
            recv_sem=recv,
            device_id=peer,
            device_id_type=MESH,
        )
        copy.start()
        return copy

    middle = pl.ds(1, layers)
    loads = [
        pltpu.make_async_copy(source, target, load_sem.at[number])
        for number, (source, target) in enumerate(
            (
                (soil_zone_in, soil_zone),
                (previous_head_in, previous_head),
                (recharge_in, recharge),
                (species_in, species),
                (species_in.at[:, :, :, columns_of(s)], conc.at[pl.ds(group * s, group), middle]),
                (mineral_zone_in, mineral_zone),
                (soil_store_in, soil_store),
                (soil_cond_in, soil_cond),
                (rate_table_in, rate_table),
                (stoich_in, stoich),
                (log_equil_in, log_equil),
            )
        )
    ]
    for copy in loads:
        copy.start()

    offsets = [(rows, columns) for rows in (-1, 0, 1) for columns in (-1, 0, 1) if (rows, columns) != (0, 0)]
    barrier = pltpu.get_barrier_semaphore()
    for peer in everyone:
        pl.semaphore_signal(barrier, inc=1, device_id=peer, device_id_type=MESH)

    for copy in loads[:3] + loads[6:7]:
        copy.wait()
    for number in range(group * sp_count):
        conc[number, 0] = jnp.zeros((8, 128), jnp.float32)
        conc[number, layers + 1] = jnp.zeros((8, 128), jnp.float32)
    zone = soil_zone[...]
    field[0] = table_lookup(zone, soil_store) * previous_head[...] + recharge[...]
    field[1] = zone.astype(jnp.float32)
    line = lax.broadcasted_iota(jnp.int32, (16, 128), 0)
    lane = lax.broadcasted_iota(jnp.int32, (16, 128), 1)
    pick = (lane == jnp.where(line < 8, line, line + 112)).astype(jnp.float32)
    edge_out[...] = column_edges(pick, field[...].reshape(128, 128))

    pl.semaphore_wait(barrier, len(everyone))
    halo = []
    for number, (rows, columns) in enumerate(offsets):
        if columns == 0:
            source, target = field, rows_in.at[0 if rows == 1 else 1]
        else:
            first = 8 if columns == 1 else 0
            source = edge_out.at[pl.ds(first, 8)]
            target = edge_in.at[1 - rows, pl.ds(first, 8)]
        halo.append(
            remote(source, target, halo_send.at[number], halo_recv.at[number], beside(rows, columns))
        )

    mine = pl.ds(group * s, group)
    loads[3].wait()
    for k in range(1, sp_count):
        to = (s + k) % sp_count
        remote(
            species.at[:, :, :, columns_of(to)],
            conc.at[mine, middle],
            spread_send.at[0],
            spread_recv.at[0],
            (g, to),
        )
    width = species.shape[3]
    line = lax.broadcasted_iota(jnp.int32, (2 * sp_count, width), 0)
    lane = lax.broadcasted_iota(jnp.int32, (2 * sp_count, width), 1)
    wanted = jnp.where(line % 2 == 0, (line // 2) * 128 - 1, (line // 2) * 128 + 128)
    tiles = group * layers * 8
    sides_out[:, :tiles] = column_edges(
        (lane == wanted).astype(jnp.float32), species[...].reshape(tiles, width)
    )
    for layer in range(layers):
        ends_out[0, :, layer : layer + 1, :] = species[:, layer, 0:1, :]
        ends_out[1, :, layer : layer + 1, :] = species[:, layer, 7:8, :]
    sides_in[s] = sides_out[...]
    for k in range(1, sp_count):
        to = (s + k) % sp_count
        remote(sides_out, sides_in.at[s], spread_send.at[1], spread_recv.at[1], (g, to))
    for k in range(sp_count):
        to = (s + k) % sp_count
        for rows in (-1, 1):
            remote(
                ends_out.at[0 if rows == -1 else 1, :, :, columns_of(to)],
                ends_in.at[1 if rows == -1 else 0, mine],
                spread_send.at[2],
                spread_recv.at[2],
                beside(rows, k),
            )

    for copy in loads[7:]:
        copy.wait()
    for copy in halo:
        copy.wait_recv()

    row_blocks = []
    for block, center in enumerate((rows_in[0], field[...], rows_in[1])):
        side = spread_edges(edge_in[block], pick).reshape(2, 8, 8, 128)
        row_blocks.append(jnp.concatenate([center, side], axis=3))
    wide = jnp.concatenate(row_blocks, axis=2)
    row = lax.broadcasted_iota(jnp.int32, (24, 256), 0)
    column = lax.broadcasted_iota(jnp.int32, (24, 256), 1)
    first_row = jnp.where(g > 0, 0, 8)
    end_row = jnp.where(g < gx_count - 1, 24, 16)
    end_right = jnp.where(s < sp_count - 1, 136, 128)
    first_left = jnp.where(s > 0, 248, 256)
    inside = (
        (row >= first_row)
        & (row < end_row)
        & ((column < end_right) | (column >= first_left))
    )[None]
    source = jnp.where(inside, wide[0], 0.0)
    conduct = jnp.where(inside, table_lookup(wide[1], soil_cond), 0.0)
    storage = jnp.where(inside, table_lookup(wide[1], soil_store), 0.0)
    faces = six_faces(conduct)

    store_most, cond_most = soil_store[0], soil_cond[0]
    for level in range(1, soil_store.shape[0]):
        store_most = jnp.maximum(store_most, soil_store[level])
        cond_most = jnp.maximum(cond_most, soil_cond[level])
    scale = 2.0 / jnp.full((1, 256), store_most + 12.0 * cond_most, jnp.float32)

    mineral_count, species_count = stoich.shape

    def fill_gram():
        columns = [
            [stoich[m, c] for c in range(species_count)] for m in range(mineral_count)
        ]
        for i in range(mineral_count):
            for j in range(i + 1):
                terms = [a * b for a, b in zip(columns[i], columns[j])]
                while len(terms) > 1:
                    terms = [sum(terms[k : k + 2][1:], terms[k]) for k in range(0, len(terms), 2)]
                gram_table[i, j] = terms[0]

    def place_species():
        whole = conc.at[pl.ds(0, group * (sp_count - 1)), middle]
        pltpu.make_async_copy(whole, whole, spread_recv.at[0]).wait()
        part = sides_in.at[pl.ds(0, sp_count - 1)]
        pltpu.make_async_copy(part, part, spread_recv.at[1]).wait()
        pltpu.make_async_copy(ends_in, ends_in, spread_recv.at[2]).wait()
        loads[4].wait()
        line = lax.broadcasted_iota(jnp.int32, (2 * sp_count, 128), 0)
        lane = lax.broadcasted_iota(jnp.int32, (2 * sp_count, 128), 1)
        place = (((line == 2 * s) & (lane == 0)) | ((line == 2 * s + 1) & (lane == 127))).astype(
            jnp.float32
        )
        row = lax.broadcasted_iota(jnp.int32, (1, 1, 8, 128), 2)
        lane = lax.broadcasted_iota(jnp.int32, (1, 1, 8, 128), 3)
        shape = (group, layers, 8, 128)
        for block in range(sp_count):
            part = pl.ds(group * block, group)
            center = conc[part, middle]
            edges = spread_edges(sides_in[block][:, :tiles], place).reshape(shape)
            upper = jnp.broadcast_to(ends_in[0, part][:, :, None, :], shape)
            under = jnp.broadcast_to(ends_in[1, part][:, :, None, :], shape)
            beside_conc[0, part] = jnp.where(row == 7, under, shifted(center, 1, 2))
            beside_conc[1, part] = jnp.where(row == 0, upper, shifted(center, -1, 2))
            beside_conc[2, part] = jnp.where(lane == 127, edges, shifted(center, 1, 3))
            beside_conc[3, part] = jnp.where(lane == 0, edges, shifted(center, -1, 3))

    def own(values):
        return values[:, 8:16, :128]

    basis = [source]
    for shift in SHIFTS:
        image = scale[None] * apply_flow(basis[-1], storage, faces)
        basis.append(image - shift * basis[-1])
    parts = [split(own(vector)) for vector in basis]
    size = len(SHIFTS)
    factors = [(own(factor), split(own(factor))) for factor in (storage,) + faces]
    scaling = (scale[:, :128], split(scale[:, :128]))
    lost = [
        rounding_left(
            own(basis[k]),
            own(basis[k + 1]),
            SHIFTS[k],
            scaling,
            factors,
            [own(other) for other in six_beside(basis[k])],
        )
        for k in range(size)
    ]
    corners = [(i, j) for i in range(size) for j in range(i, size)]
    repairs = []
    for i, j in corners:
        product = own(basis[i]) * lost[j] + own(basis[j]) * lost[i]
        repairs.append(jnp.sum(product, axis=0))
    places = [(i, j) for i in range(size) for j in range(i, size + 1)]
    products = [inner_product(parts[i], parts[j]) for i, j in places]
    lines = 32
    blank = jnp.zeros((8, 128), jnp.float32)
    products += [(blank, blank)] * (lines - len(products))
    rows = [merge_rows(products[first : first + 8]) for first in range(0, lines, 8)]
    rows = [row[0] for row in rows] + [row[1] for row in rows]
    repairs = [(repair, blank) for repair in repairs]
    repairs += [(blank, blank)] * (24 - len(repairs))
    rows += [merge_rows(repairs[first : first + 8])[0] for first in range(0, 24, 8)]
    table = jnp.concatenate(rows + [blank] * (16 - len(rows)), axis=0).T
    error = jnp.zeros_like(table)
    while table.shape[0] > 8:
        table, error = halved(table, error)
    for shift in (4, 2, 1):
        table, more = exact_sum(table, pltpu.roll(table, shift, 0))
        error = error + pltpu.roll(error, shift, 0) + more
    lane = lax.broadcasted_iota(jnp.int32, (8, 128), 1)
    table = jnp.where(
        lane < 2 * lines,
        table,
        jnp.where(
            lane < 3 * lines, pltpu.roll(error, 2 * lines, 1), pltpu.roll(table, lines, 1)
        ),
    )
    gathered[slot] = table[:1]
    for peer in everyone:
        remote(gathered.at[slot], gathered.at[slot], sum_send.at[0], sum_recv.at[0], peer)
    fill_gram()
    place_species()
    all_others = gathered.at[pl.ds(0, len(everyone))]
    pltpu.make_async_copy(all_others, all_others, sum_recv.at[0]).wait()
    table = gathered[...]
    error = jnp.zeros_like(table)
    while table.shape[0] > 1:
        table, error = halved(table, error)
    table = jnp.broadcast_to(table[0], (8, 128))
    error = jnp.broadcast_to(error[0], (8, 128))
    error = error + pltpu.roll(table, 128 - 2 * lines, 1) + pltpu.roll(table, 128 - lines, 1)
    repair = pltpu.roll(table, 128 - 3 * lines, 1)
    high, low = paired(table, error)
    entries = {
        place: tuple(
            jnp.broadcast_to(part[:1, k : k + 1], (1, 128)) for part in (high, low)
        )
        for k, place in enumerate(places)
    }
    rounding = {
        place: jnp.broadcast_to(repair[:1, k : k + 1], (1, 128))
        for k, place in enumerate(corners)
    }
    answer = solve_krylov(entries, rounding)
    head = None
    for value, vector in zip(answer, basis):
        term = (scale * jnp.concatenate([value, value], axis=1))[None] * vector
        head = term if head is None else head + term

    head_out[...] = own(head)
    kept = jnp.ones_like(own(head))
    for number, (face, head_beside) in enumerate(zip(faces, six_beside(head))):
        face = own(face)
        velocity = face * (own(head) - own(head_beside))
        kept = kept - time_step * (jnp.maximum(velocity, 0.0) + dispersion * face)
        weights[number] = time_step * (dispersion * face - jnp.minimum(velocity, 0.0))
    weights[6] = kept

    loads[5].wait()
    chunk = CHUNK

    def react_chunk(step, carry):
        span = pl.ds(step * chunk, chunk)
        gram = [
            [gram_table[max(i, j), min(i, j)] for j in range(mineral_count)]
            for i in range(mineral_count)
        ]
        scales = [weights[number, span] for number in range(7)]
        moved = []
        for c in range(species_count):
            fields = [conc[c, pl.ds(step * chunk + shift, chunk)] for shift in (2, 0)]
            fields += [beside_conc[side, c, span] for side in range(4)]
            fields.append(conc[c, pl.ds(step * chunk + 1, chunk)])
            moved.append(weighted(scales, fields))
        result = react(
            moved,
            mineral_zone[span],
            rate_table,
            stoich,
            log_equil,
            gram,
        )
        for c in range(species_count):
            reacted[c, span] = result[c]
        for k in range(1, sp_count):
            to = (s + k) % sp_count
            remote(
                reacted.at[pl.ds(group * to, group), span],
                species_out.at[:, span, :, columns_of(s)],
                result_sem.at[0],
                result_sem.at[1],
                (g, to),
            )
        pltpu.make_async_copy(
            reacted.at[mine, span], species_out.at[:, span, :, columns_of(s)], result_sem.at[2]
        ).start()
        return carry

    lax.fori_loop(0, layers // chunk, react_chunk, 0)

    for copy in halo:
        copy.wait_send()
    pltpu.make_async_copy(all_others, all_others, sum_send.at[0]).wait()
    three = conc.at[pl.ds(0, group * (sp_count - 1)), middle]
    pltpu.make_async_copy(three, three, spread_send.at[0]).wait()
    part = sides_in.at[pl.ds(0, sp_count - 1)]
    pltpu.make_async_copy(part, part, spread_send.at[1]).wait()
    pltpu.make_async_copy(ends_in, ends_in, spread_send.at[2]).wait()
    pltpu.make_async_copy(three, three, result_sem.at[0]).wait()
    pltpu.make_async_copy(three, three, result_sem.at[1]).wait()
    once = reacted.at[pl.ds(0, group)]
    pltpu.make_async_copy(once, once, result_sem.at[2]).wait()


def hand_over(head, species, head_out, species_out, head_held, species_held, load_sem, store_sem):
    parts = [(head, head_held, head_out)]
    for k in range(species.shape[0]):
        for first in range(0, species.shape[1], PIECE):
            part = (k, pl.ds(first, PIECE))
            parts.append((species.at[part], species_held.at[part], species_out.at[part]))
    loads, stores = [], []
    for number, (source, held, target) in enumerate(parts):
        loads.append(pltpu.make_async_copy(source, held, load_sem.at[number]))
        stores.append(pltpu.make_async_copy(held, target, store_sem.at[number]))
    for copy in loads:
        copy.start()
    for load, store in zip(loads, stores):
        load.wait()
        store.start()
    for copy in stores:
        copy.wait()


def per_device(mesh, *arrays):
    gx_count, sp_count = mesh.shape["gx"], mesh.shape["sp"]
    inner = min(8, gx_count // 2)
    species = arrays[5]
    group, layers, _, width = species.shape
    total = group * sp_count
    minerals = arrays[8].shape[1]
    arrays = arrays[:8] + (arrays[8].T,) + arrays[9:]
    tables = arrays[3:5] + arrays[7:]
    vmem = pl.BlockSpec(memory_space=pltpu.VMEM)
    hbm = pl.BlockSpec(memory_space=pltpu.HBM)
    cells = (layers, 8, 128)

    def floats(*shape):
        return pltpu.VMEM(shape, jnp.float32)

    results = (
        pl.pallas_call(
            functools.partial(step_kernel, gx_count, sp_count, inner),
            out_shape=(
                jax.ShapeDtypeStruct(cells, jnp.float32),
                jax.ShapeDtypeStruct(species.shape, jnp.float32),
            ),
            in_specs=[hbm] * 10,
            out_specs=(vmem, hbm),
            scratch_shapes=[
                *[pltpu.SMEM(table.shape, jnp.float32) for table in tables],
                floats(*cells),
                floats(*cells),
                pltpu.VMEM(cells, jnp.int32),
                pltpu.VMEM(cells, jnp.int32),
                floats(*species.shape),
                floats(2, *cells),
                floats(2, 2, *cells),
                floats(16, 128),
                floats(3, 16, 128),
                floats(gx_count * sp_count, 1, 128),
                floats(total, layers + 2, 8, 128),
                floats(2, group, layers, width),
                floats(2, total, layers, 128),
                floats(2 * sp_count, 256),
                floats(sp_count, 2 * sp_count, 256),
                floats(4, total, *cells),
                floats(7, *cells),
                floats(total, *cells),
                pltpu.SMEM((minerals, minerals), jnp.float32),
                pltpu.SemaphoreType.DMA((11,)),
                pltpu.SemaphoreType.DMA((8,)),
                pltpu.SemaphoreType.DMA((8,)),
                pltpu.SemaphoreType.DMA((1,)),
                pltpu.SemaphoreType.DMA((1,)),
                pltpu.SemaphoreType.DMA((3,)),
                pltpu.SemaphoreType.DMA((3,)),
                pltpu.SemaphoreType.DMA((3,)),
            ],
            compiler_params=pltpu.CompilerParams(
                collective_id=0, has_side_effects=True, vmem_limit_bytes=60 * 1024 * 1024
            ),
        )(*arrays)
    )

    return tuple(
        pl.pallas_call(
            hand_over,
            out_shape=tuple(jax.ShapeDtypeStruct(r.shape, r.dtype) for r in results),
            in_specs=[hbm, hbm],
            out_specs=(hbm, hbm),
            scratch_shapes=[
                *[floats(*r.shape) for r in results],
                pltpu.SemaphoreType.DMA((1 + group * layers // PIECE,)),
                pltpu.SemaphoreType.DMA((1 + group * layers // PIECE,)),
            ],
            compiler_params=pltpu.CompilerParams(vmem_limit_bytes=60 * 1024 * 1024),
        )(*results)
    )


def solution(mesh):
    cells = P(None, "gx", "sp")
    groups = P("sp", None, "gx", None)
    return jax.shard_map(
        functools.partial(per_device, mesh),
        mesh=mesh,
        in_specs=(cells, cells, cells, P(), P(), groups, cells, P(), P(), P()),
        out_specs=(cells, groups),
        check_vma=False,
    )
```

```python
import functools

import jax
import jax.numpy as jnp
from jax import lax
from jax.experimental import pallas as pl
from jax.experimental.pallas import tpu as pltpu
from jax.sharding import PartitionSpec as P

NEWTON = 2
ROUNDING = 4.3e-12
SHIFTS = (0.5, 0.125, 1.0, 0.25, 1.0, 0.0625)
CHUNK = 2
PIECE = 2

time_step = 0.05
dispersion = 0.5
reaction_span = 0.5
newton_damping = 0.5

MESH = pl.DeviceIdType.MESH
EXACT = lax.Precision.HIGHEST


def table_lookup(labels, table):
    size = table.shape[0] if hasattr(table, "shape") else len(table)
    found = jnp.full(labels.shape, table[0], jnp.float32)
    for level in range(1, size):
        found = jnp.where(labels == level, table[level], found)
    return found


def harmonic_safe(center, other):
    return 2.0 * center * other / jnp.maximum(center + other, 1e-30)


def shifted(field, offset, axis):
    size = field.shape[axis]
    return pltpu.roll(field, (-offset) % size, axis)


def layer_above(field):
    return jnp.concatenate([field[1:], field[-1:]], axis=0)


def layer_below(field):
    return jnp.concatenate([field[:1], field[:-1]], axis=0)


def six_faces(conduct):
    east = harmonic_safe(conduct, shifted(conduct, 1, 2))
    south = harmonic_safe(conduct, shifted(conduct, 1, 1))
    top = harmonic_safe(conduct[:-1], conduct[1:])
    none = jnp.zeros_like(conduct[:1])
    return (
        jnp.concatenate([top, none], axis=0),
        jnp.concatenate([none, top], axis=0),
        south,
        shifted(south, -1, 1),
        east,
        shifted(east, -1, 2),
    )


def six_beside(field):
    return (
        layer_above(field),
        layer_below(field),
        shifted(field, 1, 1),
        shifted(field, -1, 1),
        shifted(field, 1, 2),
        shifted(field, -1, 2),
    )


def apply_flow(field, storage, faces):
    result = storage * field
    for face, beside in zip(faces, six_beside(field)):
        result = result + face * (field - beside)
    return result


def exact_sum(left, right):
    total = left + right
    part = total - left
    return total, (left - (total - part)) + (right - part)


def split(value):
    wide = 4097.0 * value
    high = wide - (wide - value)
    return high, value - high


def paired(high, low):
    total = high + low
    return total, low - (total - high)


def pair_add(left, right):
    total, error = exact_sum(left[0], right[0])
    return paired(total, error + (left[1] + right[1]))


def pair_minus(left, right):
    return pair_add(left, (-right[0], -right[1]))


def pair_times(left, right):
    left_high, left_low = split(left[0])
    right_high, right_low = split(right[0])
    product = left[0] * right[0]
    error = left_high * right_high - product
    error = error + left_high * right_low + left_low * right_high + left_low * right_low
    return paired(product, error + (left[0] * right[1] + left[1] * right[0]))


def pair_inverse(value):
    guess = 1.0 / value[0]
    none = jnp.zeros_like(guess)
    rest = pair_minus((none + 1.0, none), pair_times(value, (guess, none)))
    return paired(guess, guess * (rest[0] + rest[1]))


def halved(total, error):
    half = total.shape[0] // 2
    total, more = exact_sum(total[:half], total[half:])
    return total, error[:half] + error[half:] + more


def inner_product(left, right):
    total = left[0] * right[0]
    error = left[0] * right[1] + left[1] * right[0] + left[1] * right[1]
    while total.shape[0] > 1:
        total, error = halved(total, error)
    return total[0], error[0]


def merge_rows(pairs):
    row = lax.broadcasted_iota(jnp.int32, (8, 128), 0)
    for shift in (4, 2, 1):
        keep = (row % (2 * shift)) < shift
        merged = []
        for left, right in zip(pairs[:shift], pairs[shift:]):
            ends = []
            for part in range(2):
                ends.append(
                    (
                        jnp.where(keep, left[part], pltpu.roll(right[part], shift, 0)),
                        jnp.where(keep, pltpu.roll(left[part], 8 - shift, 0), right[part]),
                    )
                )
            total, error = exact_sum(*ends[0])
            merged.append((total, error + (ends[1][0] + ends[1][1])))
        pairs = merged
    return pairs[0]


def solve_krylov(gram):
    size = len(SHIFTS)
    matrix = {}
    for i in range(size):
        for j in range(i, size):
            after = pair_add(gram[i, j + 1], gram[min(i + 1, j), max(i + 1, j)])
            for shift in (SHIFTS[i], SHIFTS[j]):
                after = pair_add(after, (shift * gram[i, j][0], shift * gram[i, j][1]))
            matrix[j, i] = after
    right = [gram[0, i] for i in range(size)]
    squares = [gram[k, k][0] for k in range(size)]
    mixes = []
    inverse, lower = [None] * size, {}
    for k in range(size):
        pivot = matrix[k, k]
        mix = [jnp.zeros_like(squares[0])] * k + [jnp.ones_like(squares[0])]
        for i in range(k):
            for j in range(i + 1):
                mix[j] = mix[j] - lower[k, i][0] * mixes[i][j]
        mixes.append(mix)
        noise = weighted([value * value for value in mix], squares)
        usable = pivot[0] > ROUNDING * noise
        inverse[k] = tuple(jnp.where(usable, part, 0.0) for part in pair_inverse(pivot))
        for i in range(k + 1, size):
            lower[i, k] = pair_times(matrix[i, k], inverse[k])
        for i in range(k + 1, size):
            right[i] = pair_minus(right[i], pair_times(lower[i, k], right[k]))
            for j in range(k + 1, i + 1):
                matrix[i, j] = pair_minus(
                    matrix[i, j], pair_times(lower[i, k], matrix[j, k])
                )
    answer = [None] * size
    for k in reversed(range(size)):
        value = pair_times(right[k], inverse[k])[0]
        for i in range(k + 1, size):
            value = value - lower[i, k][0] * answer[i]
        answer[k] = value
    return [2.0 * value for value in answer]


def column_edges(pick, block):
    return lax.dot_general(
        pick,
        block,
        (((1,), (1,)), ((), ())),
        precision=EXACT,
        preferred_element_type=jnp.float32,
    )


def spread_edges(edges, pick):
    return lax.dot_general(
        edges,
        pick,
        (((0,), (0,)), ((), ())),
        precision=EXACT,
        preferred_element_type=jnp.float32,
    )


def weighted(scales, fields):
    total = None
    for scale, field in zip(scales, fields):
        term = scale * field
        total = term if total is None else total + term
    return total


def mineral_correction(gram, slope, start):
    count = len(start)
    right = [weighted([gram[i][k] for k in range(count)], start) for i in range(count)]
    schur = {(i, j): gram[i][j] for i in range(count) for j in range(i + 1)}
    pivot, lower = [None] * count, {}
    for k in range(count):
        pivot[k] = slope[k] / (1.0 + slope[k] * schur[k, k])
        for i in range(k + 1, count):
            lower[i, k] = schur[i, k] * pivot[k]
        for i in range(k + 1, count):
            right[i] = right[i] - lower[i, k] * right[k]
            for j in range(k + 1, i + 1):
                schur[i, j] = schur[i, j] - lower[i, k] * schur[j, k]
    answer = [None] * count
    for k in reversed(range(count)):
        value = pivot[k] * right[k]
        for i in range(k + 1, count):
            value = value - lower[i, k] * answer[i]
        answer[k] = value
    return answer


def react(moved, labels, rate_table, stoich, log_equil, gram):
    zones, minerals = rate_table.shape
    species = len(moved)
    rates = [table_lookup(labels, [rate_table[z, m] for z in range(zones)]) for m in range(minerals)]
    base = [
        weighted([stoich[m, c] for c in range(species)], moved) - log_equil[m]
        for m in range(minerals)
    ]
    extent = None
    for newton_pass in range(NEWTON):
        affinity = base
        if extent is not None:
            affinity = [base[m] + weighted(gram[m], extent) for m in range(minerals)]
        tangent = [jnp.tanh(value) for value in affinity]
        start = [reaction_span * rates[m] * tangent[m] for m in range(minerals)]
        if extent is not None:
            start = [extent[m] + start[m] for m in range(minerals)]
        slope = [
            reaction_span * rates[m] * jnp.maximum(1.0 - tangent[m] * tangent[m], 0.0)
            for m in range(minerals)
        ]
        correction = mineral_correction(gram, slope, start)
        step = [newton_damping * (start[m] - correction[m]) for m in range(minerals)]
        extent = [-step[m] if extent is None else extent[m] - step[m] for m in range(minerals)]
    return [
        moved[c] + weighted([stoich[m, c] for m in range(minerals)], extent)
        for c in range(species)
    ]


def step_kernel(
    gx_count,
    sp_count,
    inner,
    previous_head_in,
    recharge_in,
    soil_zone_in,
    soil_cond_in,
    soil_store_in,
    species_in,
    mineral_zone_in,
    rate_table_in,
    stoich_in,
    log_equil_in,
    head_out,
    species_out,
    soil_cond,
    soil_store,
    rate_table,
    stoich,
    log_equil,
    previous_head,
    recharge,
    soil_zone,
    mineral_zone,
    species,
    field,
    rows_in,
    edge_out,
    edge_in,
    gathered,
    conc,
    ends_out,
    ends_in,
    sides_out,
    sides_in,
    beside_conc,
    weights,
    reacted,
    gram_table,
    load_sem,
    halo_send,
    halo_recv,
    sum_send,
    sum_recv,
    spread_send,
    spread_recv,
    result_sem,
):
    g = lax.axis_index("gx")
    s = lax.axis_index("sp")
    cores, across = 2, inner // 2
    down = gx_count // inner
    core, x, y = lax.rem(g, cores), lax.rem(lax.div(g, cores), across), lax.div(g, inner)
    at_core = [lax.rem(core + k, cores) for k in range(cores)]
    at_x = [lax.rem(x + k, across) * cores for k in range(across)]
    at_y = [lax.rem(y + k, down) * inner for k in range(down)]
    at_z = [lax.rem(s + k, sp_count) for k in range(sp_count)]
    at_gx = [[[a + b + c for c in at_core] for b in at_x] for a in at_y]

    def hops(k, count):
        return min(k, count - k)

    steps = [
        (hops(i, down) + hops(j, across) + hops(m, sp_count), k, i, j, m)
        for i in range(down)
        for j in range(across)
        for k in range(cores)
        for m in range(sp_count)
    ][1:]
    everyone = [
        (at_gx[i][j][k], at_z[m]) for _, k, i, j, m in sorted(steps, reverse=True)
    ]
    slot = g * sp_count + s
    group = species_in.shape[0]
    layers = species_in.shape[1]

    def columns_of(device):
        return pl.ds(pl.multiple_of(device * 128, 128), 128)

    def beside(rows, columns):
        return ((g + rows + gx_count) % gx_count, (s + columns) % sp_count)

    def remote(source, target, send, recv, peer):
        copy = pltpu.make_async_remote_copy(
            src_ref=source,
            dst_ref=target,
            send_sem=send,
            recv_sem=recv,
            device_id=peer,
            device_id_type=MESH,
        )
        copy.start()
        return copy

    middle = pl.ds(1, layers)
    loads = [
        pltpu.make_async_copy(source, target, load_sem.at[number])
        for number, (source, target) in enumerate(
            (
                (soil_zone_in, soil_zone),
                (previous_head_in, previous_head),
                (recharge_in, recharge),
                (species_in, species),
                (species_in.at[:, :, :, columns_of(s)], conc.at[pl.ds(group * s, group), middle]),
                (mineral_zone_in, mineral_zone),
                (soil_store_in, soil_store),
                (soil_cond_in, soil_cond),
                (rate_table_in, rate_table),
                (stoich_in, stoich),
                (log_equil_in, log_equil),
            )
        )
    ]
    for copy in loads:
        copy.start()

    offsets = [(rows, columns) for rows in (-1, 0, 1) for columns in (-1, 0, 1) if (rows, columns) != (0, 0)]
    barrier = pltpu.get_barrier_semaphore()
    for peer in everyone:
        pl.semaphore_signal(barrier, inc=1, device_id=peer, device_id_type=MESH)

    for copy in loads[:3] + loads[6:7]:
        copy.wait()
    for number in range(group * sp_count):
        conc[number, 0] = jnp.zeros((8, 128), jnp.float32)
        conc[number, layers + 1] = jnp.zeros((8, 128), jnp.float32)
    zone = soil_zone[...]
    field[0] = table_lookup(zone, soil_store) * previous_head[...] + recharge[...]
    field[1] = zone.astype(jnp.float32)
    line = lax.broadcasted_iota(jnp.int32, (16, 128), 0)
    lane = lax.broadcasted_iota(jnp.int32, (16, 128), 1)
    pick = (lane == jnp.where(line < 8, line, line + 112)).astype(jnp.float32)
    edge_out[...] = column_edges(pick, field[...].reshape(128, 128))

    pl.semaphore_wait(barrier, len(everyone))
    halo = []
    for number, (rows, columns) in enumerate(offsets):
        if columns == 0:
            source, target = field, rows_in.at[0 if rows == 1 else 1]
        else:
            first = 8 if columns == 1 else 0
            source = edge_out.at[pl.ds(first, 8)]
            target = edge_in.at[1 - rows, pl.ds(first, 8)]
        halo.append(
            remote(source, target, halo_send.at[number], halo_recv.at[number], beside(rows, columns))
        )

    mine = pl.ds(group * s, group)
    loads[3].wait()
    for k in range(1, sp_count):
        to = (s + k) % sp_count
        remote(
            species.at[:, :, :, columns_of(to)],
            conc.at[mine, middle],
            spread_send.at[0],
            spread_recv.at[0],
            (g, to),
        )
    width = species.shape[3]
    line = lax.broadcasted_iota(jnp.int32, (2 * sp_count, width), 0)
    lane = lax.broadcasted_iota(jnp.int32, (2 * sp_count, width), 1)
    wanted = jnp.where(line % 2 == 0, (line // 2) * 128 - 1, (line // 2) * 128 + 128)
    tiles = group * layers * 8
    sides_out[:, :tiles] = column_edges(
        (lane == wanted).astype(jnp.float32), species[...].reshape(tiles, width)
    )
    for layer in range(layers):
        ends_out[0, :, layer : layer + 1, :] = species[:, layer, 0:1, :]
        ends_out[1, :, layer : layer + 1, :] = species[:, layer, 7:8, :]
    sides_in[s] = sides_out[...]
    for k in range(1, sp_count):
        to = (s + k) % sp_count
        remote(sides_out, sides_in.at[s], spread_send.at[1], spread_recv.at[1], (g, to))
    for k in range(sp_count):
        to = (s + k) % sp_count
        for rows in (-1, 1):
            remote(
                ends_out.at[0 if rows == -1 else 1, :, :, columns_of(to)],
                ends_in.at[1 if rows == -1 else 0, mine],
                spread_send.at[2],
                spread_recv.at[2],
                beside(rows, k),
            )

    for copy in loads[7:]:
        copy.wait()
    for copy in halo:
        copy.wait_recv()

    row_blocks = []
    for block, center in enumerate((rows_in[0], field[...], rows_in[1])):
        side = spread_edges(edge_in[block], pick).reshape(2, 8, 8, 128)
        row_blocks.append(jnp.concatenate([center, side], axis=3))
    wide = jnp.concatenate(row_blocks, axis=2)
    row = lax.broadcasted_iota(jnp.int32, (24, 256), 0)
    column = lax.broadcasted_iota(jnp.int32, (24, 256), 1)
    first_row = jnp.where(g > 0, 0, 8)
    end_row = jnp.where(g < gx_count - 1, 24, 16)
    end_right = jnp.where(s < sp_count - 1, 136, 128)
    first_left = jnp.where(s > 0, 248, 256)
    inside = (
        (row >= first_row)
        & (row < end_row)
        & ((column < end_right) | (column >= first_left))
    )[None]
    source = jnp.where(inside, wide[0], 0.0)
    conduct = jnp.where(inside, table_lookup(wide[1], soil_cond), 0.0)
    storage = jnp.where(inside, table_lookup(wide[1], soil_store), 0.0)
    faces = six_faces(conduct)

    store_most, cond_most = soil_store[0], soil_cond[0]
    for level in range(1, soil_store.shape[0]):
        store_most = jnp.maximum(store_most, soil_store[level])
        cond_most = jnp.maximum(cond_most, soil_cond[level])
    scale = 2.0 / jnp.full((1, 256), store_most + 12.0 * cond_most, jnp.float32)

    mineral_count, species_count = stoich.shape

    def fill_gram():
        columns = [
            [stoich[m, c] for c in range(species_count)] for m in range(mineral_count)
        ]
        for i in range(mineral_count):
            for j in range(i + 1):
                terms = [a * b for a, b in zip(columns[i], columns[j])]
                while len(terms) > 1:
                    terms = [sum(terms[k : k + 2][1:], terms[k]) for k in range(0, len(terms), 2)]
                gram_table[i, j] = terms[0]

    def place_species():
        whole = conc.at[pl.ds(0, group * (sp_count - 1)), middle]
        pltpu.make_async_copy(whole, whole, spread_recv.at[0]).wait()
        part = sides_in.at[pl.ds(0, sp_count - 1)]
        pltpu.make_async_copy(part, part, spread_recv.at[1]).wait()
        pltpu.make_async_copy(ends_in, ends_in, spread_recv.at[2]).wait()
        loads[4].wait()
        line = lax.broadcasted_iota(jnp.int32, (2 * sp_count, 128), 0)
        lane = lax.broadcasted_iota(jnp.int32, (2 * sp_count, 128), 1)
        place = (((line == 2 * s) & (lane == 0)) | ((line == 2 * s + 1) & (lane == 127))).astype(
            jnp.float32
        )
        row = lax.broadcasted_iota(jnp.int32, (1, 1, 8, 128), 2)
        lane = lax.broadcasted_iota(jnp.int32, (1, 1, 8, 128), 3)
        shape = (group, layers, 8, 128)
        for block in range(sp_count):
            part = pl.ds(group * block, group)
            center = conc[part, middle]
            edges = spread_edges(sides_in[block][:, :tiles], place).reshape(shape)
            upper = jnp.broadcast_to(ends_in[0, part][:, :, None, :], shape)
            under = jnp.broadcast_to(ends_in[1, part][:, :, None, :], shape)
            beside_conc[0, part] = jnp.where(row == 7, under, shifted(center, 1, 2))
            beside_conc[1, part] = jnp.where(row == 0, upper, shifted(center, -1, 2))
            beside_conc[2, part] = jnp.where(lane == 127, edges, shifted(center, 1, 3))
            beside_conc[3, part] = jnp.where(lane == 0, edges, shifted(center, -1, 3))

    def own(values):
        return values[:, 8:16, :128]

    basis = [source]
    for shift in SHIFTS:
        image = scale[None] * apply_flow(basis[-1], storage, faces)
        basis.append(image - shift * basis[-1])
    parts = [split(own(vector)) for vector in basis]
    size = len(SHIFTS)
    places = [(i, j) for i in range(size) for j in range(i, size + 1)]
    products = [inner_product(parts[i], parts[j]) for i, j in places]
    lines = 32
    blank = jnp.zeros((8, 128), jnp.float32)
    products += [(blank, blank)] * (lines - len(products))
    rows = [merge_rows(products[first : first + 8]) for first in range(0, lines, 8)]
    rows = [row[0] for row in rows] + [row[1] for row in rows]
    table = jnp.concatenate(rows + [blank] * (16 - len(rows)), axis=0).T
    error = jnp.zeros_like(table)
    while table.shape[0] > 8:
        table, error = halved(table, error)
    for shift in (4, 2, 1):
        table, more = exact_sum(table, pltpu.roll(table, shift, 0))
        error = error + pltpu.roll(error, shift, 0) + more
    lane = lax.broadcasted_iota(jnp.int32, (8, 128), 1)
    table = jnp.where(lane < 2 * lines, table, pltpu.roll(error, 2 * lines, 1))
    gathered[slot] = table[:1]
    for peer in everyone:
        remote(gathered.at[slot], gathered.at[slot], sum_send.at[0], sum_recv.at[0], peer)
    fill_gram()
    place_species()
    all_others = gathered.at[pl.ds(0, len(everyone))]
    pltpu.make_async_copy(all_others, all_others, sum_recv.at[0]).wait()
    table = gathered[...]
    error = jnp.zeros_like(table)
    while table.shape[0] > 1:
        table, error = halved(table, error)
    table = jnp.broadcast_to(table[0], (8, 128))
    error = jnp.broadcast_to(error[0], (8, 128))
    error = error + pltpu.roll(table, 128 - 2 * lines, 1) + pltpu.roll(table, 128 - lines, 1)
    high, low = paired(table, error)
    entries = {
        place: tuple(
            jnp.broadcast_to(part[:1, k : k + 1], (1, 128)) for part in (high, low)
        )
        for k, place in enumerate(places)
    }
    answer = solve_krylov(entries)
    head = None
    for value, vector in zip(answer, basis):
        term = (scale * jnp.concatenate([value, value], axis=1))[None] * vector
        head = term if head is None else head + term

    head_out[...] = own(head)
    kept = jnp.ones_like(own(head))
    for number, (face, head_beside) in enumerate(zip(faces, six_beside(head))):
        face = own(face)
        velocity = face * (own(head) - own(head_beside))
        kept = kept - time_step * (jnp.maximum(velocity, 0.0) + dispersion * face)
        weights[number] = time_step * (dispersion * face - jnp.minimum(velocity, 0.0))
    weights[6] = kept

    loads[5].wait()
    chunk = CHUNK

    def react_chunk(step, carry):
        span = pl.ds(step * chunk, chunk)
        gram = [
            [gram_table[max(i, j), min(i, j)] for j in range(mineral_count)]
            for i in range(mineral_count)
        ]
        scales = [weights[number, span] for number in range(7)]
        moved = []
        for c in range(species_count):
            fields = [conc[c, pl.ds(step * chunk + shift, chunk)] for shift in (2, 0)]
            fields += [beside_conc[side, c, span] for side in range(4)]
            fields.append(conc[c, pl.ds(step * chunk + 1, chunk)])
            moved.append(weighted(scales, fields))
        result = react(
            moved,
            mineral_zone[span],
            rate_table,
            stoich,
            log_equil,
            gram,
        )
        for c in range(species_count):
            reacted[c, span] = result[c]
        for k in sorted(range(1, sp_count), key=lambda k: -hops(k, sp_count)):
            to = (s + k) % sp_count
            remote(
                reacted.at[pl.ds(group * to, group), span],
                species_out.at[:, span, :, columns_of(s)],
                result_sem.at[0],
                result_sem.at[1],
                (g, to),
            )
        pltpu.make_async_copy(
            reacted.at[mine, span], species_out.at[:, span, :, columns_of(s)], result_sem.at[2]
        ).start()
        return carry

    lax.fori_loop(0, layers // chunk, react_chunk, 0)

    for copy in halo:
        copy.wait_send()
    pltpu.make_async_copy(all_others, all_others, sum_send.at[0]).wait()
    three = conc.at[pl.ds(0, group * (sp_count - 1)), middle]
    pltpu.make_async_copy(three, three, spread_send.at[0]).wait()
    part = sides_in.at[pl.ds(0, sp_count - 1)]
    pltpu.make_async_copy(part, part, spread_send.at[1]).wait()
    pltpu.make_async_copy(ends_in, ends_in, spread_send.at[2]).wait()
    pltpu.make_async_copy(three, three, result_sem.at[0]).wait()
    pltpu.make_async_copy(three, three, result_sem.at[1]).wait()
    once = reacted.at[pl.ds(0, group)]
    pltpu.make_async_copy(once, once, result_sem.at[2]).wait()


def hand_over(head, species, head_out, species_out, head_held, species_held, load_sem, store_sem):
    parts = [(head, head_held, head_out)]
    for k in range(species.shape[0]):
        for first in range(0, species.shape[1], PIECE):
            part = (k, pl.ds(first, PIECE))
            parts.append((species.at[part], species_held.at[part], species_out.at[part]))
    loads, stores = [], []
    for number, (source, held, target) in enumerate(parts):
        loads.append(pltpu.make_async_copy(source, held, load_sem.at[number]))
        stores.append(pltpu.make_async_copy(held, target, store_sem.at[number]))
    for copy in loads:
        copy.start()
    for load, store in zip(loads, stores):
        load.wait()
        store.start()
    for copy in stores:
        copy.wait()


def per_device(mesh, *arrays):
    gx_count, sp_count = mesh.shape["gx"], mesh.shape["sp"]
    inner = min(8, gx_count // 2)
    species = arrays[5]
    group, layers, _, width = species.shape
    total = group * sp_count
    minerals = arrays[8].shape[1]
    arrays = arrays[:8] + (arrays[8].T,) + arrays[9:]
    tables = arrays[3:5] + arrays[7:]
    vmem = pl.BlockSpec(memory_space=pltpu.VMEM)
    hbm = pl.BlockSpec(memory_space=pltpu.HBM)
    cells = (layers, 8, 128)

    def floats(*shape):
        return pltpu.VMEM(shape, jnp.float32)

    results = (
        pl.pallas_call(
            functools.partial(step_kernel, gx_count, sp_count, inner),
            out_shape=(
                jax.ShapeDtypeStruct(cells, jnp.float32),
                jax.ShapeDtypeStruct(species.shape, jnp.float32),
            ),
            in_specs=[hbm] * 10,
            out_specs=(vmem, hbm),
            scratch_shapes=[
                *[pltpu.SMEM(table.shape, jnp.float32) for table in tables],
                floats(*cells),
                floats(*cells),
                pltpu.VMEM(cells, jnp.int32),
                pltpu.VMEM(cells, jnp.int32),
                floats(*species.shape),
                floats(2, *cells),
                floats(2, 2, *cells),
                floats(16, 128),
                floats(3, 16, 128),
                floats(gx_count * sp_count, 1, 128),
                floats(total, layers + 2, 8, 128),
                floats(2, group, layers, width),
                floats(2, total, layers, 128),
                floats(2 * sp_count, 256),
                floats(sp_count, 2 * sp_count, 256),
                floats(4, total, *cells),
                floats(7, *cells),
                floats(total, *cells),
                pltpu.SMEM((minerals, minerals), jnp.float32),
                pltpu.SemaphoreType.DMA((11,)),
                pltpu.SemaphoreType.DMA((8,)),
                pltpu.SemaphoreType.DMA((8,)),
                pltpu.SemaphoreType.DMA((1,)),
                pltpu.SemaphoreType.DMA((1,)),
                pltpu.SemaphoreType.DMA((3,)),
                pltpu.SemaphoreType.DMA((3,)),
                pltpu.SemaphoreType.DMA((3,)),
            ],
            compiler_params=pltpu.CompilerParams(
                collective_id=0, has_side_effects=True, vmem_limit_bytes=60 * 1024 * 1024
            ),
        )(*arrays)
    )

    return tuple(
        pl.pallas_call(
            hand_over,
            out_shape=tuple(jax.ShapeDtypeStruct(r.shape, r.dtype) for r in results),
            in_specs=[hbm, hbm],
            out_specs=(hbm, hbm),
            scratch_shapes=[
                *[floats(*r.shape) for r in results],
                pltpu.SemaphoreType.DMA((1 + group * layers // PIECE,)),
                pltpu.SemaphoreType.DMA((1 + group * layers // PIECE,)),
            ],
            compiler_params=pltpu.CompilerParams(vmem_limit_bytes=60 * 1024 * 1024),
        )(*results)
    )


def solution(mesh):
    cells = P(None, "gx", "sp")
    groups = P("sp", None, "gx", None)
    return jax.shard_map(
        functools.partial(per_device, mesh),
        mesh=mesh,
        in_specs=(cells, cells, cells, P(), P(), groups, cells, P(), P(), P()),
        out_specs=(cells, groups),
        check_vma=False,
    )
```
